128 devices in a mesh: ctx: 8 (over z_lo, x), fsdp: 16 (over z_hi, y, core).
Axes of the slice: x: 4, y: 4, z: 4 (z_hi: 2, z_lo: 2; z = z_hi * 2 + z_lo), core: 2. Of those that a mesh axis runs over, the one named last changes fastest.
Arguments:
- tokens: bfloat16 [32, 1024, 768], P('fsdp', 'ctx'), may hold values from -6 to 6
- lengths: int32 [32], P('fsdp'), may hold values from 1 to 1024, as said below
- deal: int32 [8], replicated, may hold values from 0 to 7, each once
- gain_attn: bfloat16 [768], P('fsdp'), may hold values from 0.25 to 1.75
- w_qkv: bfloat16 [768, 2304], P('fsdp'), may hold values from -0.3125 to 0.3125
- w_out: bfloat16 [768, 768], P('fsdp'), may hold values from -0.625 to 0.625
- gain_mlp: bfloat16 [768], P('fsdp'), may hold values from 0.25 to 1.75
- w_in: bfloat16 [768, 2304], P('fsdp'), may hold values from -0.21875 to 0.21875
- w_down: bfloat16 [1152, 768], P('fsdp'), may hold values from -0.375 to 0.375
- cotangent: bfloat16 [32, 1024, 768], P('fsdp', 'ctx'), may hold values from -6 to 6
Outputs:
- layer_out: bfloat16 [32, 1024, 768], P('fsdp', 'ctx')
- grad_tokens: float32 [32, 1024, 768], P('fsdp', 'ctx')
- grad_gain_attn: float32 [768], P('fsdp')
- grad_w_qkv: float32 [768, 2304], P('fsdp')
- grad_w_out: float32 [768, 768], P('fsdp')
- grad_gain_mlp: float32 [768], P('fsdp')
- grad_w_in: float32 [768, 2304], P('fsdp')
- grad_w_down: float32 [1152, 768], P('fsdp')
The draws below stay inside these ranges and needn't reach their ends.
Inputs may be any that keep to these rules, and one draw needn't show every extreme that they name: `lengths`: in each aligned group of 2 sequences one, drawn from the seed, has length 1024.
All inputs are finite; a program needn't handle non-finite values.
Results may differ from the reference program's by a relative error of at most 0.028.
Values may be sent and summed in bfloat16 or wider, within the bound.
No kernel may reach another device: no remote copies, remote signals or barrier semaphores. Data moves between devices by JAX's collectives and lax.ppermute only.
A program may use at most 128 MiB of HBM per device.

```python
from functools import partial
import jax
import jax.numpy as jnp
from jax import lax

D = 768
FF = 1152
HEADS = 12
HD = 64
SEQ_DEV = 2
SEQ_LEN = 1024
BLK = 128
NBLK = 8
SEQS = 32


def draw_lengths(key, part):
    key = jax.random.fold_in(key, 11)
    first_key, second_key = jax.random.split(key)
    drawn = jax.random.randint(first_key, (SEQS,), 1, SEQ_LEN + 1)
    chosen = jax.random.randint(second_key, (SEQS // SEQ_DEV,), 0, SEQ_DEV)
    index = jnp.arange(SEQS, dtype=jnp.int32)
    full_row = index % SEQ_DEV == chosen[index // SEQ_DEV]
    return jnp.where(full_row, SEQ_LEN, drawn).astype(jnp.int32)


def shard_levels(own_key, extent, shards, least, high):
    def one(position, parts):
        heights = jax.random.uniform(jax.random.fold_in(jax.random.fold_in(own_key, 6), position), (parts,), jnp.float32, least / len(shards), high / len(shards))
        return jnp.repeat(jnp.exp(heights), extent[position] // parts).reshape((-1,) + (1,) * (len(extent) - position - 1))

    level = one(*shards[0])
    for cut in shards[1:]:
        level = level * one(*cut)
    return level


def normal_values(key, shape, spread, limit, shards=(), held_as=jnp.bfloat16):
    values = spread * jax.random.normal(key, shape, jnp.float32)
    if shards:
        values = values * shard_levels(key, shape, shards, -0.22, 0.18)
    return jnp.clip(values, -limit, limit).astype(held_as)


def setup_inputs(seed: int = 0) -> dict:
    splits = jax.random.split(jax.random.key(seed), 11)
    tokens = normal_values(splits[0], (SEQS, SEQ_LEN, D), 1.0, 6.0, ((0, 16), (1, 8)))
    lengths = draw_lengths(jax.random.fold_in(splits[10], 71), 0)
    deal = jax.random.permutation(splits[2], NBLK).astype(jnp.int32)
    gain_attn = jnp.clip(1.0 + 0.15 * jax.random.normal(splits[3], (D,), jnp.float32), 0.25, 1.75).astype(jnp.bfloat16)
    w_qkv = normal_values(splits[4], (D, 3 * D), (D // 2) ** -0.5, 0.3125, ((0, 16),))
    w_out = normal_values(splits[5], (D, D), (D // 8) ** -0.5, 0.625, ((0, 16),))
    gain_mlp = jnp.clip(1.0 + 0.15 * jax.random.normal(splits[6], (D,), jnp.float32), 0.25, 1.75).astype(jnp.bfloat16)
    w_in = normal_values(splits[7], (D, 2 * FF), D ** -0.5, 0.21875, ((0, 16),))
    w_down = normal_values(splits[8], (FF, D), (FF // 4) ** -0.5, 0.375, ((0, 16),))
    cotangent = normal_values(splits[9], (SEQS, SEQ_LEN, D), 1.0, 6.0, ((0, 16), (1, 8)))
    return {"tokens": tokens, "lengths": lengths, "deal": deal, "gain_attn": gain_attn, "w_qkv": w_qkv, "w_out": w_out, "gain_mlp": gain_mlp, "w_in": w_in, "w_down": w_down, "cotangent": cotangent}


EPS = 1e-05
THETA = 160000.0
NEGATIVE = -1e+30
HIGH = lax.Precision.HIGHEST

@jax.custom_vjp
def low(v):
    return lax.optimization_barrier(v.astype(jnp.bfloat16)).astype(jnp.float32)

@jax.custom_vjp
def low_back(v):
    return v

def low_keep(v):
    return (low(v), None)

def low_pass(kept, grad):
    return (grad,)

def back_keep(v):
    return (v, None)

def back_low(kept, grad):
    return (low(grad),)
low.defvjp(low_keep, low_pass)
low_back.defvjp(back_keep, back_low)

def tables(positions):
    halves = jnp.arange(HD // 2, dtype=jnp.float32)
    frequency = THETA ** (-2.0 * halves / HD)
    angles = positions.astype(jnp.float32)[:, None] * frequency[None, :]
    cosine = jnp.cos(angles)
    sine = jnp.sin(angles)
    return (jnp.concatenate([cosine, cosine], -1), jnp.concatenate([sine, sine], -1))

def turned(values):
    halfway = values.shape[-1] // 2
    return jnp.concatenate([-values[..., halfway:], values[..., :halfway]], -1)

def rotary(values, cosine, sine):
    return values * cosine + turned(values) * sine

def layer_norm(rows_in, gain):
    centre = rows_in - lax.optimization_barrier(jnp.mean(rows_in, -1, keepdims=True))
    variance = lax.optimization_barrier(jnp.mean(centre * centre, -1, keepdims=True))
    return centre * lax.rsqrt(variance + EPS) * gain

def matmul(left, right):
    return jnp.dot(left, right, precision=HIGH)

def one_sequence(weights, positions, rows_in, length):
    gain_one, w_qkv, w_out, gain_two, w_in, w_down = weights
    cosine, sine = tables(positions)
    cosine = cosine[:, None, :]
    sine = sine[:, None, :]
    seq_rows = rows_in.shape[0]
    normed = low(layer_norm(rows_in, gain_one))
    joined = low_back(matmul(normed, w_qkv))
    query = low(rotary(joined[:, :D].reshape(seq_rows, HEADS, HD), cosine, sine))
    key_rot = low(rotary(joined[:, D:2 * D].reshape(seq_rows, HEADS, HD), cosine, sine))
    value_rows = low(joined[:, 2 * D:].reshape(seq_rows, HEADS, HD))
    keep = positions < length
    scores = low_back(jnp.einsum('qhd,khd->hqk', query, key_rot, precision=HIGH) * HD ** (-0.5))
    scores = jnp.where(keep[None, None, :], scores, NEGATIVE)
    shifted = scores - lax.optimization_barrier(jnp.max(scores, -1, keepdims=True))
    exponent = jnp.exp(shifted)
    attention = exponent / lax.optimization_barrier(jnp.sum(exponent, -1, keepdims=True))
    attended = jnp.einsum('hqk,khd->qhd', low(attention), value_rows, precision=HIGH).reshape(seq_rows, D)
    attended = low(low_back(jnp.where(keep[:, None], attended, 0.0)))
    mixed = rows_in + low_back(matmul(attended, w_out))
    normed_two = low(layer_norm(mixed, gain_two))
    gate_up = low_back(matmul(normed_two, w_in))
    hidden_rows = low(jax.nn.gelu(gate_up[:, :FF], approximate=False) * gate_up[:, FF:])
    return mixed + low_back(matmul(hidden_rows, w_down))

def reference(tokens, lengths, deal, gain_attn, w_qkv, w_out, gain_mlp, w_in, w_down, cotangent):
    offsets = jnp.arange(BLK, dtype=jnp.int32)
    positions = (deal.astype(jnp.int32)[:, None] * BLK + offsets[None, :]).reshape(SEQ_LEN)
    params = tuple((weight_item.astype(jnp.float32) for weight_item in (gain_attn, w_qkv, w_out, gain_mlp, w_in, w_down)))

    def forward(rows_all, weights):
        layer = jax.checkpoint(partial(one_sequence, weights, positions))
        return lax.map(lambda couple: layer(couple[0], couple[1]), (rows_all, lengths))
    outputs, pullback = jax.vjp(forward, tokens.astype(jnp.float32), params)
    grad_in, grads = pullback(cotangent.astype(jnp.float32))
    return (outputs.astype(jnp.bfloat16), grad_in, grads[0], grads[1], grads[2], grads[3], grads[4], grads[5])
```

```python
import math

import jax
import jax.numpy as jnp
from jax import lax
from jax.sharding import PartitionSpec as P

HEADS = 12
HD = 64
BLK = 128


EPS = 1e-05
THETA = 160000.0
NEGATIVE = -1e30
INV_ROOT_TWO = 0.7071067811865476
INV_ROOT_TWO_PI = 0.3989422804014327


def gather_by_exchange(part, axis, n):
    return lax.all_to_all(jnp.broadcast_to(part[None], (n, *part.shape)), axis, 0, 0)


def low(values):
    return values.astype(jnp.bfloat16)


def tables(positions):
    halves = jnp.arange(HD // 2, dtype=jnp.float32)
    frequency = THETA ** (-2.0 * halves / HD)
    angles = positions.astype(jnp.float32)[:, None] * frequency[None, :]
    cosine = jnp.cos(angles)
    sine = jnp.sin(angles)
    return (jnp.concatenate([cosine, cosine], -1), jnp.concatenate([sine, sine], -1))


def turned(values):
    halfway = values.shape[-1] // 2
    return jnp.concatenate([-values[..., halfway:], values[..., :halfway]], -1)


def rotary(values, cosine, sine):
    return values * cosine + turned(values) * sine


def unrotary(grads_in, cosine, sine):
    return grads_in * cosine - turned(grads_in) * sine


def norm_forward(rows_in, gain):
    centre = rows_in - jnp.mean(rows_in, -1, keepdims=True)
    variance = jnp.mean(centre * centre, -1, keepdims=True)
    inverse = lax.rsqrt(variance + EPS)
    normed = centre * inverse
    return (normed * gain.astype(jnp.float32), normed, inverse)


def norm_backward(grad_rows, gain, normed, inverse):
    scaled = grad_rows * gain.astype(jnp.float32)
    grad_gain = jnp.sum(grad_rows * normed, 0)
    grad_rows_in = inverse * (
        scaled
        - jnp.mean(scaled, -1, keepdims=True)
        - normed * jnp.mean(scaled * normed, -1, keepdims=True)
    )
    return (grad_rows_in, grad_gain)


def attention_forward(query, keys, values, keep, factor):
    scores = jnp.einsum("qhd,khd->hqk", query, keys, preferred_element_type=jnp.float32) * factor
    scores = jnp.where(keep[None, None, :], scores, NEGATIVE)
    maximum = jnp.max(scores, -1, keepdims=True)
    exponent = jnp.exp(scores - maximum)
    row_total = jnp.sum(exponent, -1, keepdims=True)
    probs = exponent / row_total
    attended = jnp.einsum("hqk,khd->qhd", low(probs), values, preferred_element_type=jnp.float32)
    return attended, (maximum + jnp.log(row_total))[..., 0]


def attention_backward(query, keys, values, grad_heads, log_total, keep, factor):
    scores = jnp.einsum("qhd,khd->hqk", query, keys, preferred_element_type=jnp.float32) * factor
    scores = jnp.where(keep[None, None, :], scores, NEGATIVE)
    probs = jnp.exp(scores - log_total[..., None])
    grad_probs = jnp.einsum("qhd,khd->hqk", grad_heads, values, preferred_element_type=jnp.float32)
    delta = jnp.sum(probs * grad_probs, -1, keepdims=True)
    grad_scores = low(probs * (grad_probs - delta))
    grad_query = factor * jnp.einsum(
        "hqk,khd->qhd", grad_scores, keys, preferred_element_type=jnp.float32
    )
    grad_key = factor * jnp.einsum(
        "hqk,qhd->khd", grad_scores, query, preferred_element_type=jnp.float32
    )
    grad_value = jnp.einsum(
        "hqk,qhd->khd", low(probs), grad_heads, preferred_element_type=jnp.float32
    )
    return grad_query, grad_key, grad_value


def body(tokens, lengths, deal, gain_attn, w_qkv, w_out, gain_mlp, w_in, w_down, cotangent):
    seqs, local_len, width = tokens.shape
    ctx = lax.axis_size("ctx")
    fsdp = lax.axis_size("fsdp")
    spread = ctx // seqs
    group = HEADS // spread
    span = group * HD
    full_len = local_len * ctx
    rows = seqs * local_len
    factor = HD ** (-0.5)
    context = lax.axis_index("ctx")
    own_seq = context // spread
    own_group = context % spread
    depth = w_qkv.shape[0]
    hidden = w_in.shape[1] // 2
    down_rows = w_down.shape[0]
    f32 = jnp.float32

    offsets = jnp.arange(BLK, dtype=jnp.int32)
    own_pos = lax.dynamic_slice_in_dim(deal, context, 1)[0] * BLK + offsets
    all_pos = (deal[:, None] * BLK + offsets[None, :]).reshape(full_len)
    length = lax.dynamic_slice_in_dim(lengths, own_seq, 1)[0]
    own_keep = own_pos[None, :] < lengths[:, None]
    all_keep = all_pos < length

    pieces = [w_in[:, k * width : (k + 1) * width] for k in range(w_in.shape[1] // width)]
    stacked = jnp.concatenate([*pieces, w_out, w_down], 0)
    stacked_all = lax.all_gather(stacked, "fsdp", axis=0)

    qkv_own = lax.dynamic_index_in_dim(
        w_qkv.reshape(depth, 3, spread, span), own_group, 2, keepdims=False
    ).reshape(depth, 3 * span)
    gains_wide = jnp.stack([gain_attn, gain_mlp], 1)
    fill = jnp.zeros((depth, 640 - 3 * span - 2), jnp.bfloat16)
    first_all = lax.all_gather(
        jnp.concatenate([qkv_own, gains_wide, fill], 1), "fsdp", axis=0, tiled=True
    )
    sequence = lax.all_to_all(jnp.repeat(tokens, spread, axis=0), "ctx", 0, 0, tiled=True)

    wqkv_part = first_all[:, : 3 * span]
    gain_one = first_all[:, 3 * span]
    gain_two = first_all[:, 3 * span + 1]

    cosine, sine = tables(all_pos)
    cosine = cosine[:, None, :]
    sine = sine[:, None, :]

    a_rows, _, _ = norm_forward(sequence.astype(f32).reshape(full_len, width), gain_one)
    a_low = low(a_rows)
    joined = jnp.dot(a_low, wqkv_part, preferred_element_type=f32).reshape(
        full_len, 3, group, HD
    )
    query = low(rotary(joined[:, 0], cosine, sine))
    keys = low(rotary(joined[:, 1], cosine, sine))
    values = low(joined[:, 2])
    attended, log_total = attention_forward(query, keys, values, all_keep, factor)
    attended = low(jnp.where(all_keep[:, None, None], attended, 0.0))
    att_back = lax.all_to_all(attended.reshape(ctx, local_len, span), "ctx", 0, 0, tiled=True)
    att_low = (
        att_back.reshape(seqs, spread, local_len, span).transpose(0, 2, 1, 3).reshape(rows, width)
    )

    count = len(pieces)
    win_all = jnp.concatenate(
        [
            stacked_all[:, k * depth : (k + 1) * depth].reshape(fsdp * depth, width)
            for k in range(count)
        ],
        1,
    )
    wout_all = stacked_all[:, count * depth : (count + 1) * depth].reshape(fsdp * depth, width)
    wdown_all = stacked_all[:, (count + 1) * depth :].reshape(fsdp * down_rows, width)

    resid = tokens.astype(f32).reshape(rows, width)
    mixed = resid + jnp.dot(att_low, wout_all, preferred_element_type=f32)
    normed_mid, normed_two, inverse_two = norm_forward(mixed, gain_two)
    b_low = low(normed_mid)
    gate_up = jnp.dot(b_low, win_all, preferred_element_type=f32)
    gate_in = gate_up[:, :hidden]
    up_half = gate_up[:, hidden:]
    normal_cdf = 0.5 * (1.0 + lax.erf(gate_in * INV_ROOT_TWO))
    gelu_out = gate_in * normal_cdf
    hid_low = low(gelu_out * up_half)
    output = mixed + jnp.dot(hid_low, wdown_all, preferred_element_type=f32)

    grad_low = cotangent.reshape(rows, width)
    grad_out = grad_low.astype(f32)
    grad_wdown = jnp.einsum("rf,rd->fd", hid_low, grad_low, preferred_element_type=f32)
    grad_hid = jnp.einsum("rd,fd->rf", grad_low, wdown_all, preferred_element_type=f32)
    normal_pdf = jnp.exp(-0.5 * gate_in * gate_in) * INV_ROOT_TWO_PI
    grad_gate = grad_hid * up_half * (normal_cdf + gate_in * normal_pdf)
    grad_up = grad_hid * gelu_out
    grad_gate_up = low(jnp.concatenate([grad_gate, grad_up], 1))
    grad_win = low(jnp.einsum("rd,rf->df", b_low, grad_gate_up, preferred_element_type=f32))
    grad_b = jnp.einsum("rf,df->rd", grad_gate_up, win_all, preferred_element_type=f32)
    grad_norm_two, grad_gain_two = norm_backward(grad_b, gain_two, normed_two, inverse_two)
    grad_mixed = grad_out + grad_norm_two
    grad_att = low(grad_mixed)
    grad_wout = jnp.einsum("rd,re->de", att_low, grad_att, preferred_element_type=f32)
    grad_attended = jnp.einsum("re,de->rd", grad_att, wout_all, preferred_element_type=f32)
    grad_heads = jnp.where(own_keep.reshape(rows, 1), grad_attended, 0.0)
    grad_heads = (
        low(grad_heads)
        .reshape(seqs, local_len, spread, span)
        .transpose(0, 2, 1, 3)
        .reshape(ctx, local_len, span)
    )
    grads_stacked = jnp.concatenate(
        [
            *[
                grad_win[:, k * width : (k + 1) * width].reshape(fsdp, depth, width)
                for k in range(count)
            ],
            low(grad_wout).reshape(fsdp, depth, width),
            low(grad_wdown).reshape(fsdp, down_rows, width),
        ],
        1,
    )
    grads_part = lax.psum_scatter(
        grads_stacked.reshape(-1, width), "fsdp", scatter_dimension=0, tiled=True
    )

    all_grad = lax.all_to_all(grad_heads, "ctx", 0, 0, tiled=True).reshape(full_len, group, HD)
    grad_query, grad_key, grad_value = attention_backward(
        query, keys, values, all_grad, log_total, all_keep, factor
    )
    grad_qkv = low(
        jnp.concatenate(
            [
                unrotary(grad_query, cosine, sine).reshape(full_len, span),
                unrotary(grad_key, cosine, sine).reshape(full_len, span),
                grad_value.reshape(full_len, span),
            ],
            1,
        )
    )
    grad_a_part = low(jnp.einsum("rf,df->rd", grad_qkv, wqkv_part, preferred_element_type=f32))
    grad_a_parts = lax.all_to_all(
        grad_a_part.reshape(ctx, local_len, width), "ctx", 0, 0, tiled=True
    )
    grad_wqkv = low(jnp.einsum("rd,rf->df", a_low, grad_qkv, preferred_element_type=f32))
    grad_a = jnp.sum(
        grad_a_parts.reshape(seqs, spread, local_len, width).astype(f32), 1
    ).reshape(rows, width)
    _, normed_one, inverse_one = norm_forward(resid, gain_one)
    grad_norm_one, grad_gain_one = norm_backward(grad_a, gain_one, normed_one, inverse_one)
    grad_input = grad_mixed + grad_norm_one

    last = jnp.concatenate(
        [
            grad_wqkv,
            jnp.stack([low(grad_gain_one), low(grad_gain_two)], 1),
            jnp.zeros((fsdp * depth, 640 - 3 * span - 2), jnp.bfloat16),
        ],
        1,
    )
    last = lax.all_to_all(last, "fsdp", 0, 0, tiled=True).reshape(fsdp, depth, 640)
    last = low(jnp.sum(last.astype(f32), 0))
    last_rows = last.size // width

    own_rows = grads_part.shape[0] // ctx
    shares = lax.all_to_all(grads_part.reshape(ctx, own_rows, width), "ctx", 0, 0, tiled=True)
    share = low(jnp.sum(shares.astype(f32), 0))
    ends = gather_by_exchange(
        jnp.concatenate([last.reshape(last_rows, width), share], 0), "ctx", ctx
    )
    last_all = ends[:, :last_rows].reshape(ctx, depth, 640).astype(f32)
    summed = ends[:, last_rows:].reshape(ctx * own_rows, width).astype(f32)
    grad_wqkv_out = (
        jnp.sum(last_all[:, :, : 3 * span].reshape(seqs, spread, depth, 3, span), 0)
        .transpose(1, 2, 0, 3)
        .reshape(depth, 3 * width)
    )
    gains_out = jnp.sum(last_all[:, :, 3 * span : 3 * span + 2], 0)
    return (
        low(output.reshape(tokens.shape)),
        grad_input.reshape(tokens.shape),
        gains_out[:, 0],
        grad_wqkv_out,
        summed[count * depth : (count + 1) * depth],
        gains_out[:, 1],
        jnp.concatenate([summed[k * depth : (k + 1) * depth] for k in range(count)], 1),
        summed[(count + 1) * depth :],
    )


def solution(mesh):
    placed = (
        P("fsdp", "ctx", None),
        P("fsdp"),
        P(),
        P("fsdp"),
        P("fsdp", None),
        P("fsdp", None),
        P("fsdp"),
        P("fsdp", None),
        P("fsdp", None),
        P("fsdp", "ctx", None),
    )
    return jax.shard_map(
        body,
        mesh=mesh,
        in_specs=placed,
        out_specs=(
            P("fsdp", "ctx", None),
            P("fsdp", "ctx", None),
            P("fsdp"),
            P("fsdp", None),
            P("fsdp", None),
            P("fsdp"),
            P("fsdp", None),
            P("fsdp", None),
        ),
        check_vma=False,
    )
```

```python
import math

import jax
import jax.numpy as jnp
from jax import lax
from jax.sharding import PartitionSpec as P

HEADS = 12
HD = 64
BLK = 128


EPS = 1e-05
THETA = 160000.0
NEGATIVE = -1e30
INV_ROOT_TWO = 0.7071067811865476
INV_ROOT_TWO_PI = 0.3989422804014327


def gather_by_exchange(part, axis, n):
    return lax.all_to_all(jnp.broadcast_to(part[None], (n, *part.shape)), axis, 0, 0)


def core_pairs(n):
    return [(k, k ^ 1) for k in range(n)]


def core_groups(n):
    return [list(range(first, n, 2)) for first in range(2)]


def gather_two_level(part, axis):
    n = lax.axis_size(axis)
    mine = lax.all_to_all(
        jnp.broadcast_to(part[None], (n // 2, *part.shape)),
        axis,
        0,
        0,
        axis_index_groups=core_groups(n),
    )
    other = lax.ppermute(mine, axis, core_pairs(n))
    even = lax.axis_index(axis) % 2 == 0
    return jnp.where(even, mine, other), jnp.where(even, other, mine)


def reduce_two_level(parts, axis):
    n = lax.axis_size(axis)
    core = lax.axis_index(axis) % 2
    paired = parts.reshape(n // 2, 2, *parts.shape[1:])
    away = lax.dynamic_index_in_dim(paired, 1 - core, 1, keepdims=False)
    kept = lax.dynamic_index_in_dim(paired, core, 1, keepdims=False)
    came = lax.ppermute(away, axis, core_pairs(n))
    both = low(kept.astype(jnp.float32) + came.astype(jnp.float32))
    shares = lax.all_to_all(both, axis, 0, 0, tiled=True, axis_index_groups=core_groups(n))
    return low(jnp.sum(shares.astype(jnp.float32), 0))


def low(values):
    return values.astype(jnp.bfloat16)


def tables(positions):
    halves = jnp.arange(HD // 2, dtype=jnp.float32)
    frequency = THETA ** (-2.0 * halves / HD)
    angles = positions.astype(jnp.float32)[:, None] * frequency[None, :]
    cosine = jnp.cos(angles)
    sine = jnp.sin(angles)
    return (jnp.concatenate([cosine, cosine], -1), jnp.concatenate([sine, sine], -1))


def turned(values):
    halfway = values.shape[-1] // 2
    return jnp.concatenate([-values[..., halfway:], values[..., :halfway]], -1)


def rotary(values, cosine, sine):
    return values * cosine + turned(values) * sine


def unrotary(grads_in, cosine, sine):
    return grads_in * cosine - turned(grads_in) * sine


def norm_forward(rows_in, gain):
    centre = rows_in - jnp.mean(rows_in, -1, keepdims=True)
    variance = jnp.mean(centre * centre, -1, keepdims=True)
    inverse = lax.rsqrt(variance + EPS)
    normed = centre * inverse
    return (normed * gain.astype(jnp.float32), normed, inverse)


def norm_backward(grad_rows, gain, normed, inverse):
    scaled = grad_rows * gain.astype(jnp.float32)
    grad_gain = jnp.sum(grad_rows * normed, 0)
    grad_rows_in = inverse * (
        scaled
        - jnp.mean(scaled, -1, keepdims=True)
        - normed * jnp.mean(scaled * normed, -1, keepdims=True)
    )
    return (grad_rows_in, grad_gain)


def attention_forward(query, keys, values, keep, factor):
    scores = jnp.einsum("qhd,khd->hqk", query, keys, preferred_element_type=jnp.float32) * factor
    scores = jnp.where(keep[None, None, :], scores, NEGATIVE)
    maximum = jnp.max(scores, -1, keepdims=True)
    exponent = jnp.exp(scores - maximum)
    row_total = jnp.sum(exponent, -1, keepdims=True)
    probs = exponent / row_total
    attended = jnp.einsum("hqk,khd->qhd", low(probs), values, preferred_element_type=jnp.float32)
    return attended, (maximum + jnp.log(row_total))[..., 0]


def attention_backward(query, keys, values, grad_heads, log_total, keep, factor):
    scores = jnp.einsum("qhd,khd->hqk", query, keys, preferred_element_type=jnp.float32) * factor
    scores = jnp.where(keep[None, None, :], scores, NEGATIVE)
    probs = jnp.exp(scores - log_total[..., None])
    grad_probs = jnp.einsum("qhd,khd->hqk", grad_heads, values, preferred_element_type=jnp.float32)
    delta = jnp.sum(probs * grad_probs, -1, keepdims=True)
    grad_scores = low(probs * (grad_probs - delta))
    grad_query = factor * jnp.einsum(
        "hqk,khd->qhd", grad_scores, keys, preferred_element_type=jnp.float32
    )
    grad_key = factor * jnp.einsum(
        "hqk,qhd->khd", grad_scores, query, preferred_element_type=jnp.float32
    )
    grad_value = jnp.einsum(
        "hqk,qhd->khd", low(probs), grad_heads, preferred_element_type=jnp.float32
    )
    return grad_query, grad_key, grad_value


def body(tokens, lengths, deal, gain_attn, w_qkv, w_out, gain_mlp, w_in, w_down, cotangent):
    seqs, local_len, width = tokens.shape
    ctx = lax.axis_size("ctx")
    fsdp = lax.axis_size("fsdp")
    spread = ctx // seqs
    group = HEADS // spread
    span = group * HD
    full_len = local_len * ctx
    rows = seqs * local_len
    factor = HD ** (-0.5)
    context = lax.axis_index("ctx")
    own_seq = context // spread
    own_group = context % spread
    depth = w_qkv.shape[0]
    hidden = w_in.shape[1] // 2
    down_rows = w_down.shape[0]
    f32 = jnp.float32

    offsets = jnp.arange(BLK, dtype=jnp.int32)
    own_pos = lax.dynamic_slice_in_dim(deal, context, 1)[0] * BLK + offsets
    all_pos = (deal[:, None] * BLK + offsets[None, :]).reshape(full_len)
    length = lax.dynamic_slice_in_dim(lengths, own_seq, 1)[0]
    own_keep = own_pos[None, :] < lengths[:, None]
    all_keep = all_pos < length

    qkv_own = lax.dynamic_index_in_dim(
        w_qkv.reshape(depth, 3, spread, span), own_group, 2, keepdims=False
    ).reshape(depth, 3 * span)
    gains_wide = jnp.stack([gain_attn, gain_mlp], 1)
    fill = jnp.zeros((depth, 640 - 3 * span - 2), jnp.bfloat16)
    first_all = jnp.stack(
        gather_two_level(jnp.concatenate([qkv_own, gains_wide, fill], 1), "fsdp"), 1
    ).reshape(fsdp * depth, 640)
    sequence = lax.all_to_all(jnp.repeat(tokens, spread, axis=0), "ctx", 0, 0, tiled=True)

    wqkv_part = first_all[:, : 3 * span]
    gain_one = first_all[:, 3 * span]
    gain_two = first_all[:, 3 * span + 1]

    count = w_in.shape[1] // width
    pieces = [w_in[:, k * width : (k + 1) * width] for k in range(count)]
    stacked = jnp.concatenate([*pieces, w_out, w_down], 0)
    stacked, first_all = lax.optimization_barrier((stacked, first_all))
    stacked_all = gather_two_level(stacked, "fsdp")

    cosine, sine = tables(all_pos)
    cosine = cosine[:, None, :]
    sine = sine[:, None, :]

    a_rows, seq_normed, _ = norm_forward(sequence.astype(f32).reshape(full_len, width), gain_one)
    a_low = low(a_rows)
    joined = jnp.dot(a_low, wqkv_part, preferred_element_type=f32).reshape(
        full_len, 3, group, HD
    )
    query = low(rotary(joined[:, 0], cosine, sine))
    keys = low(rotary(joined[:, 1], cosine, sine))
    values = low(joined[:, 2])
    attended, log_total = attention_forward(query, keys, values, all_keep, factor)
    attended = low(jnp.where(all_keep[:, None, None], attended, 0.0))
    att_back = lax.all_to_all(attended.reshape(ctx, local_len, span), "ctx", 0, 0, tiled=True)
    att_low = (
        att_back.reshape(seqs, spread, local_len, span).transpose(0, 2, 1, 3).reshape(rows, width)
    )

    def whole(start, height):
        halves = [part[:, start : start + height] for part in stacked_all]
        return jnp.stack(halves, 1).reshape(fsdp * height, width)

    win_all = jnp.concatenate([whole(k * depth, depth) for k in range(count)], 1)
    wout_all = whole(count * depth, depth)
    wdown_all = whole((count + 1) * depth, down_rows)

    resid = tokens.astype(f32).reshape(rows, width)
    mixed = resid + jnp.dot(att_low, wout_all, preferred_element_type=f32)
    normed_mid, normed_two, inverse_two = norm_forward(mixed, gain_two)
    b_low = low(normed_mid)
    gate_up = jnp.dot(b_low, win_all, preferred_element_type=f32)
    gate_in = gate_up[:, :hidden]
    up_half = gate_up[:, hidden:]
    normal_cdf = 0.5 * (1.0 + lax.erf(gate_in * INV_ROOT_TWO))
    gelu_out = gate_in * normal_cdf
    hid_low = low(gelu_out * up_half)
    output = mixed + jnp.dot(hid_low, wdown_all, preferred_element_type=f32)

    grad_low = cotangent.reshape(rows, width)
    grad_out = grad_low.astype(f32)
    grad_wdown = jnp.einsum("rf,rd->fd", hid_low, grad_low, preferred_element_type=f32)
    grad_hid = jnp.einsum("rd,fd->rf", grad_low, wdown_all, preferred_element_type=f32)
    normal_pdf = jnp.exp(-0.5 * gate_in * gate_in) * INV_ROOT_TWO_PI
    grad_gate = grad_hid * up_half * (normal_cdf + gate_in * normal_pdf)
    grad_up = grad_hid * gelu_out
    grad_gate_up = low(jnp.concatenate([grad_gate, grad_up], 1))
    grad_win = low(jnp.einsum("rd,rf->df", b_low, grad_gate_up, preferred_element_type=f32))
    grad_b = jnp.einsum("rf,df->rd", grad_gate_up, win_all, preferred_element_type=f32)
    grad_norm_two, grad_gain_two = norm_backward(grad_b, gain_two, normed_two, inverse_two)
    grad_mixed = grad_out + grad_norm_two
    grad_att = low(grad_mixed)
    grad_wout = jnp.einsum("rd,re->de", att_low, grad_att, preferred_element_type=f32)
    grad_attended = jnp.einsum("re,de->rd", grad_att, wout_all, preferred_element_type=f32)
    grad_heads = jnp.where(own_keep.reshape(rows, 1), grad_attended, 0.0)
    grad_heads = (
        low(grad_heads)
        .reshape(seqs, local_len, spread, span)
        .transpose(0, 2, 1, 3)
        .reshape(ctx, local_len, span)
    )
    grads_stacked = jnp.concatenate(
        [
            *[
                grad_win[:, k * width : (k + 1) * width].reshape(fsdp, depth, width)
                for k in range(count)
            ],
            low(grad_wout).reshape(fsdp, depth, width),
            low(grad_wdown).reshape(fsdp, down_rows, width),
        ],
        1,
    )
    grads_stacked, grad_heads = lax.optimization_barrier((grads_stacked, grad_heads))

    all_grad = lax.all_to_all(grad_heads, "ctx", 0, 0, tiled=True).reshape(full_len, group, HD)
    grads_part = reduce_two_level(grads_stacked, "fsdp")
    grad_query, grad_key, grad_value = attention_backward(
        query, keys, values, all_grad, log_total, all_keep, factor
    )
    grad_qkv = low(
        jnp.concatenate(
            [
                unrotary(grad_query, cosine, sine).reshape(full_len, span),
                unrotary(grad_key, cosine, sine).reshape(full_len, span),
                grad_value.reshape(full_len, span),
            ],
            1,
        )
    )
    grad_wqkv = low(jnp.einsum("rd,rf->df", a_low, grad_qkv, preferred_element_type=f32))
    grad_a_part = jnp.einsum("rf,df->rd", grad_qkv, wqkv_part, preferred_element_type=f32)
    grad_gain_one = jnp.sum(grad_a_part * seq_normed, 0)
    last = jnp.concatenate(
        [
            grad_wqkv,
            jnp.stack([low(grad_gain_one), low(grad_gain_two)], 1),
            jnp.zeros((fsdp * depth, 640 - 3 * span - 2), jnp.bfloat16),
        ],
        1,
    )
    last = reduce_two_level(last.reshape(fsdp, depth, 640), "fsdp")
    last_rows = last.size // width
    grad_a_parts = lax.all_to_all(
        low(grad_a_part).reshape(ctx, local_len, width), "ctx", 0, 0, tiled=True
    )
    grad_a = jnp.sum(
        grad_a_parts.reshape(seqs, spread, local_len, width).astype(f32), 1
    ).reshape(rows, width)
    _, normed_one, inverse_one = norm_forward(resid, gain_one)
    grad_norm_one, _ = norm_backward(grad_a, gain_one, normed_one, inverse_one)
    grad_input = grad_mixed + grad_norm_one

    own_rows = grads_part.shape[0] // ctx
    shares = lax.all_to_all(grads_part.reshape(ctx, own_rows, width), "ctx", 0, 0, tiled=True)
    share = low(jnp.sum(shares.astype(f32), 0))
    ends = gather_by_exchange(
        jnp.concatenate([last.reshape(last_rows, width), share], 0), "ctx", ctx
    )
    last_all = ends[:, :last_rows].reshape(ctx, depth, 640).astype(f32)
    summed = ends[:, last_rows:].reshape(ctx * own_rows, width).astype(f32)
    grad_wqkv_out = (
        jnp.sum(last_all[:, :, : 3 * span].reshape(seqs, spread, depth, 3, span), 0)
        .transpose(1, 2, 0, 3)
        .reshape(depth, 3 * width)
    )
    gains_out = jnp.sum(last_all[:, :, 3 * span : 3 * span + 2], 0)
    return (
        low(output.reshape(tokens.shape)),
        grad_input.reshape(tokens.shape),
        gains_out[:, 0],
        grad_wqkv_out,
        summed[count * depth : (count + 1) * depth],
        gains_out[:, 1],
        jnp.concatenate([summed[k * depth : (k + 1) * depth] for k in range(count)], 1),
        summed[(count + 1) * depth :],
    )


def solution(mesh):
    placed = (
        P("fsdp", "ctx", None),
        P("fsdp"),
        P(),
        P("fsdp"),
        P("fsdp", None),
        P("fsdp", None),
        P("fsdp"),
        P("fsdp", None),
        P("fsdp", None),
        P("fsdp", "ctx", None),
    )
    return jax.shard_map(
        body,
        mesh=mesh,
        in_specs=placed,
        out_specs=(
            P("fsdp", "ctx", None),
            P("fsdp", "ctx", None),
            P("fsdp"),
            P("fsdp", None),
            P("fsdp", None),
            P("fsdp"),
            P("fsdp", None),
            P("fsdp", None),
        ),
        check_vma=False,
    )
```

```python
import math

import jax
import jax.numpy as jnp
from jax import lax
from jax.sharding import PartitionSpec as P

HEADS = 12
HD = 64
BLK = 128


EPS = 1e-05
THETA = 160000.0
NEGATIVE = -1e30
INV_ROOT_TWO = 0.7071067811865476
INV_ROOT_TWO_PI = 0.3989422804014327


def gather_by_exchange(part, axis, n):
    return lax.all_to_all(jnp.broadcast_to(part[None], (n, *part.shape)), axis, 0, 0)


def core_pairs(n):
    return [(k, k ^ 1) for k in range(n)]


def core_groups(n):
    return [list(range(first, n, 2)) for first in range(2)]


def gather_doubling(part, axis):
    n = lax.axis_size(axis)
    index = lax.axis_index(axis)
    held = part[None]
    bit = n // 2
    while bit:
        came = lax.ppermute(held, axis, [(k, k ^ bit) for k in range(n)])
        first = (index & bit) == 0
        held = jnp.where(first, jnp.stack([held, came], 1), jnp.stack([came, held], 1))
        held = held.reshape(-1, *part.shape)
        bit //= 2
    return held


def core_sum(parts, axis):
    n = lax.axis_size(axis)
    core = lax.axis_index(axis) % 2
    paired = parts.reshape(n // 2, 2, *parts.shape[1:])
    away = lax.dynamic_index_in_dim(paired, 1 - core, 1, keepdims=False)
    kept = lax.dynamic_index_in_dim(paired, core, 1, keepdims=False)
    came = lax.ppermute(away, axis, core_pairs(n))
    return low(kept.astype(jnp.float32) + came.astype(jnp.float32))


def low(values):
    return values.astype(jnp.bfloat16)


def tables(positions):
    halves = jnp.arange(HD // 2, dtype=jnp.float32)
    frequency = THETA ** (-2.0 * halves / HD)
    angles = positions.astype(jnp.float32)[:, None] * frequency[None, :]
    cosine = jnp.cos(angles)
    sine = jnp.sin(angles)
    return (jnp.concatenate([cosine, cosine], -1), jnp.concatenate([sine, sine], -1))


def turned(values):
    halfway = values.shape[-1] // 2
    return jnp.concatenate([-values[..., halfway:], values[..., :halfway]], -1)


def rotary(values, cosine, sine):
    return values * cosine + turned(values) * sine


def unrotary(grads_in, cosine, sine):
    return grads_in * cosine - turned(grads_in) * sine


def norm_forward(rows_in, gain):
    centre = rows_in - jnp.mean(rows_in, -1, keepdims=True)
    variance = jnp.mean(centre * centre, -1, keepdims=True)
    inverse = lax.rsqrt(variance + EPS)
    normed = centre * inverse
    return (normed * gain.astype(jnp.float32), normed, inverse)


def norm_backward(grad_rows, gain, normed, inverse):
    scaled = grad_rows * gain.astype(jnp.float32)
    grad_gain = jnp.sum(grad_rows * normed, 0)
    grad_rows_in = inverse * (
        scaled
        - jnp.mean(scaled, -1, keepdims=True)
        - normed * jnp.mean(scaled * normed, -1, keepdims=True)
    )
    return (grad_rows_in, grad_gain)


def attention_forward(query, keys, values, keep, factor):
    scores = jnp.einsum("qhd,khd->hqk", query, keys, preferred_element_type=jnp.float32) * factor
    scores = jnp.where(keep[None, None, :], scores, NEGATIVE)
    maximum = jnp.max(scores, -1, keepdims=True)
    exponent = jnp.exp(scores - maximum)
    row_total = jnp.sum(exponent, -1, keepdims=True)
    probs = exponent / row_total
    attended = jnp.einsum("hqk,khd->qhd", low(probs), values, preferred_element_type=jnp.float32)
    return attended, (maximum + jnp.log(row_total))[..., 0]


def attention_backward(query, keys, values, grad_heads, log_total, keep, factor):
    scores = jnp.einsum("qhd,khd->hqk", query, keys, preferred_element_type=jnp.float32) * factor
    scores = jnp.where(keep[None, None, :], scores, NEGATIVE)
    probs = jnp.exp(scores - log_total[..., None])
    grad_probs = jnp.einsum("qhd,khd->hqk", grad_heads, values, preferred_element_type=jnp.float32)
    delta = jnp.sum(probs * grad_probs, -1, keepdims=True)
    grad_scores = low(probs * (grad_probs - delta))
    grad_query = factor * jnp.einsum(
        "hqk,khd->qhd", grad_scores, keys, preferred_element_type=jnp.float32
    )
    grad_key = factor * jnp.einsum(
        "hqk,qhd->khd", grad_scores, query, preferred_element_type=jnp.float32
    )
    grad_value = jnp.einsum(
        "hqk,qhd->khd", low(probs), grad_heads, preferred_element_type=jnp.float32
    )
    return grad_query, grad_key, grad_value


def body(tokens, lengths, deal, gain_attn, w_qkv, w_out, gain_mlp, w_in, w_down, cotangent):
    seqs, local_len, width = tokens.shape
    ctx = lax.axis_size("ctx")
    fsdp = lax.axis_size("fsdp")
    spread = ctx // seqs
    group = HEADS // spread
    span = group * HD
    full_len = local_len * ctx
    rows = seqs * local_len
    factor = HD ** (-0.5)
    context = lax.axis_index("ctx")
    own_seq = context // spread
    own_group = context % spread
    depth = w_qkv.shape[0]
    hidden = w_in.shape[1] // 2
    down_rows = w_down.shape[0]
    f32 = jnp.float32

    offsets = jnp.arange(BLK, dtype=jnp.int32)
    own_pos = lax.dynamic_slice_in_dim(deal, context, 1)[0] * BLK + offsets
    all_pos = (deal[:, None] * BLK + offsets[None, :]).reshape(full_len)
    length = lax.dynamic_slice_in_dim(lengths, own_seq, 1)[0]
    own_keep = own_pos[None, :] < lengths[:, None]
    all_keep = all_pos < length

    qkv_own = lax.dynamic_index_in_dim(
        w_qkv.reshape(depth, 3, spread, span), own_group, 2, keepdims=False
    ).reshape(depth, 3 * span)
    gains_wide = jnp.stack([gain_attn, gain_mlp], 1)
    fill = jnp.zeros((depth, 640 - 3 * span - 2), jnp.bfloat16)
    first_all = gather_doubling(
        jnp.concatenate([qkv_own, gains_wide, fill], 1), "fsdp"
    ).reshape(fsdp * depth, 640)
    sequence = lax.all_to_all(jnp.repeat(tokens, spread, axis=0), "ctx", 0, 0, tiled=True)

    wqkv_part = first_all[:, : 3 * span]
    gain_one = first_all[:, 3 * span]
    gain_two = first_all[:, 3 * span + 1]

    count = w_in.shape[1] // width
    pieces = [w_in[:, k * width : (k + 1) * width] for k in range(count)]
    stacked = jnp.concatenate([*pieces, w_out, w_down], 0)
    stacked_all = lax.all_gather(stacked, "fsdp", axis=0)

    cosine, sine = tables(all_pos)
    cosine = cosine[:, None, :]
    sine = sine[:, None, :]

    a_rows, seq_normed, _ = norm_forward(sequence.astype(f32).reshape(full_len, width), gain_one)
    a_low = low(a_rows)
    joined = jnp.dot(a_low, wqkv_part, preferred_element_type=f32).reshape(
        full_len, 3, group, HD
    )
    query = low(rotary(joined[:, 0], cosine, sine))
    keys = low(rotary(joined[:, 1], cosine, sine))
    values = low(joined[:, 2])
    attended, log_total = attention_forward(query, keys, values, all_keep, factor)
    attended = low(jnp.where(all_keep[:, None, None], attended, 0.0))
    att_back = lax.all_to_all(attended.reshape(ctx, local_len, span), "ctx", 0, 0, tiled=True)
    att_low = (
        att_back.reshape(seqs, spread, local_len, span).transpose(0, 2, 1, 3).reshape(rows, width)
    )

    def whole(start, height):
        return stacked_all[:, start : start + height].reshape(fsdp * height, width)

    win_all = jnp.concatenate([whole(k * depth, depth) for k in range(count)], 1)
    wout_all = whole(count * depth, depth)
    wdown_all = whole((count + 1) * depth, down_rows)

    resid = tokens.astype(f32).reshape(rows, width)
    mixed = resid + jnp.dot(att_low, wout_all, preferred_element_type=f32)
    normed_mid, normed_two, inverse_two = norm_forward(mixed, gain_two)
    b_low = low(normed_mid)
    gate_up = jnp.dot(b_low, win_all, preferred_element_type=f32)
    gate_in = gate_up[:, :hidden]
    up_half = gate_up[:, hidden:]
    normal_cdf = 0.5 * (1.0 + lax.erf(gate_in * INV_ROOT_TWO))
    gelu_out = gate_in * normal_cdf
    hid_low = low(gelu_out * up_half)
    output = mixed + jnp.dot(hid_low, wdown_all, preferred_element_type=f32)

    grad_low = cotangent.reshape(rows, width)
    grad_out = grad_low.astype(f32)
    grad_wdown = jnp.einsum("rf,rd->fd", hid_low, grad_low, preferred_element_type=f32)
    grad_hid = jnp.einsum("rd,fd->rf", grad_low, wdown_all, preferred_element_type=f32)
    normal_pdf = jnp.exp(-0.5 * gate_in * gate_in) * INV_ROOT_TWO_PI
    grad_gate = grad_hid * up_half * (normal_cdf + gate_in * normal_pdf)
    grad_up = grad_hid * gelu_out
    grad_gate_up = low(jnp.concatenate([grad_gate, grad_up], 1))
    grad_win = low(jnp.einsum("rd,rf->df", b_low, grad_gate_up, preferred_element_type=f32))
    grad_b = jnp.einsum("rf,df->rd", grad_gate_up, win_all, preferred_element_type=f32)
    grad_norm_two, grad_gain_two = norm_backward(grad_b, gain_two, normed_two, inverse_two)
    grad_mixed = grad_out + grad_norm_two
    grad_att = low(grad_mixed)
    grad_wout = jnp.einsum("rd,re->de", att_low, grad_att, preferred_element_type=f32)
    grad_attended = jnp.einsum("re,de->rd", grad_att, wout_all, preferred_element_type=f32)
    grad_heads = jnp.where(own_keep.reshape(rows, 1), grad_attended, 0.0)
    grad_heads = (
        low(grad_heads)
        .reshape(seqs, local_len, spread, span)
        .transpose(0, 2, 1, 3)
        .reshape(ctx, local_len, span)
    )
    main_rows = ((count + 1) * depth + down_rows) // (8 * ctx) * 8 * ctx
    chunk = main_rows // ctx
    grad_wdown = low(grad_wdown).reshape(fsdp, down_rows, width)
    split = main_rows - (count + 1) * depth
    grads_main = jnp.concatenate(
        [
            *[
                grad_win[:, k * width : (k + 1) * width].reshape(fsdp, depth, width)
                for k in range(count)
            ],
            low(grad_wout).reshape(fsdp, depth, width),
            grad_wdown[:, :split],
        ],
        1,
    )
    main_pair = core_sum(grads_main, "fsdp")
    main_pair = main_pair.reshape(fsdp // 2, ctx, chunk, width).transpose(1, 0, 2, 3)
    main_part = lax.psum_scatter(main_pair, "ctx", scatter_dimension=0, tiled=True)
    main_part = main_part.reshape(fsdp // 2, chunk, width)

    all_grad = lax.all_to_all(grad_heads, "ctx", 0, 0, tiled=True).reshape(full_len, group, HD)
    grad_query, grad_key, grad_value = attention_backward(
        query, keys, values, all_grad, log_total, all_keep, factor
    )
    grad_qkv = low(
        jnp.concatenate(
            [
                unrotary(grad_query, cosine, sine).reshape(full_len, span),
                unrotary(grad_key, cosine, sine).reshape(full_len, span),
                grad_value.reshape(full_len, span),
            ],
            1,
        )
    )
    grad_wqkv = low(jnp.einsum("rd,rf->df", a_low, grad_qkv, preferred_element_type=f32))
    grad_a_part = jnp.einsum("rf,df->rd", grad_qkv, wqkv_part, preferred_element_type=f32)
    grad_gain_one = jnp.sum(grad_a_part * seq_normed, 0)
    last = jnp.concatenate(
        [
            grad_wqkv,
            jnp.stack([low(grad_gain_one), low(grad_gain_two)], 1),
            jnp.zeros((fsdp * depth, 640 - 3 * span - 2), jnp.bfloat16),
        ],
        1,
    )
    last = jnp.concatenate(
        [last.reshape(fsdp, -1, width), grad_wdown[:, split:]], 1
    )
    last = core_sum(last, "fsdp")
    last_rows = last.shape[1]
    grad_a_parts = lax.all_to_all(
        low(grad_a_part).reshape(ctx, local_len, width), "ctx", 0, 0, tiled=True
    )
    grad_a = jnp.sum(
        grad_a_parts.reshape(seqs, spread, local_len, width).astype(f32), 1
    ).reshape(rows, width)
    _, normed_one, inverse_one = norm_forward(resid, gain_one)
    grad_norm_one, _ = norm_backward(grad_a, gain_one, normed_one, inverse_one)
    grad_input = grad_mixed + grad_norm_one

    shares = lax.all_to_all(
        jnp.concatenate([last, main_part], 1),
        "fsdp",
        0,
        0,
        tiled=True,
        axis_index_groups=core_groups(fsdp),
    )
    share = low(jnp.sum(shares.astype(f32), 0))
    ends = gather_by_exchange(share, "ctx", ctx)
    extra = down_rows - split
    last_all = ends[:, : last_rows - extra].reshape(ctx, depth, 640).astype(f32)
    down_end = jnp.sum(ends[:, last_rows - extra : last_rows].astype(f32), 0)
    summed = ends[:, last_rows:].reshape(main_rows, width).astype(f32)
    grad_wqkv_out = (
        jnp.sum(last_all[:, :, : 3 * span].reshape(seqs, spread, depth, 3, span), 0)
        .transpose(1, 2, 0, 3)
        .reshape(depth, 3 * width)
    )
    gains_out = jnp.sum(last_all[:, :, 3 * span : 3 * span + 2], 0)
    return (
        low(output.reshape(tokens.shape)),
        grad_input.reshape(tokens.shape),
        gains_out[:, 0],
        grad_wqkv_out,
        summed[count * depth : (count + 1) * depth],
        gains_out[:, 1],
        jnp.concatenate([summed[k * depth : (k + 1) * depth] for k in range(count)], 1),
        jnp.concatenate([summed[(count + 1) * depth :], down_end], 0),
    )


def solution(mesh):
    placed = (
        P("fsdp", "ctx", None),
        P("fsdp"),
        P(),
        P("fsdp"),
        P("fsdp", None),
        P("fsdp", None),
        P("fsdp"),
        P("fsdp", None),
        P("fsdp", None),
        P("fsdp", "ctx", None),
    )
    return jax.shard_map(
        body,
        mesh=mesh,
        in_specs=placed,
        out_specs=(
            P("fsdp", "ctx", None),
            P("fsdp", "ctx", None),
            P("fsdp"),
            P("fsdp", None),
            P("fsdp", None),
            P("fsdp"),
            P("fsdp", None),
            P("fsdp", None),
        ),
        check_vma=False,
    )
```

```python
import math

import jax
import jax.numpy as jnp
from jax import lax
from jax.experimental import pallas as pl
from jax.experimental.pallas import tpu as pltpu
from jax.sharding import PartitionSpec as P

HEADS = 12
HD = 64
BLK = 128


EPS = 1e-05
THETA = 160000.0
NEGATIVE = -1e30
INV_ROOT_TWO = 0.7071067811865476
INV_ROOT_TWO_PI = 0.3989422804014327


def gather_by_exchange(part, axis, n):
    return lax.all_to_all(jnp.broadcast_to(part[None], (n, *part.shape)), axis, 0, 0)


def core_pairs(n):
    return [(k, k ^ 1) for k in range(n)]


def core_groups(n):
    return [list(range(first, n, 2)) for first in range(2)]


def gather_doubling(part, axis):
    n = lax.axis_size(axis)
    index = lax.axis_index(axis)
    held = part[None]
    bit = n // 2
    while bit:
        came = lax.ppermute(held, axis, [(k, k ^ bit) for k in range(n)])
        first = (index & bit) == 0
        held = jnp.where(first, jnp.stack([held, came], 1), jnp.stack([came, held], 1))
        held = held.reshape(-1, *part.shape)
        bit //= 2
    return held


def gather_two_level(part, axis):
    n = lax.axis_size(axis)
    mine = lax.all_to_all(
        jnp.broadcast_to(part[None], (n // 2, *part.shape)),
        axis,
        0,
        0,
        axis_index_groups=core_groups(n),
    )
    other = lax.ppermute(mine, axis, core_pairs(n))
    even = lax.axis_index(axis) % 2 == 0
    return jnp.where(even, mine, other), jnp.where(even, other, mine)


def core_sum(parts, axis):
    n = lax.axis_size(axis)
    core = lax.axis_index(axis) % 2
    paired = parts.reshape(n // 2, 2, *parts.shape[1:])
    away = lax.dynamic_index_in_dim(paired, 1 - core, 1, keepdims=False)
    kept = lax.dynamic_index_in_dim(paired, core, 1, keepdims=False)
    came = lax.ppermute(away, axis, core_pairs(n))
    return low(kept.astype(jnp.float32) + came.astype(jnp.float32))


def spread_sum(parts, axis):
    groups = core_groups(lax.axis_size(axis))
    shares = lax.all_to_all(parts, axis, 0, 0, tiled=True, axis_index_groups=groups)
    return low(jnp.sum(shares.astype(jnp.float32), 0))


def low(values):
    return values.astype(jnp.bfloat16)


def tables(positions):
    halves = jnp.arange(HD // 2, dtype=jnp.float32)
    frequency = THETA ** (-2.0 * halves / HD)
    angles = frequency[:, None] * positions.astype(jnp.float32)[None, :]
    return jnp.cos(angles), jnp.sin(angles)


def norm_forward(rows_in, gain):
    centre = rows_in - jnp.mean(rows_in, -1, keepdims=True)
    variance = jnp.mean(centre * centre, -1, keepdims=True)
    inverse = lax.rsqrt(variance + EPS)
    normed = centre * inverse
    return (normed * gain.astype(jnp.float32), normed, inverse)


def norm_backward(grad_rows, gain, normed, inverse):
    scaled = grad_rows * gain.astype(jnp.float32)
    grad_gain = jnp.sum(grad_rows * normed, 0)
    grad_rows_in = inverse * (
        scaled
        - jnp.mean(scaled, -1, keepdims=True)
        - normed * jnp.mean(scaled * normed, -1, keepdims=True)
    )
    return (grad_rows_in, grad_gain)


NN = (((1,), (0,)), ((), ()))
NT = (((1,), (1,)), ((), ()))
ROWS = 256
COLS = 256


def product(left, right, dims=NN):
    return lax.dot_general(left, right, dims, preferred_element_type=jnp.float32)


def forward_kernel(
    seq_ref, w_ref, cos_ref, sin_ref, bias_ref, keep_ref, out_ref, a_ref, qkv_ref, lse_ref, o_ref
):
    full_len, width = seq_ref.shape
    span = o_ref.shape[0]
    group = span // HD
    half = HD // 2
    blk = out_ref.shape[2]
    gain = w_ref[:, 512:640].astype(jnp.float32).T[3 * span - 512 : 3 * span - 511]
    w_turned = w_ref[:, : 3 * span].astype(jnp.float32).T.astype(jnp.bfloat16)
    for start in range(0, full_len, ROWS):
        rows = slice(start, start + ROWS)
        x = seq_ref[rows].astype(jnp.float32)
        centre = x - jnp.mean(x, -1, keepdims=True)
        variance = jnp.mean(centre * centre, -1, keepdims=True)
        a_low = (centre * lax.rsqrt(variance + EPS) * gain).astype(jnp.bfloat16)
        a_ref[rows] = a_low
        joined = product(w_turned, a_low, NT)
        cosine = cos_ref[:, rows]
        sine = sin_ref[:, rows]
        for part in range(2 * group):
            one = joined[part * HD : part * HD + half]
            two = joined[part * HD + half : (part + 1) * HD]
            scale = HD ** (-0.5) if part < group else 1.0
            for at, value in (
                (0, one * cosine - two * sine),
                (half, two * cosine + one * sine),
            ):
                qkv_ref[part * HD + at : part * HD + at + half, rows] = (
                    value.astype(jnp.bfloat16) * scale
                ).astype(jnp.bfloat16)
        qkv_ref[2 * span :, rows] = joined[2 * span :].astype(jnp.bfloat16)
    for head in range(group):
        here = slice(head * HD, (head + 1) * HD)
        keys = qkv_ref[span + head * HD : span + (head + 1) * HD].T
        values = qkv_ref[2 * span + head * HD : 2 * span + (head + 1) * HD]
        for start in range(0, full_len, COLS):
            cols = slice(start, start + COLS)
            scores = product(keys, qkv_ref[here, cols]) + bias_ref[...]
            maximum = jnp.max(scores, 0, keepdims=True)
            exponent = jnp.exp(scores - maximum)
            total = jnp.sum(exponent, 0, keepdims=True)
            attended = product(values, exponent.astype(jnp.bfloat16))
            attended = attended * (keep_ref[:, cols] / total)
            o_ref[here, cols] = attended
            lse_ref[head : head + 1, cols] = maximum + jnp.log(total)
            for first in range(0, COLS, blk):
                out_ref[(start + first) // blk, here, :] = attended[
                    :, first : first + blk
                ].astype(jnp.bfloat16)


def backward_kernel(
    do_ref, qkv_ref, lse_ref, o_ref, cos_ref, sin_ref, bias_ref, keep_ref, g_ref, dk_ref, dv_ref
):
    span, full_len = o_ref.shape
    group = span // HD
    half = HD // 2
    blk = do_ref.shape[2]
    for head in range(group):
        here = slice(head * HD, (head + 1) * HD)
        keys_turned = qkv_ref[span + head * HD : span + (head + 1) * HD]
        keys = keys_turned.T
        values = qkv_ref[2 * span + head * HD : 2 * span + (head + 1) * HD].T
        for start in range(0, full_len, COLS):
            cols = slice(start, start + COLS)
            query = qkv_ref[here, cols]
            grad_out = jnp.concatenate(
                [do_ref[(start + first) // blk, here, :] for first in range(0, COLS, blk)], 1
            )
            grad_out = grad_out.astype(jnp.float32) * keep_ref[:, cols]
            delta = jnp.sum(grad_out * o_ref[here, cols], 0, keepdims=True)
            grad_out = grad_out.astype(jnp.bfloat16)
            scores = product(keys, query) + bias_ref[...]
            probs = jnp.exp(scores - lse_ref[head : head + 1, cols])
            grad_scores = (probs * (product(values, grad_out) - delta)).astype(jnp.bfloat16)
            grad_value = product(grad_out, probs.astype(jnp.bfloat16), NT)
            grad_key = product(query, grad_scores, NT)
            if start == 0:
                dv_ref[...] = grad_value
                dk_ref[...] = grad_key
            else:
                dv_ref[...] += grad_value
                dk_ref[...] += grad_key
            grad_query = product(keys_turned, grad_scores) * HD ** (-0.5)
            cosine = cos_ref[:, cols]
            sine = sin_ref[:, cols]
            one, two = grad_query[:half], grad_query[half:]
            g_ref[head * HD : head * HD + half, cols] = (one * cosine + two * sine).astype(
                jnp.bfloat16
            )
            g_ref[head * HD + half : (head + 1) * HD, cols] = (
                two * cosine - one * sine
            ).astype(jnp.bfloat16)
        one, two = dk_ref[:half], dk_ref[half:]
        cosine = cos_ref[...]
        sine = sin_ref[...]
        low_at = span + head * HD
        g_ref[low_at : low_at + half] = (one * cosine + two * sine).astype(jnp.bfloat16)
        g_ref[low_at + half : low_at + HD] = (two * cosine - one * sine).astype(jnp.bfloat16)
        g_ref[2 * span + head * HD : 2 * span + (head + 1) * HD] = dv_ref[...].astype(
            jnp.bfloat16
        )


def on_device(kernel, outs, args, scratch=(), name=None):
    space = pl.BlockSpec(memory_space=pltpu.VMEM)
    return pl.pallas_call(
        kernel,
        out_shape=[jax.ShapeDtypeStruct(shape, dtype) for shape, dtype in outs],
        in_specs=[space] * len(args),
        out_specs=[space] * len(outs),
        scratch_shapes=list(scratch),
        compiler_params=pltpu.CompilerParams(vmem_limit_bytes=48 * 1024 * 1024),
        name=name,
    )(*args)


def body(tokens, lengths, deal, gain_attn, w_qkv, w_out, gain_mlp, w_in, w_down, cotangent):
    seqs, local_len, width = tokens.shape
    ctx = lax.axis_size("ctx")
    fsdp = lax.axis_size("fsdp")
    spread = ctx // seqs
    group = HEADS // spread
    span = group * HD
    full_len = local_len * ctx
    rows = seqs * local_len
    context = lax.axis_index("ctx")
    own_seq = context // spread
    own_group = context % spread
    depth = w_qkv.shape[0]
    hidden = w_in.shape[1] // 2
    down_rows = w_down.shape[0]
    f32 = jnp.float32

    offsets = jnp.arange(BLK, dtype=jnp.int32)
    all_pos = (deal[:, None] * BLK + offsets[None, :]).reshape(full_len)
    length = lax.dynamic_slice_in_dim(lengths, own_seq, 1)[0]
    all_keep = all_pos < length

    qkv_own = lax.dynamic_index_in_dim(
        w_qkv.reshape(depth, 3, spread, span), own_group, 2, keepdims=False
    ).reshape(depth, 3 * span)
    gains_wide = jnp.stack([gain_attn, gain_mlp], 1)
    fill = jnp.zeros((depth, 640 - 3 * span - 2), jnp.bfloat16)
    first_all = gather_doubling(
        jnp.concatenate([qkv_own, gains_wide, fill], 1), "fsdp"
    ).reshape(fsdp * depth, 640)
    sequence = lax.all_to_all(jnp.repeat(tokens, spread, axis=0), "ctx", 0, 0, tiled=True)

    wqkv_part = first_all[:, : 3 * span]
    gain_one = first_all[:, 3 * span]
    gain_two = first_all[:, 3 * span + 1]

    win_all = lax.all_gather(w_in, "fsdp", axis=0, tiled=True)
    stacked, sequence = lax.optimization_barrier(
        (jnp.concatenate([w_out, w_down], 0), sequence)
    )
    stacked_all = gather_two_level(stacked, "fsdp")

    cosine, sine = tables(all_pos)
    bias = jnp.where(all_keep, 0.0, NEGATIVE).astype(f32)[:, None]
    keep_row = all_keep.astype(f32)[None, :]
    sequence = sequence.reshape(full_len, width)
    attended, a_low, qkv, log_total, unrounded = on_device(
        forward_kernel,
        [
            ((ctx, span, local_len), jnp.bfloat16),
            ((full_len, width), jnp.bfloat16),
            ((3 * span, full_len), jnp.bfloat16),
            ((8, full_len), f32),
            ((span, full_len), f32),
        ],
        (sequence, first_all, cosine, sine, bias, keep_row),
        name="attention_forward",
    )
    att_back = lax.all_to_all(attended, "ctx", 0, 0, tiled=True)
    att_turned = att_back.reshape(seqs, width, local_len)

    def whole(start, height):
        halves = [part[:, start : start + height] for part in stacked_all]
        return jnp.stack(halves, 1).reshape(fsdp * height, width)

    wout_all = whole(0, depth)
    wdown_all = whole(depth, down_rows)

    resid = tokens.astype(f32).reshape(rows, width)
    mixed = resid + jnp.einsum(
        "sdr,de->sre", att_turned, wout_all, preferred_element_type=f32
    ).reshape(rows, width)
    normed_mid, normed_two, inverse_two = norm_forward(mixed, gain_two)
    b_low = low(normed_mid)
    gate_up = jnp.dot(b_low, win_all, preferred_element_type=f32)
    gate_in = gate_up[:, :hidden]
    up_half = gate_up[:, hidden:]
    normal_cdf = 0.5 * (1.0 + lax.erf(gate_in * INV_ROOT_TWO))
    gelu_out = gate_in * normal_cdf
    hid_low = low(gelu_out * up_half)
    output = mixed + jnp.dot(hid_low, wdown_all, preferred_element_type=f32)

    grad_low = cotangent.reshape(rows, width)
    grad_out = grad_low.astype(f32)
    grad_hid = jnp.einsum("rd,fd->rf", grad_low, wdown_all, preferred_element_type=f32)
    normal_pdf = jnp.exp(-0.5 * gate_in * gate_in) * INV_ROOT_TWO_PI
    grad_gate = grad_hid * up_half * (normal_cdf + gate_in * normal_pdf)
    grad_up = grad_hid * gelu_out
    grad_gate_up = low(jnp.concatenate([grad_gate, grad_up], 1))
    grad_b = jnp.einsum("rf,df->rd", grad_gate_up, win_all, preferred_element_type=f32)
    grad_norm_two, grad_gain_two = norm_backward(grad_b, gain_two, normed_two, inverse_two)
    grad_mixed = grad_out + grad_norm_two
    grad_att = low(grad_mixed)
    grad_att = grad_att.reshape(seqs, local_len, width)
    grad_heads = low(
        jnp.einsum("de,sre->sdr", wout_all, grad_att, preferred_element_type=f32)
    ).reshape(ctx, span, local_len)
    hid_low, b_low, grad_gate_up, grad_heads = lax.optimization_barrier(
        (hid_low, b_low, grad_gate_up, grad_heads)
    )
    grad_wout = jnp.einsum("sdr,sre->de", att_turned, grad_att, preferred_element_type=f32)
    grad_wdown = jnp.einsum("rf,rd->fd", hid_low, grad_low, preferred_element_type=f32)
    grad_win = low(jnp.einsum("rd,rf->df", b_low, grad_gate_up, preferred_element_type=f32))
    count = w_in.shape[1] // width
    main_rows = ((count + 1) * depth + down_rows) // (8 * ctx) * 8 * ctx
    chunk = main_rows // ctx
    grad_wdown = low(grad_wdown).reshape(fsdp, down_rows, width)
    split = main_rows - (count + 1) * depth
    grads_main = jnp.concatenate(
        [
            *[
                grad_win[:, k * width : (k + 1) * width].reshape(fsdp, depth, width)
                for k in range(count)
            ],
            low(grad_wout).reshape(fsdp, depth, width),
            grad_wdown[:, :split],
        ],
        1,
    )
    main_pair = core_sum(grads_main, "fsdp")
    main_pair = main_pair.reshape(fsdp // 2, ctx, chunk, width).transpose(1, 0, 2, 3)
    main_part = lax.psum_scatter(main_pair, "ctx", scatter_dimension=0, tiled=True)
    main_part = main_part.reshape(fsdp // 2, chunk, width)

    all_grad = lax.all_to_all(grad_heads, "ctx", 0, 0, tiled=True)
    grad_qkv = on_device(
        backward_kernel,
        [((3 * span, full_len), jnp.bfloat16)],
        (all_grad, qkv, log_total, unrounded, cosine, sine, bias, keep_row),
        [pltpu.VMEM((HD, full_len), f32)] * 2,
        name="attention_backward",
    )[0]
    grad_a_part = jnp.einsum("fr,df->rd", grad_qkv, wqkv_part, preferred_element_type=f32)
    grad_wqkv = low(jnp.einsum("rd,fr->df", a_low, grad_qkv, preferred_element_type=f32))
    _, seq_normed, _ = norm_forward(sequence.astype(f32), gain_one)
    grad_gain_one = jnp.sum(grad_a_part * seq_normed, 0)
    last = jnp.concatenate(
        [
            grad_wqkv,
            jnp.stack([low(grad_gain_one), low(grad_gain_two)], 1),
            jnp.zeros((fsdp * depth, 640 - 3 * span - 2), jnp.bfloat16),
        ],
        1,
    )
    last = jnp.concatenate(
        [last.reshape(fsdp, -1, width), grad_wdown[:, split:]], 1
    )
    last = core_sum(last, "fsdp")
    last_rows = last.shape[1]
    grad_a_parts = lax.all_to_all(
        low(grad_a_part).reshape(ctx, local_len, width), "ctx", 0, 0, tiled=True
    )
    grad_a = jnp.sum(
        grad_a_parts.reshape(seqs, spread, local_len, width).astype(f32), 1
    ).reshape(rows, width)
    _, normed_one, inverse_one = norm_forward(resid, gain_one)
    grad_norm_one, _ = norm_backward(grad_a, gain_one, normed_one, inverse_one)
    grad_input = grad_mixed + grad_norm_one

    last = spread_sum(last, "fsdp")
    main_part = spread_sum(main_part, "fsdp")
    share = jnp.concatenate([last, main_part], 0)
    ends = gather_by_exchange(share, "ctx", ctx)
    extra = down_rows - split
    last_all = ends[:, : last_rows - extra].reshape(ctx, depth, 640).astype(f32)
    down_end = jnp.sum(ends[:, last_rows - extra : last_rows].astype(f32), 0)
    summed = ends[:, last_rows:].reshape(main_rows, width).astype(f32)
    grad_wqkv_out = (
        jnp.sum(last_all[:, :, : 3 * span].reshape(seqs, spread, depth, 3, span), 0)
        .transpose(1, 2, 0, 3)
        .reshape(depth, 3 * width)
    )
    gains_out = jnp.sum(last_all[:, :, 3 * span : 3 * span + 2], 0)
    return (
        low(output.reshape(tokens.shape)),
        grad_input.reshape(tokens.shape),
        gains_out[:, 0],
        grad_wqkv_out,
        summed[count * depth : (count + 1) * depth],
        gains_out[:, 1],
        jnp.concatenate([summed[k * depth : (k + 1) * depth] for k in range(count)], 1),
        jnp.concatenate([summed[(count + 1) * depth :], down_end], 0),
    )


def solution(mesh):
    placed = (
        P("fsdp", "ctx", None),
        P("fsdp"),
        P(),
        P("fsdp"),
        P("fsdp", None),
        P("fsdp", None),
        P("fsdp"),
        P("fsdp", None),
        P("fsdp", None),
        P("fsdp", "ctx", None),
    )
    return jax.shard_map(
        body,
        mesh=mesh,
        in_specs=placed,
        out_specs=(
            P("fsdp", "ctx", None),
            P("fsdp", "ctx", None),
            P("fsdp"),
            P("fsdp", None),
            P("fsdp", None),
            P("fsdp"),
            P("fsdp", None),
            P("fsdp", None),
        ),
        check_vma=False,
    )
```

```python
import math

import jax
import jax.numpy as jnp
from jax import lax
from jax.experimental import pallas as pl
from jax.experimental.pallas import tpu as pltpu
from jax.sharding import PartitionSpec as P

HEADS = 12
HD = 64
BLK = 128


EPS = 1e-05
THETA = 160000.0
NEGATIVE = -1e30
INV_ROOT_TWO = 0.7071067811865476
INV_ROOT_TWO_PI = 0.3989422804014327


def gather_by_exchange(part, axis, n):
    return lax.all_to_all(jnp.broadcast_to(part[None], (n, *part.shape)), axis, 0, 0)


def core_pairs(n):
    return [(k, k ^ 1) for k in range(n)]


def core_groups(n):
    return [list(range(first, n, 2)) for first in range(2)]


def gather_doubling(part, axis):
    n = lax.axis_size(axis)
    index = lax.axis_index(axis)
    held = part[None]
    bit = n // 2
    while bit:
        came = lax.ppermute(held, axis, [(k, k ^ bit) for k in range(n)])
        first = (index & bit) == 0
        held = jnp.where(first, jnp.stack([held, came], 1), jnp.stack([came, held], 1))
        held = held.reshape(-1, *part.shape)
        bit //= 2
    return held


def gather_two_level(part, axis):
    n = lax.axis_size(axis)
    mine = lax.all_to_all(
        jnp.broadcast_to(part[None], (n // 2, *part.shape)),
        axis,
        0,
        0,
        axis_index_groups=core_groups(n),
    )
    other = lax.ppermute(mine, axis, core_pairs(n))
    even = lax.axis_index(axis) % 2 == 0
    return jnp.where(even, mine, other), jnp.where(even, other, mine)


def core_sum(kept, away, axis):
    came = lax.ppermute(away, axis, core_pairs(lax.axis_size(axis)))
    return low(kept.astype(jnp.float32) + came.astype(jnp.float32))


def spread_sum(parts, axis):
    groups = core_groups(lax.axis_size(axis))
    shares = lax.all_to_all(parts, axis, 0, 0, tiled=True, axis_index_groups=groups)
    return low(jnp.sum(shares.astype(jnp.float32), 0))


def low(values):
    return values.astype(jnp.bfloat16)


def tables(positions):
    halves = jnp.arange(HD // 2, dtype=jnp.float32)
    frequency = THETA ** (-2.0 * halves / HD)
    angles = frequency[:, None] * positions.astype(jnp.float32)[None, :]
    return jnp.cos(angles), jnp.sin(angles)


def norm_forward(rows_in, gain):
    centre = rows_in - jnp.mean(rows_in, -1, keepdims=True)
    variance = jnp.mean(centre * centre, -1, keepdims=True)
    inverse = lax.rsqrt(variance + EPS)
    normed = centre * inverse
    return (normed * gain.astype(jnp.float32), normed, inverse)


def norm_backward(grad_rows, gain, normed, inverse):
    scaled = grad_rows * gain.astype(jnp.float32)
    grad_gain = jnp.sum(grad_rows * normed, 0)
    grad_rows_in = inverse * (
        scaled
        - jnp.mean(scaled, -1, keepdims=True)
        - normed * jnp.mean(scaled * normed, -1, keepdims=True)
    )
    return (grad_rows_in, grad_gain)


NN = (((1,), (0,)), ((), ()))
NT = (((1,), (1,)), ((), ()))
ROWS = 256
COLS = 256


def product(left, right, dims=NN):
    return lax.dot_general(left, right, dims, preferred_element_type=jnp.float32)


def forward_kernel(
    seq_ref, w_ref, cos_ref, sin_ref, bias_ref, keep_ref, out_ref, a_ref, qkv_ref, lse_ref, o_ref
):
    full_len, width = seq_ref.shape
    span = o_ref.shape[0]
    group = span // HD
    half = HD // 2
    blk = out_ref.shape[2]
    gain = w_ref[:, 512:640].astype(jnp.float32).T[3 * span - 512 : 3 * span - 511]
    w_turned = w_ref[:, : 3 * span].astype(jnp.float32).T.astype(jnp.bfloat16)
    for start in range(0, full_len, ROWS):
        rows = slice(start, start + ROWS)
        x = seq_ref[rows].astype(jnp.float32)
        centre = x - jnp.mean(x, -1, keepdims=True)
        variance = jnp.mean(centre * centre, -1, keepdims=True)
        a_low = (centre * lax.rsqrt(variance + EPS) * gain).astype(jnp.bfloat16)
        a_ref[rows] = a_low
        joined = product(w_turned, a_low, NT)
        cosine = cos_ref[:, rows]
        sine = sin_ref[:, rows]
        for part in range(2 * group):
            one = joined[part * HD : part * HD + half]
            two = joined[part * HD + half : (part + 1) * HD]
            scale = HD ** (-0.5) if part < group else 1.0
            for at, value in (
                (0, one * cosine - two * sine),
                (half, two * cosine + one * sine),
            ):
                qkv_ref[part * HD + at : part * HD + at + half, rows] = (
                    value.astype(jnp.bfloat16) * scale
                ).astype(jnp.bfloat16)
        qkv_ref[2 * span :, rows] = joined[2 * span :].astype(jnp.bfloat16)
    for head in range(group):
        here = slice(head * HD, (head + 1) * HD)
        keys = qkv_ref[span + head * HD : span + (head + 1) * HD].T
        values = qkv_ref[2 * span + head * HD : 2 * span + (head + 1) * HD]
        for start in range(0, full_len, COLS):
            cols = slice(start, start + COLS)
            scores = product(keys, qkv_ref[here, cols]) + bias_ref[...]
            maximum = jnp.max(scores, 0, keepdims=True)
            exponent = jnp.exp(scores - maximum)
            total = jnp.sum(exponent, 0, keepdims=True)
            attended = product(values, exponent.astype(jnp.bfloat16))
            attended = attended * (keep_ref[:, cols] / total)
            o_ref[here, cols] = attended
            lse_ref[head : head + 1, cols] = maximum + jnp.log(total)
            for first in range(0, COLS, blk):
                out_ref[(start + first) // blk, here, :] = attended[
                    :, first : first + blk
                ].astype(jnp.bfloat16)


def backward_kernel(
    do_ref,
    qkv_ref,
    lse_ref,
    o_ref,
    cos_ref,
    sin_ref,
    bias_ref,
    keep_ref,
    seq_ref,
    w_ref,
    g_ref,
    ga_ref,
    gain_ref,
    dk_ref,
    dv_ref,
):
    span, full_len = o_ref.shape
    group = span // HD
    half = HD // 2
    blk = do_ref.shape[2]
    for head in range(group):
        here = slice(head * HD, (head + 1) * HD)
        keys_turned = qkv_ref[span + head * HD : span + (head + 1) * HD]
        keys = keys_turned.T
        values = qkv_ref[2 * span + head * HD : 2 * span + (head + 1) * HD].T
        for start in range(0, full_len, COLS):
            cols = slice(start, start + COLS)
            query = qkv_ref[here, cols]
            grad_out = jnp.concatenate(
                [do_ref[(start + first) // blk, here, :] for first in range(0, COLS, blk)], 1
            )
            grad_out = grad_out.astype(jnp.float32) * keep_ref[:, cols]
            delta = jnp.sum(grad_out * o_ref[here, cols], 0, keepdims=True)
            grad_out = grad_out.astype(jnp.bfloat16)
            scores = product(keys, query) + bias_ref[...]
            probs = jnp.exp(scores - lse_ref[head : head + 1, cols])
            grad_scores = (probs * (product(values, grad_out) - delta)).astype(jnp.bfloat16)
            grad_value = product(grad_out, probs.astype(jnp.bfloat16), NT)
            grad_key = product(query, grad_scores, NT)
            if start == 0:
                dv_ref[...] = grad_value
                dk_ref[...] = grad_key
            else:
                dv_ref[...] += grad_value
                dk_ref[...] += grad_key
            grad_query = product(keys_turned, grad_scores) * HD ** (-0.5)
            cosine = cos_ref[:, cols]
            sine = sin_ref[:, cols]
            one, two = grad_query[:half], grad_query[half:]
            g_ref[head * HD : head * HD + half, cols] = (one * cosine + two * sine).astype(
                jnp.bfloat16
            )
            g_ref[head * HD + half : (head + 1) * HD, cols] = (
                two * cosine - one * sine
            ).astype(jnp.bfloat16)
        one, two = dk_ref[:half], dk_ref[half:]
        cosine = cos_ref[...]
        sine = sin_ref[...]
        low_at = span + head * HD
        g_ref[low_at : low_at + half] = (one * cosine + two * sine).astype(jnp.bfloat16)
        g_ref[low_at + half : low_at + HD] = (two * cosine - one * sine).astype(jnp.bfloat16)
        g_ref[2 * span + head * HD : 2 * span + (head + 1) * HD] = dv_ref[...].astype(
            jnp.bfloat16
        )
    for start in range(0, full_len, ROWS):
        rows = slice(start, start + ROWS)
        grad_a = product(g_ref[:, rows].T, w_ref[:, : 3 * span], NT)
        x = seq_ref[rows].astype(jnp.float32)
        centre = x - jnp.mean(x, -1, keepdims=True)
        variance = jnp.mean(centre * centre, -1, keepdims=True)
        summed = jnp.sum(grad_a * (centre * lax.rsqrt(variance + EPS)), 0, keepdims=True)
        gain_ref[...] = summed if start == 0 else gain_ref[...] + summed
        for first in range(0, ROWS, blk):
            ga_ref[(start + first) // blk] = grad_a[first : first + blk].astype(jnp.bfloat16)


def mlp_kernel(
    tok_ref,
    att_ref,
    cot_ref,
    gain_ref,
    wout_ref,
    win_ref,
    wdown_ref,
    do_ref,
    gm_ref,
    mixed_ref,
    b_ref,
    hid_ref,
    gg_ref,
    grad_gain_ref,
):
    seqs, local_len, width = tok_ref.shape
    spread = do_ref.shape[0] // seqs
    span = do_ref.shape[1]
    hidden = hid_ref.shape[1]
    resid = jnp.concatenate([tok_ref[k] for k in range(seqs)], 0).astype(jnp.float32)
    att = jnp.concatenate([att_ref[k].T for k in range(seqs)], 0)
    cot = jnp.concatenate([cot_ref[k] for k in range(seqs)], 0)
    mixed = resid + product(att, wout_ref[...])
    mixed_ref[...] = mixed
    centre = mixed - jnp.mean(mixed, -1, keepdims=True)
    inverse = lax.rsqrt(jnp.mean(centre * centre, -1, keepdims=True) + EPS)
    normed = centre * inverse
    b_low = (normed * gain_ref[...]).astype(jnp.bfloat16)
    b_ref[...] = b_low
    for first in range(0, hidden, hidden // 3):
        here = slice(first, first + hidden // 3)
        there = slice(hidden + first, hidden + first + hidden // 3)
        gate_in = product(b_low, win_ref[:, here])
        up_half = product(b_low, win_ref[:, there])
        grad_hid = product(cot, wdown_ref[here], NT)
        normal_cdf = 0.5 * (1.0 + lax.erf(gate_in * INV_ROOT_TWO))
        gelu_out = gate_in * normal_cdf
        hid_ref[:, here] = (gelu_out * up_half).astype(jnp.bfloat16)
        normal_pdf = jnp.exp(-0.5 * gate_in * gate_in) * INV_ROOT_TWO_PI
        gg_ref[:, here] = (grad_hid * up_half * (normal_cdf + gate_in * normal_pdf)).astype(
            jnp.bfloat16
        )
        gg_ref[:, there] = (grad_hid * gelu_out).astype(jnp.bfloat16)
    grad_b = product(gg_ref[...], win_ref[...], NT)
    grad_gain_ref[...] = jnp.sum(grad_b * normed, 0, keepdims=True)
    scaled = grad_b * gain_ref[...]
    grad_mixed = cot.astype(jnp.float32) + inverse * (
        scaled
        - jnp.mean(scaled, -1, keepdims=True)
        - normed * jnp.mean(scaled * normed, -1, keepdims=True)
    )
    gm_ref[...] = grad_mixed
    grad_heads = product(wout_ref[...], grad_mixed.astype(jnp.bfloat16), NT).astype(jnp.bfloat16)
    for seq in range(seqs):
        for part in range(spread):
            do_ref[seq * spread + part] = grad_heads[
                part * span : (part + 1) * span, seq * local_len : (seq + 1) * local_len
            ]


def mlp_weights_kernel(
    core_ref,
    att_ref,
    cot_ref,
    wdown_ref,
    gm_ref,
    mixed_ref,
    b_ref,
    hid_ref,
    gg_ref,
    out_ref,
    kept_ref,
    away_ref,
    extra_ref,
    in_ref,
    up_ref,
    down_ref,
):
    seqs, _, local_len = att_ref.shape
    width = cot_ref.shape[2]
    ctx, pairs, chunk, _ = kept_ref.shape
    depth = in_ref.shape[0] // (2 * pairs)
    down_rows = down_ref.shape[0] // (2 * pairs)
    count = in_ref.shape[1] // width
    split = ctx * chunk - (count + 1) * depth
    cot = jnp.concatenate([cot_ref[k] for k in range(seqs)], 0)
    att = jnp.concatenate([att_ref[k] for k in range(seqs)], 1)
    in_ref[...] = product(b_ref[...].T, gg_ref[...])
    up_ref[...] = product(att, gm_ref[...].astype(jnp.bfloat16))
    down_ref[...] = product(hid_ref[...].T, cot)
    core = core_ref[0]
    for pair in range(pairs):
        for ref, which in ((kept_ref, core), (away_ref, 1 - core)):
            wide = pl.ds(pl.multiple_of((2 * pair + which) * depth, 8), depth)
            tall = pl.ds(pl.multiple_of((2 * pair + which) * down_rows, 8), split)
            rows = jnp.concatenate(
                [in_ref[wide, k * width : (k + 1) * width] for k in range(count)]
                + [up_ref[wide], down_ref[tall]],
                0,
            ).astype(jnp.bfloat16)
            for part in range(ctx):
                ref[part, pair] = rows[part * chunk : (part + 1) * chunk]
    for owner in range(2 * pairs):
        extra_ref[owner] = down_ref[owner * down_rows + split : (owner + 1) * down_rows]
    result = mixed_ref[...] + product(hid_ref[...], wdown_ref[...])
    for seq in range(seqs):
        out_ref[seq] = result[seq * local_len : (seq + 1) * local_len].astype(jnp.bfloat16)


def qkv_weights_kernel(
    core_ref, a_ref, g_ref, gain_one_ref, gain_two_ref, extra_ref, kept_ref, away_ref, w_ref
):
    pairs, depth, width = kept_ref.shape
    span3 = g_ref.shape[0]
    used = width - 128
    w_ref[:, :span3] = product(a_ref[...].T, g_ref[...], NT)
    lane = used - 128
    gains = jnp.concatenate(
        [
            jnp.zeros((span3 - lane, width), jnp.float32),
            gain_one_ref[...],
            gain_two_ref[...],
            jnp.zeros((used - span3 - 2, width), jnp.float32),
        ],
        0,
    ).T
    w_ref[:, span3:used] = gains[:, span3 - lane :]
    for owner in range(2 * pairs):
        extra = extra_ref[owner]
        w_ref[owner * depth : (owner + 1) * depth, used:] = jnp.concatenate(
            [extra[:, k * 128 : (k + 1) * 128] for k in range(width // 128)], 0
        )
    core = core_ref[0]
    for pair in range(pairs):
        for ref, which in ((kept_ref, core), (away_ref, 1 - core)):
            rows = pl.ds(pl.multiple_of((2 * pair + which) * depth, 8), depth)
            ref[pair] = w_ref[rows].astype(jnp.bfloat16)


def on_device(kernel, outs, args, scratch=(), scalars=0, name=None):
    space = pl.BlockSpec(memory_space=pltpu.VMEM)
    scalar = pl.BlockSpec(memory_space=pltpu.SMEM)
    return pl.pallas_call(
        kernel,
        out_shape=[jax.ShapeDtypeStruct(shape, dtype) for shape, dtype in outs],
        in_specs=[scalar] * scalars + [space] * (len(args) - scalars),
        out_specs=[space] * len(outs),
        scratch_shapes=list(scratch),
        compiler_params=pltpu.CompilerParams(vmem_limit_bytes=56 * 1024 * 1024),
        name=name,
    )(*args)


def body(tokens, lengths, deal, gain_attn, w_qkv, w_out, gain_mlp, w_in, w_down, cotangent):
    seqs, local_len, width = tokens.shape
    ctx = lax.axis_size("ctx")
    fsdp = lax.axis_size("fsdp")
    spread = ctx // seqs
    group = HEADS // spread
    span = group * HD
    full_len = local_len * ctx
    rows = seqs * local_len
    context = lax.axis_index("ctx")
    own_seq = context // spread
    own_group = context % spread
    depth = w_qkv.shape[0]
    hidden = w_in.shape[1] // 2
    down_rows = w_down.shape[0]
    f32 = jnp.float32

    offsets = jnp.arange(BLK, dtype=jnp.int32)
    all_pos = (deal[:, None] * BLK + offsets[None, :]).reshape(full_len)
    length = lax.dynamic_slice_in_dim(lengths, own_seq, 1)[0]
    all_keep = all_pos < length

    qkv_own = lax.dynamic_index_in_dim(
        w_qkv.reshape(depth, 3, spread, span), own_group, 2, keepdims=False
    ).reshape(depth, 3 * span)
    gains_wide = jnp.stack([gain_attn, gain_mlp], 1)
    fill = jnp.zeros((depth, 640 - 3 * span - 2), jnp.bfloat16)
    first_all = gather_doubling(
        jnp.concatenate([qkv_own, gains_wide, fill], 1), "fsdp"
    ).reshape(fsdp * depth, 640)
    sequence = lax.all_to_all(jnp.repeat(tokens, spread, axis=0), "ctx", 0, 0, tiled=True)

    win_all = lax.all_gather(w_in, "fsdp", axis=0, tiled=True)
    stacked, sequence, first_all = lax.optimization_barrier(
        (jnp.concatenate([w_out, w_down], 0), sequence, first_all)
    )
    stacked_all = gather_two_level(stacked, "fsdp")

    gain_one = first_all[:, 3 * span]
    gain_two = first_all[:, 3 * span + 1]

    cosine, sine = tables(all_pos)
    bias = jnp.where(all_keep, 0.0, NEGATIVE).astype(f32)[:, None]
    keep_row = all_keep.astype(f32)[None, :]
    sequence = sequence.reshape(full_len, width)
    attended, a_low, qkv, log_total, unrounded = on_device(
        forward_kernel,
        [
            ((ctx, span, local_len), jnp.bfloat16),
            ((full_len, width), jnp.bfloat16),
            ((3 * span, full_len), jnp.bfloat16),
            ((8, full_len), f32),
            ((span, full_len), f32),
        ],
        (sequence, first_all, cosine, sine, bias, keep_row),
        name="attention_forward",
    )
    att_back = lax.all_to_all(attended, "ctx", 0, 0, tiled=True)
    att_turned = att_back.reshape(seqs, width, local_len)

    def whole(start, height):
        halves = [part[:, start : start + height] for part in stacked_all]
        return jnp.stack(halves, 1).reshape(fsdp * height, width)

    wout_all = whole(0, depth)
    wdown_all = whole(depth, down_rows)

    resid = tokens.astype(f32).reshape(rows, width)
    count = w_in.shape[1] // width
    main_rows = ((count + 1) * depth + down_rows) // (8 * ctx) * 8 * ctx
    chunk = main_rows // ctx
    split = main_rows - (count + 1) * depth
    extra = down_rows - split
    pairs = fsdp // 2
    core = (lax.axis_index("fsdp") % 2).astype(jnp.int32)[None]
    grad_heads, grad_mixed, mixed, b_low, hid_low, grad_gate_up, grad_gain_two = on_device(
        mlp_kernel,
        [
            ((ctx, span, local_len), jnp.bfloat16),
            ((rows, width), f32),
            ((rows, width), f32),
            ((rows, width), jnp.bfloat16),
            ((rows, hidden), jnp.bfloat16),
            ((rows, 2 * hidden), jnp.bfloat16),
            ((1, width), f32),
        ],
        (
            tokens,
            att_turned,
            cotangent,
            gain_two.astype(f32)[None, :],
            wout_all,
            win_all,
            wdown_all,
        ),
        name="mlp",
    )
    output, main_kept, main_away, down_extra = on_device(
        mlp_weights_kernel,
        [
            (tokens.shape, jnp.bfloat16),
            ((ctx, pairs, chunk, width), jnp.bfloat16),
            ((ctx, pairs, chunk, width), jnp.bfloat16),
            ((fsdp, extra, width), f32),
        ],
        (
            core,
            att_turned,
            cotangent,
            wdown_all,
            grad_mixed,
            mixed,
            b_low,
            hid_low,
            grad_gate_up,
        ),
        [
            pltpu.VMEM((fsdp * depth, 2 * hidden), f32),
            pltpu.VMEM((width, width), f32),
            pltpu.VMEM((hidden, width), f32),
        ],
        scalars=1,
        name="mlp_weights",
    )
    main_pair = core_sum(main_kept, main_away, "fsdp")
    main_part = lax.psum_scatter(
        main_pair.reshape(-1, chunk, width), "ctx", scatter_dimension=0, tiled=True
    )
    main_part = lax.optimization_barrier(main_part)

    all_grad = lax.all_to_all(grad_heads, "ctx", 0, 0, tiled=True)
    grad_qkv, grad_a_part, grad_gain_one = on_device(
        backward_kernel,
        [
            ((3 * span, full_len), jnp.bfloat16),
            ((ctx, local_len, width), jnp.bfloat16),
            ((1, width), f32),
        ],
        (
            all_grad,
            qkv,
            log_total,
            unrounded,
            cosine,
            sine,
            bias,
            keep_row,
            sequence,
            first_all,
        ),
        [pltpu.VMEM((HD, full_len), f32)] * 2,
        name="attention_backward",
    )
    grad_a_parts = lax.all_to_all(grad_a_part, "ctx", 0, 0, tiled=True)
    last_kept, last_away = on_device(
        qkv_weights_kernel,
        [((pairs, depth, width), jnp.bfloat16)] * 2,
        (core, a_low, grad_qkv, grad_gain_one, grad_gain_two, down_extra),
        [pltpu.VMEM((width, width), f32)],
        scalars=1,
        name="qkv_weights",
    )
    last = core_sum(last_kept, last_away, "fsdp")
    grad_a = jnp.sum(
        grad_a_parts.reshape(seqs, spread, local_len, width).astype(f32), 1
    ).reshape(rows, width)
    _, normed_one, inverse_one = norm_forward(resid, gain_one)
    grad_norm_one, _ = norm_backward(grad_a, gain_one, normed_one, inverse_one)
    grad_input = grad_mixed + grad_norm_one

    last = spread_sum(last, "fsdp")
    main_part = spread_sum(main_part, "fsdp")
    share = jnp.concatenate([last, main_part], 0)
    ends = gather_by_exchange(share, "ctx", ctx)
    last_all = ends[:, :depth].astype(f32)
    down_end = jnp.sum(last_all[:, :, width - 128 :], 0)
    down_end = down_end.reshape(-1, extra, 128).transpose(1, 0, 2).reshape(extra, width)
    summed = ends[:, depth:].reshape(main_rows, width).astype(f32)
    grad_wqkv_out = (
        jnp.sum(last_all[:, :, : 3 * span].reshape(seqs, spread, depth, 3, span), 0)
        .transpose(1, 2, 0, 3)
        .reshape(depth, 3 * width)
    )
    gains_out = jnp.sum(last_all[:, :, 3 * span : 3 * span + 2], 0)
    return (
        output,
        grad_input.reshape(tokens.shape),
        gains_out[:, 0],
        grad_wqkv_out,
        summed[count * depth : (count + 1) * depth],
        gains_out[:, 1],
        jnp.concatenate([summed[k * depth : (k + 1) * depth] for k in range(count)], 1),
        jnp.concatenate([summed[(count + 1) * depth :], down_end], 0),
    )


def solution(mesh):
    placed = (
        P("fsdp", "ctx", None),
        P("fsdp"),
        P(),
        P("fsdp"),
        P("fsdp", None),
        P("fsdp", None),
        P("fsdp"),
        P("fsdp", None),
        P("fsdp", None),
        P("fsdp", "ctx", None),
    )
    return jax.shard_map(
        body,
        mesh=mesh,
        in_specs=placed,
        out_specs=(
            P("fsdp", "ctx", None),
            P("fsdp", "ctx", None),
            P("fsdp"),
            P("fsdp", None),
            P("fsdp", None),
            P("fsdp"),
            P("fsdp", None),
            P("fsdp", None),
        ),
        check_vma=False,
    )
```

```python
import math

import jax
import jax.numpy as jnp
from jax import lax
from jax.experimental import pallas as pl
from jax.experimental.pallas import tpu as pltpu
from jax.sharding import PartitionSpec as P

HEADS = 12
HD = 64
BLK = 128


EPS = 1e-05
THETA = 160000.0
NEGATIVE = -1e30
INV_ROOT_TWO = 0.7071067811865476
INV_ROOT_TWO_PI = 0.3989422804014327


def gather_by_exchange(part, axis, n):
    return lax.all_to_all(jnp.broadcast_to(part[None], (n, *part.shape)), axis, 0, 0)


def core_pairs(n):
    return [(k, k ^ 1) for k in range(n)]


def core_groups(n):
    return [list(range(first, n, 2)) for first in range(2)]


def gather_doubling(part, axis):
    n = lax.axis_size(axis)
    index = lax.axis_index(axis)
    held = part[None]
    bit = n // 2
    while bit:
        came = lax.ppermute(held, axis, [(k, k ^ bit) for k in range(n)])
        first = (index & bit) == 0
        held = jnp.where(first, jnp.stack([held, came], 1), jnp.stack([came, held], 1))
        held = held.reshape(-1, *part.shape)
        bit //= 2
    return held


def gather_two_level(part, axis):
    n = lax.axis_size(axis)
    mine = lax.all_to_all(
        jnp.broadcast_to(part[None], (n // 2, *part.shape)),
        axis,
        0,
        0,
        axis_index_groups=core_groups(n),
    )
    other = lax.ppermute(mine, axis, core_pairs(n))
    even = lax.axis_index(axis) % 2 == 0
    return mine, (jnp.where(even, mine, other), jnp.where(even, other, mine))


def core_sum(kept, away, axis, micros, after=(), name=None):
    came = lax.ppermute(away, axis, core_pairs(lax.axis_size(axis)))
    return on_device(
        sum_kernel, [(kept.shape, jnp.bfloat16)], (kept, came), micros, after=after, name=name
    )[0]


def spread_sum(parts, axis):
    groups = core_groups(lax.axis_size(axis))
    shares = lax.all_to_all(parts, axis, 0, 0, tiled=True, axis_index_groups=groups)
    return low(jnp.sum(shares.astype(jnp.float32), 0))


def low(values):
    return values.astype(jnp.bfloat16)


def tables(positions):
    halves = jnp.arange(HD // 2, dtype=jnp.float32)
    frequency = THETA ** (-2.0 * halves / HD)
    angles = frequency[:, None] * positions.astype(jnp.float32)[None, :]
    return jnp.cos(angles), jnp.sin(angles)


def norm_forward(rows_in, gain):
    centre = rows_in - jnp.mean(rows_in, -1, keepdims=True)
    variance = jnp.mean(centre * centre, -1, keepdims=True)
    inverse = lax.rsqrt(variance + EPS)
    normed = centre * inverse
    return (normed * gain.astype(jnp.float32), normed, inverse)


def norm_backward(grad_rows, gain, normed, inverse):
    scaled = grad_rows * gain.astype(jnp.float32)
    grad_gain = jnp.sum(grad_rows * normed, 0)
    grad_rows_in = inverse * (
        scaled
        - jnp.mean(scaled, -1, keepdims=True)
        - normed * jnp.mean(scaled * normed, -1, keepdims=True)
    )
    return (grad_rows_in, grad_gain)


NN = (((1,), (0,)), ((), ()))
NT = (((1,), (1,)), ((), ()))
ROWS = 256
COLS = 256


def product(left, right, dims=NN):
    return lax.dot_general(left, right, dims, preferred_element_type=jnp.float32)


def forward_kernel(
    seq_ref,
    w_ref,
    cos_ref,
    sin_ref,
    bias_ref,
    keep_ref,
    out_ref,
    a_ref,
    qkv_ref,
    lse_ref,
    o_ref,
    mean_ref,
    inverse_ref,
):
    full_len, width = seq_ref.shape
    span = o_ref.shape[0]
    group = span // HD
    half = HD // 2
    blk = out_ref.shape[2]
    gain = w_ref[:, 512:640].astype(jnp.float32).T[3 * span - 512 : 3 * span - 511]
    w_turned = w_ref[:, : 3 * span].astype(jnp.float32).T.astype(jnp.bfloat16)
    for start in range(0, full_len, ROWS):
        rows = slice(start, start + ROWS)
        x = seq_ref[rows].astype(jnp.float32)
        mean = jnp.mean(x, -1, keepdims=True)
        centre = x - mean
        inverse = lax.rsqrt(jnp.mean(centre * centre, -1, keepdims=True) + EPS)
        mean_ref[rows] = mean
        inverse_ref[rows] = inverse
        a_low = (centre * inverse * gain).astype(jnp.bfloat16)
        a_ref[rows] = a_low
        joined = product(w_turned, a_low, NT)
        cosine = cos_ref[:, rows]
        sine = sin_ref[:, rows]
        for part in range(2 * group):
            one = joined[part * HD : part * HD + half]
            two = joined[part * HD + half : (part + 1) * HD]
            scale = HD ** (-0.5) if part < group else 1.0
            for at, value in (
                (0, one * cosine - two * sine),
                (half, two * cosine + one * sine),
            ):
                qkv_ref[part * HD + at : part * HD + at + half, rows] = (
                    value.astype(jnp.bfloat16) * scale
                ).astype(jnp.bfloat16)
        qkv_ref[2 * span :, rows] = joined[2 * span :].astype(jnp.bfloat16)
    for head in range(group):
        here = slice(head * HD, (head + 1) * HD)
        keys = qkv_ref[span + head * HD : span + (head + 1) * HD].T
        values = qkv_ref[2 * span + head * HD : 2 * span + (head + 1) * HD]
        for start in range(0, full_len, COLS):
            cols = slice(start, start + COLS)
            scores = product(keys, qkv_ref[here, cols]) + bias_ref[...]
            maximum = jnp.max(scores, 0, keepdims=True)
            exponent = jnp.exp(scores - maximum)
            total = jnp.sum(exponent, 0, keepdims=True)
            attended = product(values, exponent.astype(jnp.bfloat16))
            attended = attended * (keep_ref[:, cols] / total)
            o_ref[here, cols] = attended
            lse_ref[head : head + 1, cols] = maximum + jnp.log(total)
            for first in range(0, COLS, blk):
                out_ref[(start + first) // blk, here, :] = attended[
                    :, first : first + blk
                ].astype(jnp.bfloat16)


def backward_kernel(
    do_ref,
    qkv_ref,
    lse_ref,
    o_ref,
    cos_ref,
    sin_ref,
    bias_ref,
    keep_ref,
    seq_ref,
    mean_ref,
    inverse_ref,
    w_ref,
    g_ref,
    ga_ref,
    gain_ref,
    dk_ref,
    dv_ref,
):
    span, full_len = o_ref.shape
    group = span // HD
    half = HD // 2
    blk = do_ref.shape[2]
    for head in range(group):
        here = slice(head * HD, (head + 1) * HD)
        keys_turned = qkv_ref[span + head * HD : span + (head + 1) * HD]
        keys = keys_turned.T
        values = qkv_ref[2 * span + head * HD : 2 * span + (head + 1) * HD].T
        for start in range(0, full_len, COLS):
            cols = slice(start, start + COLS)
            query = qkv_ref[here, cols]
            grad_out = jnp.concatenate(
                [do_ref[(start + first) // blk, here, :] for first in range(0, COLS, blk)], 1
            )
            grad_out = grad_out.astype(jnp.float32) * keep_ref[:, cols]
            delta = jnp.sum(grad_out * o_ref[here, cols], 0, keepdims=True)
            grad_out = grad_out.astype(jnp.bfloat16)
            scores = product(keys, query) + bias_ref[...]
            probs = jnp.exp(scores - lse_ref[head : head + 1, cols])
            grad_scores = (probs * (product(values, grad_out) - delta)).astype(jnp.bfloat16)
            grad_value = product(grad_out, probs.astype(jnp.bfloat16), NT)
            grad_key = product(query, grad_scores, NT)
            if start == 0:
                dv_ref[...] = grad_value
                dk_ref[...] = grad_key
            else:
                dv_ref[...] += grad_value
                dk_ref[...] += grad_key
            grad_query = product(keys_turned, grad_scores) * HD ** (-0.5)
            cosine = cos_ref[:, cols]
            sine = sin_ref[:, cols]
            one, two = grad_query[:half], grad_query[half:]
            g_ref[head * HD : head * HD + half, cols] = (one * cosine + two * sine).astype(
                jnp.bfloat16
            )
            g_ref[head * HD + half : (head + 1) * HD, cols] = (
                two * cosine - one * sine
            ).astype(jnp.bfloat16)
        one, two = dk_ref[:half], dk_ref[half:]
        cosine = cos_ref[...]
        sine = sin_ref[...]
        low_at = span + head * HD
        g_ref[low_at : low_at + half] = (one * cosine + two * sine).astype(jnp.bfloat16)
        g_ref[low_at + half : low_at + HD] = (two * cosine - one * sine).astype(jnp.bfloat16)
        g_ref[2 * span + head * HD : 2 * span + (head + 1) * HD] = dv_ref[...].astype(
            jnp.bfloat16
        )
    for start in range(0, full_len, ROWS):
        rows = slice(start, start + ROWS)
        grad_a = product(g_ref[:, rows].T, w_ref[:, : 3 * span], NT)
        normed = (seq_ref[rows].astype(jnp.float32) - mean_ref[rows]) * inverse_ref[rows]
        summed = jnp.sum(grad_a * normed, 0, keepdims=True)
        gain_ref[...] = summed if start == 0 else gain_ref[...] + summed
        for first in range(0, ROWS, blk):
            ga_ref[(start + first) // blk] = grad_a[first : first + blk].astype(jnp.bfloat16)


def mlp_kernel(
    tok_ref,
    att_ref,
    cot_ref,
    gain_ref,
    wout_ref,
    win_ref,
    wdown_ref,
    do_ref,
    gm_ref,
    mixed_ref,
    b_ref,
    hid_ref,
    gg_ref,
    grad_gain_ref,
):
    seqs, local_len, width = tok_ref.shape
    spread = do_ref.shape[0] // seqs
    span = do_ref.shape[1]
    hidden = hid_ref.shape[1]
    resid = jnp.concatenate([tok_ref[k] for k in range(seqs)], 0).astype(jnp.float32)
    att = jnp.concatenate([att_ref[k].T for k in range(seqs)], 0)
    cot = jnp.concatenate([cot_ref[k] for k in range(seqs)], 0)
    mixed = resid + product(att, wout_ref[...])
    mixed_ref[...] = mixed
    centre = mixed - jnp.mean(mixed, -1, keepdims=True)
    inverse = lax.rsqrt(jnp.mean(centre * centre, -1, keepdims=True) + EPS)
    normed = centre * inverse
    b_low = (normed * gain_ref[...]).astype(jnp.bfloat16)
    b_ref[...] = b_low
    for first in range(0, hidden, hidden // 3):
        here = slice(first, first + hidden // 3)
        there = slice(hidden + first, hidden + first + hidden // 3)
        gate_in = product(b_low, win_ref[:, here])
        up_half = product(b_low, win_ref[:, there])
        grad_hid = product(cot, wdown_ref[here], NT)
        normal_cdf = 0.5 * (1.0 + lax.erf(gate_in * INV_ROOT_TWO))
        gelu_out = gate_in * normal_cdf
        hid_ref[:, here] = (gelu_out * up_half).astype(jnp.bfloat16)
        normal_pdf = jnp.exp(-0.5 * gate_in * gate_in) * INV_ROOT_TWO_PI
        gg_ref[:, here] = (grad_hid * up_half * (normal_cdf + gate_in * normal_pdf)).astype(
            jnp.bfloat16
        )
        gg_ref[:, there] = (grad_hid * gelu_out).astype(jnp.bfloat16)
    grad_b = product(gg_ref[...], win_ref[...], NT)
    grad_gain_ref[...] = jnp.sum(grad_b * normed, 0, keepdims=True)
    scaled = grad_b * gain_ref[...]
    grad_mixed = cot.astype(jnp.float32) + inverse * (
        scaled
        - jnp.mean(scaled, -1, keepdims=True)
        - normed * jnp.mean(scaled * normed, -1, keepdims=True)
    )
    gm_ref[...] = grad_mixed
    grad_heads = product(wout_ref[...], grad_mixed.astype(jnp.bfloat16), NT).astype(jnp.bfloat16)
    for seq in range(seqs):
        for part in range(spread):
            do_ref[seq * spread + part] = grad_heads[
                part * span : (part + 1) * span, seq * local_len : (seq + 1) * local_len
            ]


def half_weights(which, att_ref, cot_ref, gm_ref, b_ref, hid_ref, gg_ref, part_ref, extra_ref, turned, tall):
    seqs, width, local_len = att_ref.shape
    ctx, pairs, chunk, _ = part_ref.shape
    count = gg_ref.shape[1] // width
    depth = width // (2 * pairs)
    down_rows = hid_ref.shape[1] // (2 * pairs)
    split = ctx * chunk - (count + 1) * depth
    cot = jnp.concatenate([cot_ref[k] for k in range(seqs)], 0)
    turned[:width] = b_ref[...].astype(jnp.float32).T
    turned[width : 2 * width] = jnp.concatenate(
        [att_ref[k] for k in range(seqs)], 1
    ).astype(jnp.float32)
    turned[2 * width :] = hid_ref[...].astype(jnp.float32).T

    def chosen(first, height):
        return jnp.concatenate(
            [
                turned[pl.ds(pl.multiple_of(first + (2 * k + which) * height, 8), height)]
                for k in range(pairs)
            ],
            0,
        ).astype(jnp.bfloat16)

    grad_up = product(chosen(width, depth), gm_ref[...].astype(jnp.bfloat16))
    tall[...] = product(chosen(2 * width, down_rows), cot)
    grad_in = product(chosen(0, depth), gg_ref[...])
    for pair in range(pairs):
        wide = slice(pair * depth, (pair + 1) * depth)
        rows = jnp.concatenate(
            [grad_in[wide, k * width : (k + 1) * width] for k in range(count)]
            + [grad_up[wide], tall[pair * down_rows : pair * down_rows + split]],
            0,
        ).astype(jnp.bfloat16)
        for part in range(ctx):
            part_ref[part, pair] = rows[part * chunk : (part + 1) * chunk]
        extra_ref[pair] = tall[pair * down_rows + split : (pair + 1) * down_rows]


def sent_weights_kernel(core_ref, *refs):
    half_weights(1 - core_ref[0], *refs)


def kept_weights_kernel(
    core_ref,
    att_ref,
    cot_ref,
    gm_ref,
    b_ref,
    hid_ref,
    gg_ref,
    wdown_ref,
    mixed_ref,
    part_ref,
    extra_ref,
    out_ref,
    turned,
    tall,
):
    half_weights(
        core_ref[0],
        att_ref,
        cot_ref,
        gm_ref,
        b_ref,
        hid_ref,
        gg_ref,
        part_ref,
        extra_ref,
        turned,
        tall,
    )
    local_len = out_ref.shape[1]
    result = mixed_ref[...] + product(hid_ref[...], wdown_ref[...])
    for seq in range(out_ref.shape[0]):
        out_ref[seq] = result[seq * local_len : (seq + 1) * local_len].astype(jnp.bfloat16)


def qkv_weights_kernel(
    core_ref,
    a_ref,
    g_ref,
    gain_one_ref,
    gain_two_ref,
    kept_extra_ref,
    away_extra_ref,
    kept_ref,
    away_ref,
    w_ref,
):
    pairs, depth, width = kept_ref.shape
    span3 = g_ref.shape[0]
    used = width - 128
    w_ref[:, :span3] = product(a_ref[...].T, g_ref[...], NT)
    lane = used - 128
    gains = jnp.concatenate(
        [
            jnp.zeros((span3 - lane, width), jnp.float32),
            gain_one_ref[...],
            gain_two_ref[...],
            jnp.zeros((used - span3 - 2, width), jnp.float32),
        ],
        0,
    ).T
    w_ref[:, span3:] = gains[:, span3 - lane :]
    core = core_ref[0]
    for pair in range(pairs):
        for ref, extra_ref, which in (
            (kept_ref, kept_extra_ref, core),
            (away_ref, away_extra_ref, 1 - core),
        ):
            rows = pl.ds(pl.multiple_of((2 * pair + which) * depth, 8), depth)
            extra = extra_ref[pair]
            ref[pair] = jnp.concatenate(
                [
                    w_ref[rows],
                    jnp.concatenate(
                        [extra[:, k * 128 : (k + 1) * 128] for k in range(width // 128)], 0
                    ),
                ],
                1,
            ).astype(jnp.bfloat16)


def first_kernel(group_ref, w_ref, gains_ref, out_ref):
    depth, used = out_ref.shape
    spread = 4
    span = w_ref.shape[1] // (3 * spread)
    own_group = group_ref[0]
    gains = gains_ref[...]

    for which in range(spread):

        @pl.when(own_group == which)
        def _():
            picked = [
                w_ref[
                    :, (k * spread + which) * span : (k * spread + which + 1) * span
                ].astype(jnp.float32)
                for k in range(3)
            ]
            out_ref[...] = jnp.concatenate([*picked, gains], 1).astype(jnp.bfloat16)


def finish_kernel(
    ends_ref, gain_one_ref, qkv_ref, wout_ref, gain_two_ref, win_ref, wdown_ref
):
    ctx, _, width = ends_ref.shape
    depth = qkv_ref.shape[0]
    down_rows = wdown_ref.shape[0]
    count = win_ref.shape[1] // width
    spread = ctx // 2
    span = width // spread
    f32 = jnp.float32
    last = [ends_ref[k, :depth].astype(f32) for k in range(ctx)]
    for group in range(spread):
        both = last[group] + last[group + spread]
        for part in range(3):
            qkv_ref[:, part * width + group * span : part * width + (group + 1) * span] = both[
                :, part * span : (part + 1) * span
            ]
    total = last[0]
    for k in range(1, ctx):
        total = total + last[k]
    lane = 3 * span // 128 * 128
    gains = total[:, lane : lane + 128].T
    gain_one_ref[...] = gains[3 * span - lane : 3 * span - lane + 1]
    gain_two_ref[...] = gains[3 * span - lane + 1 : 3 * span - lane + 2]
    main = jnp.concatenate([ends_ref[k, depth:].astype(f32) for k in range(ctx)], 0)
    for k in range(count):
        win_ref[:, k * width : (k + 1) * width] = main[k * depth : (k + 1) * depth]
    wout_ref[...] = main[count * depth : (count + 1) * depth]
    split = main.shape[0] - (count + 1) * depth
    extra = down_rows - split
    wdown_ref[:split] = main[(count + 1) * depth :]
    wdown_ref[split:] = jnp.concatenate(
        [total[k * extra : (k + 1) * extra, width - 128 :] for k in range(width // 128)], 1
    )


def on_device(kernel, outs, args, micros, scratch=(), scalars=0, after=(), name=None):
    space = pl.BlockSpec(memory_space=pltpu.VMEM)
    scalar = pl.BlockSpec(memory_space=pltpu.SMEM)
    given = len(args)

    def ordered(*refs):
        kernel(*refs[:given], *refs[given + len(after) :])

    return pl.pallas_call(
        ordered,
        out_shape=[jax.ShapeDtypeStruct(shape, dtype) for shape, dtype in outs],
        in_specs=[scalar] * scalars
        + [space] * (given - scalars)
        + [pl.BlockSpec(memory_space=pl.ANY)] * len(after),
        out_specs=[space] * len(outs),
        scratch_shapes=list(scratch),
        compiler_params=pltpu.CompilerParams(vmem_limit_bytes=56 * 1024 * 1024),
        cost_estimate=pl.CostEstimate(
            flops=int(micros * 2e10), bytes_accessed=int(micros * 4e7), transcendentals=0
        ),
        name=name,
    )(*args, *after)


def sum_kernel(left_ref, right_ref, out_ref):
    for k in range(out_ref.shape[0]):
        out_ref[k] = (left_ref[k].astype(jnp.float32) + right_ref[k].astype(jnp.float32)).astype(
            jnp.bfloat16
        )


def spread_kernel(tokens_ref, out_ref):
    copies = out_ref.shape[0] // tokens_ref.shape[0]
    for k in range(out_ref.shape[0]):
        out_ref[k] = tokens_ref[k // copies]


def body(tokens, lengths, deal, gain_attn, w_qkv, w_out, gain_mlp, w_in, w_down, cotangent):
    seqs, local_len, width = tokens.shape
    ctx = lax.axis_size("ctx")
    fsdp = lax.axis_size("fsdp")
    spread = ctx // seqs
    group = HEADS // spread
    span = group * HD
    full_len = local_len * ctx
    rows = seqs * local_len
    context = lax.axis_index("ctx")
    own_seq = context // spread
    own_group = context % spread
    depth = w_qkv.shape[0]
    hidden = w_in.shape[1] // 2
    down_rows = w_down.shape[0]
    f32 = jnp.float32

    offsets = jnp.arange(BLK, dtype=jnp.int32)
    all_pos = (deal[:, None] * BLK + offsets[None, :]).reshape(full_len)
    length = lax.dynamic_slice_in_dim(lengths, own_seq, 1)[0]
    all_keep = all_pos < length

    used = 3 * span + 64
    gains_wide = jnp.pad(
        jnp.stack([gain_attn, gain_mlp], 1).astype(f32), ((0, 0), (0, used - 3 * span - 2))
    )
    first = on_device(
        first_kernel,
        [((depth, used), jnp.bfloat16)],
        (own_group.astype(jnp.int32)[None], w_qkv, gains_wide),
        1,
        scalars=1,
        name="first_pack",
    )[0]
    first_all = gather_doubling(first, "fsdp").reshape(fsdp * depth, used)
    win_all = lax.all_gather(w_in, "fsdp", axis=0, tiled=True)
    stacked_mine, stacked_all = gather_two_level(jnp.concatenate([w_out, w_down], 0), "fsdp")
    to_send = on_device(
        spread_kernel,
        [((ctx, local_len, width), jnp.bfloat16)],
        (tokens,),
        1,
        after=(stacked_mine,),
        name="spread_tokens",
    )[0]
    sequence = lax.all_to_all(to_send, "ctx", 0, 0, tiled=True)
    gain_one = first_all[:, 3 * span]
    gain_two = first_all[:, 3 * span + 1]

    cosine, sine = tables(all_pos)
    bias = jnp.where(all_keep, 0.0, NEGATIVE).astype(f32)[:, None]
    keep_row = all_keep.astype(f32)[None, :]
    sequence = sequence.reshape(full_len, width)
    attended, a_low, qkv, log_total, unrounded, mean, inverse = on_device(
        forward_kernel,
        [
            ((ctx, span, local_len), jnp.bfloat16),
            ((full_len, width), jnp.bfloat16),
            ((3 * span, full_len), jnp.bfloat16),
            ((8, full_len), f32),
            ((span, full_len), f32),
            ((full_len, 1), f32),
            ((full_len, 1), f32),
        ],
        (sequence, first_all, cosine, sine, bias, keep_row),
        12,
        name="attention_forward",
    )
    att_back = lax.all_to_all(attended, "ctx", 0, 0, tiled=True)
    att_turned = att_back.reshape(seqs, width, local_len)

    def whole(start, height):
        halves = [part[:, start : start + height] for part in stacked_all]
        return jnp.stack(halves, 1).reshape(fsdp * height, width)

    wout_all = whole(0, depth)
    wdown_all = whole(depth, down_rows)

    resid = tokens.astype(f32).reshape(rows, width)
    count = w_in.shape[1] // width
    main_rows = ((count + 1) * depth + down_rows) // (8 * ctx) * 8 * ctx
    chunk = main_rows // ctx
    split = main_rows - (count + 1) * depth
    extra = down_rows - split
    pairs = fsdp // 2
    core = (lax.axis_index("fsdp") % 2).astype(jnp.int32)[None]
    grad_heads, grad_mixed, mixed, b_low, hid_low, grad_gate_up, grad_gain_two = on_device(
        mlp_kernel,
        [
            ((ctx, span, local_len), jnp.bfloat16),
            ((rows, width), f32),
            ((rows, width), f32),
            ((rows, width), jnp.bfloat16),
            ((rows, hidden), jnp.bfloat16),
            ((rows, 2 * hidden), jnp.bfloat16),
            ((1, width), f32),
        ],
        (
            tokens,
            att_turned,
            cotangent,
            gain_two.astype(f32)[None, :],
            wout_all,
            win_all,
            wdown_all,
        ),
        9,
        name="mlp",
    )
    weights_in = (core, att_turned, cotangent, grad_mixed, b_low, hid_low, grad_gate_up)
    half_outs = [
        ((ctx, pairs, chunk, width), jnp.bfloat16),
        ((pairs, extra, width), f32),
    ]
    half_scratch = [
        pltpu.VMEM((2 * width + hidden, rows), f32),
        pltpu.VMEM((hidden // 2, width), f32),
    ]
    main_away, away_extra = on_device(
        sent_weights_kernel,
        half_outs,
        weights_in,
        5,
        half_scratch,
        scalars=1,
        name="sent_weights",
    )
    main_kept, kept_extra, output = on_device(
        kept_weights_kernel,
        [*half_outs, (tokens.shape, jnp.bfloat16)],
        (*weights_in, wdown_all, mixed),
        0.05,
        half_scratch,
        scalars=1,
        after=(main_away,),
        name="kept_weights",
    )
    main_pair = core_sum(main_kept, main_away, "fsdp", 0.02, name="sum_cores")
    main_part = lax.psum_scatter(
        main_pair.reshape(-1, chunk, width), "ctx", scatter_dimension=0, tiled=True
    )

    all_grad = lax.all_to_all(grad_heads, "ctx", 0, 0, tiled=True)
    grad_qkv, grad_a_part, grad_gain_one = on_device(
        backward_kernel,
        [
            ((3 * span, full_len), jnp.bfloat16),
            ((ctx, local_len, width), jnp.bfloat16),
            ((1, width), f32),
        ],
        (
            all_grad,
            qkv,
            log_total,
            unrounded,
            cosine,
            sine,
            bias,
            keep_row,
            sequence,
            mean,
            inverse,
            first_all,
        ),
        12,
        [pltpu.VMEM((HD, full_len), f32)] * 2,
        after=(main_pair,),
        name="attention_backward",
    )
    grad_a_parts = lax.all_to_all(grad_a_part, "ctx", 0, 0, tiled=True)
    last_kept, last_away = on_device(
        qkv_weights_kernel,
        [((pairs, depth, width), jnp.bfloat16)] * 2,
        (core, a_low, grad_qkv, grad_gain_one, grad_gain_two, kept_extra, away_extra),
        0.1,
        [pltpu.VMEM((width, used), f32)],
        scalars=1,
        name="qkv_weights",
    )
    last = core_sum(
        last_kept, last_away, "fsdp", 0.05, after=(grad_a_parts,), name="sum_cores_last"
    )
    grad_a = jnp.sum(
        grad_a_parts.reshape(seqs, spread, local_len, width).astype(f32), 1
    ).reshape(rows, width)
    _, normed_one, inverse_one = norm_forward(resid, gain_one)
    grad_norm_one, _ = norm_backward(grad_a, gain_one, normed_one, inverse_one)
    grad_input = grad_mixed + grad_norm_one

    last = spread_sum(last, "fsdp")
    main_part = spread_sum(main_part, "fsdp")
    share = jnp.concatenate([last, main_part], 0)
    ends = gather_by_exchange(share, "ctx", ctx)
    finished = on_device(
        finish_kernel,
        [
            ((1, depth), f32),
            (w_qkv.shape, f32),
            (w_out.shape, f32),
            ((1, depth), f32),
            (w_in.shape, f32),
            (w_down.shape, f32),
        ],
        (ends,),
        3,
        name="finish",
    )
    return (
        output,
        grad_input.reshape(tokens.shape),
        finished[0].reshape(depth),
        finished[1],
        finished[2],
        finished[3].reshape(depth),
        finished[4],
        finished[5],
    )


def solution(mesh):
    placed = (
        P("fsdp", "ctx", None),
        P("fsdp"),
        P(),
        P("fsdp"),
        P("fsdp", None),
        P("fsdp", None),
        P("fsdp"),
        P("fsdp", None),
        P("fsdp", None),
        P("fsdp", "ctx", None),
    )
    return jax.shard_map(
        body,
        mesh=mesh,
        in_specs=placed,
        out_specs=(
            P("fsdp", "ctx", None),
            P("fsdp", "ctx", None),
            P("fsdp"),
            P("fsdp", None),
            P("fsdp", None),
            P("fsdp"),
            P("fsdp", None),
            P("fsdp", None),
        ),
        check_vma=False,
    )
```

```python
import math

import jax
import jax.numpy as jnp
from jax import lax
from jax.experimental import pallas as pl
from jax.experimental.pallas import tpu as pltpu
from jax.sharding import PartitionSpec as P

HEADS = 12
HD = 64
BLK = 128


EPS = 1e-05
THETA = 160000.0
NEGATIVE = -1e30
INV_ROOT_TWO = 0.7071067811865476
INV_ROOT_TWO_PI = 0.3989422804014327


def gather_by_exchange(part, axis, n):
    return lax.all_to_all(jnp.broadcast_to(part[None], (n, *part.shape)), axis, 0, 0)


def core_pairs(n):
    return [(k, k ^ 1) for k in range(n)]


def core_groups(n):
    return [list(range(first, n, 2)) for first in range(2)]


def doubled(held, axis, bit, after=()):
    n = lax.axis_size(axis)
    index = lax.axis_index(axis)
    came = lax.ppermute(held, axis, [(k, k ^ bit) for k in range(n)])
    if after:
        held = on_device(
            interleave_kernel,
            [((held.shape[0], 2, *held.shape[1:]), held.dtype)],
            ((index // bit % 2).astype(jnp.int32)[None], held, came),
            0.02,
            scalars=1,
            after=after,
            name="interleave",
        )[0]
    else:
        first = (index & bit) == 0
        held = jnp.where(first, jnp.stack([held, came], 1), jnp.stack([came, held], 1))
    return held.reshape(-1, *held.shape[2:])


def core_sum(kept, away, axis, micros, after=(), name=None):
    came = lax.ppermute(away, axis, core_pairs(lax.axis_size(axis)))
    return on_device(
        sum_kernel, [(kept.shape, jnp.bfloat16)], (kept, came), micros, after=after, name=name
    )[0]


def spread_sum(parts, axis):
    groups = core_groups(lax.axis_size(axis))
    shares = lax.all_to_all(parts, axis, 0, 0, tiled=True, axis_index_groups=groups)
    return low(jnp.sum(shares.astype(jnp.float32), 0))


def low(values):
    return values.astype(jnp.bfloat16)


def tables(positions):
    halves = jnp.arange(HD // 2, dtype=jnp.float32)
    frequency = THETA ** (-2.0 * halves / HD)
    angles = frequency[:, None] * positions.astype(jnp.float32)[None, :]
    return jnp.cos(angles), jnp.sin(angles)


def norm_forward(rows_in, gain):
    centre = rows_in - jnp.mean(rows_in, -1, keepdims=True)
    variance = jnp.mean(centre * centre, -1, keepdims=True)
    inverse = lax.rsqrt(variance + EPS)
    normed = centre * inverse
    return (normed * gain.astype(jnp.float32), normed, inverse)


def norm_backward(grad_rows, gain, normed, inverse):
    scaled = grad_rows * gain.astype(jnp.float32)
    grad_gain = jnp.sum(grad_rows * normed, 0)
    grad_rows_in = inverse * (
        scaled
        - jnp.mean(scaled, -1, keepdims=True)
        - normed * jnp.mean(scaled * normed, -1, keepdims=True)
    )
    return (grad_rows_in, grad_gain)


NN = (((1,), (0,)), ((), ()))
NT = (((1,), (1,)), ((), ()))
ROWS = 256
COLS = 256


def product(left, right, dims=NN):
    return lax.dot_general(left, right, dims, preferred_element_type=jnp.float32)


def forward_kernel(
    seq_ref,
    w_ref,
    cos_ref,
    sin_ref,
    bias_ref,
    keep_ref,
    out_ref,
    a_ref,
    qkv_ref,
    lse_ref,
    o_ref,
    mean_ref,
    inverse_ref,
):
    full_len, width = seq_ref.shape
    span = o_ref.shape[0]
    group = span // HD
    half = HD // 2
    blk = out_ref.shape[2]
    gain = w_ref[:, 512:640].astype(jnp.float32).T[3 * span - 512 : 3 * span - 511]
    w_turned = w_ref[:, : 3 * span].astype(jnp.float32).T.astype(jnp.bfloat16)
    for start in range(0, full_len, ROWS):
        rows = slice(start, start + ROWS)
        x = seq_ref[rows].astype(jnp.float32)
        mean = jnp.mean(x, -1, keepdims=True)
        centre = x - mean
        inverse = lax.rsqrt(jnp.mean(centre * centre, -1, keepdims=True) + EPS)
        mean_ref[rows] = mean
        inverse_ref[rows] = inverse
        a_low = (centre * inverse * gain).astype(jnp.bfloat16)
        a_ref[rows] = a_low
        joined = product(w_turned, a_low, NT)
        cosine = cos_ref[:, rows]
        sine = sin_ref[:, rows]
        for part in range(2 * group):
            one = joined[part * HD : part * HD + half]
            two = joined[part * HD + half : (part + 1) * HD]
            scale = HD ** (-0.5) if part < group else 1.0
            for at, value in (
                (0, one * cosine - two * sine),
                (half, two * cosine + one * sine),
            ):
                qkv_ref[part * HD + at : part * HD + at + half, rows] = (
                    value.astype(jnp.bfloat16) * scale
                ).astype(jnp.bfloat16)
        qkv_ref[2 * span :, rows] = joined[2 * span :].astype(jnp.bfloat16)
    for head in range(group):
        here = slice(head * HD, (head + 1) * HD)
        keys = qkv_ref[span + head * HD : span + (head + 1) * HD].T
        values = qkv_ref[2 * span + head * HD : 2 * span + (head + 1) * HD]
        for start in range(0, full_len, COLS):
            cols = slice(start, start + COLS)
            scores = product(keys, qkv_ref[here, cols]) + bias_ref[...]
            maximum = jnp.max(scores, 0, keepdims=True)
            exponent = jnp.exp(scores - maximum)
            total = jnp.sum(exponent, 0, keepdims=True)
            attended = product(values, exponent.astype(jnp.bfloat16))
            attended = attended * (keep_ref[:, cols] / total)
            o_ref[here, cols] = attended
            lse_ref[head : head + 1, cols] = maximum + jnp.log(total)
            for first in range(0, COLS, blk):
                out_ref[(start + first) // blk, here, :] = attended[
                    :, first : first + blk
                ].astype(jnp.bfloat16)


def backward_kernel(
    do_ref,
    qkv_ref,
    lse_ref,
    o_ref,
    cos_ref,
    sin_ref,
    bias_ref,
    keep_ref,
    seq_ref,
    mean_ref,
    inverse_ref,
    w_ref,
    g_ref,
    ga_ref,
    gain_ref,
    dk_ref,
    dv_ref,
):
    span, full_len = o_ref.shape
    group = span // HD
    half = HD // 2
    blk = do_ref.shape[2]
    for head in range(group):
        here = slice(head * HD, (head + 1) * HD)
        keys_turned = qkv_ref[span + head * HD : span + (head + 1) * HD]
        keys = keys_turned.T
        values = qkv_ref[2 * span + head * HD : 2 * span + (head + 1) * HD].T
        for start in range(0, full_len, COLS):
            cols = slice(start, start + COLS)
            query = qkv_ref[here, cols]
            grad_out = jnp.concatenate(
                [do_ref[(start + first) // blk, here, :] for first in range(0, COLS, blk)], 1
            )
            grad_out = grad_out.astype(jnp.float32) * keep_ref[:, cols]
            delta = jnp.sum(grad_out * o_ref[here, cols], 0, keepdims=True)
            grad_out = grad_out.astype(jnp.bfloat16)
            scores = product(keys, query) + bias_ref[...]
            probs = jnp.exp(scores - lse_ref[head : head + 1, cols])
            grad_scores = (probs * (product(values, grad_out) - delta)).astype(jnp.bfloat16)
            grad_value = product(grad_out, probs.astype(jnp.bfloat16), NT)
            grad_key = product(query, grad_scores, NT)
            if start == 0:
                dv_ref[...] = grad_value
                dk_ref[...] = grad_key
            else:
                dv_ref[...] += grad_value
                dk_ref[...] += grad_key
            grad_query = product(keys_turned, grad_scores) * HD ** (-0.5)
            cosine = cos_ref[:, cols]
            sine = sin_ref[:, cols]
            one, two = grad_query[:half], grad_query[half:]
            g_ref[head * HD : head * HD + half, cols] = (one * cosine + two * sine).astype(
                jnp.bfloat16
            )
            g_ref[head * HD + half : (head + 1) * HD, cols] = (
                two * cosine - one * sine
            ).astype(jnp.bfloat16)
        one, two = dk_ref[:half], dk_ref[half:]
        cosine = cos_ref[...]
        sine = sin_ref[...]
        low_at = span + head * HD
        g_ref[low_at : low_at + half] = (one * cosine + two * sine).astype(jnp.bfloat16)
        g_ref[low_at + half : low_at + HD] = (two * cosine - one * sine).astype(jnp.bfloat16)
        g_ref[2 * span + head * HD : 2 * span + (head + 1) * HD] = dv_ref[...].astype(
            jnp.bfloat16
        )
    for start in range(0, full_len, ROWS):
        rows = slice(start, start + ROWS)
        grad_a = product(g_ref[:, rows].T, w_ref[:, : 3 * span], NT)
        normed = (seq_ref[rows].astype(jnp.float32) - mean_ref[rows]) * inverse_ref[rows]
        summed = jnp.sum(grad_a * normed, 0, keepdims=True)
        gain_ref[...] = summed if start == 0 else gain_ref[...] + summed
        for first in range(0, ROWS, blk):
            ga_ref[(start + first) // blk] = grad_a[first : first + blk].astype(jnp.bfloat16)


def mlp_kernel(
    tok_ref,
    att_ref,
    cot_ref,
    gain_ref,
    wout_ref,
    win_ref,
    wdown_ref,
    do_ref,
    gm_ref,
    mixed_ref,
    b_ref,
    hid_ref,
    gg_ref,
    grad_gain_ref,
):
    seqs, local_len, width = tok_ref.shape
    spread = do_ref.shape[0] // seqs
    span = do_ref.shape[1]
    hidden = hid_ref.shape[1]
    resid = jnp.concatenate([tok_ref[k] for k in range(seqs)], 0).astype(jnp.float32)
    att = jnp.concatenate([att_ref[k].T for k in range(seqs)], 0)
    cot = jnp.concatenate([cot_ref[k] for k in range(seqs)], 0)
    mixed = resid + product(att, wout_ref[...])
    mixed_ref[...] = mixed
    centre = mixed - jnp.mean(mixed, -1, keepdims=True)
    inverse = lax.rsqrt(jnp.mean(centre * centre, -1, keepdims=True) + EPS)
    normed = centre * inverse
    b_low = (normed * gain_ref[...]).astype(jnp.bfloat16)
    b_ref[...] = b_low
    for first in range(0, hidden, hidden // 3):
        here = slice(first, first + hidden // 3)
        there = slice(hidden + first, hidden + first + hidden // 3)
        gate_in = product(b_low, win_ref[:, here])
        up_half = product(b_low, win_ref[:, there])
        grad_hid = product(cot, wdown_ref[here], NT)
        normal_cdf = 0.5 * (1.0 + lax.erf(gate_in * INV_ROOT_TWO))
        gelu_out = gate_in * normal_cdf
        hid_ref[:, here] = (gelu_out * up_half).astype(jnp.bfloat16)
        normal_pdf = jnp.exp(-0.5 * gate_in * gate_in) * INV_ROOT_TWO_PI
        gg_ref[:, here] = (grad_hid * up_half * (normal_cdf + gate_in * normal_pdf)).astype(
            jnp.bfloat16
        )
        gg_ref[:, there] = (grad_hid * gelu_out).astype(jnp.bfloat16)
    grad_b = product(gg_ref[...], win_ref[...], NT)
    grad_gain_ref[...] = jnp.sum(grad_b * normed, 0, keepdims=True)
    scaled = grad_b * gain_ref[...]
    grad_mixed = cot.astype(jnp.float32) + inverse * (
        scaled
        - jnp.mean(scaled, -1, keepdims=True)
        - normed * jnp.mean(scaled * normed, -1, keepdims=True)
    )
    gm_ref[...] = grad_mixed
    grad_heads = product(wout_ref[...], grad_mixed.astype(jnp.bfloat16), NT).astype(jnp.bfloat16)
    for seq in range(seqs):
        for part in range(spread):
            do_ref[seq * spread + part] = grad_heads[
                part * span : (part + 1) * span, seq * local_len : (seq + 1) * local_len
            ]


def half_weights(
    which,
    att_ref,
    cot_ref,
    gm_ref,
    b_ref,
    hid_ref,
    gg_ref,
    part_ref,
    tail_ref,
    extra_ref,
    turned,
    tall,
):
    seqs, width, local_len = att_ref.shape
    ctx, pairs, chunk, _ = part_ref.shape
    count = gg_ref.shape[1] // width
    depth = width // (2 * pairs)
    down_rows = hid_ref.shape[1] // (2 * pairs)
    front = ctx * chunk
    split = front + tail_ref.shape[1] - (count + 1) * depth
    cot = jnp.concatenate([cot_ref[k] for k in range(seqs)], 0)
    turned[:width] = b_ref[...].astype(jnp.float32).T
    turned[width : 2 * width] = jnp.concatenate(
        [att_ref[k] for k in range(seqs)], 1
    ).astype(jnp.float32)
    turned[2 * width :] = hid_ref[...].astype(jnp.float32).T

    def chosen(first, height):
        return jnp.concatenate(
            [
                turned[pl.ds(pl.multiple_of(first + (2 * k + which) * height, 8), height)]
                for k in range(pairs)
            ],
            0,
        ).astype(jnp.bfloat16)

    grad_up = product(chosen(width, depth), gm_ref[...].astype(jnp.bfloat16))
    tall[...] = product(chosen(2 * width, down_rows), cot)
    grad_in = product(chosen(0, depth), gg_ref[...])
    for pair in range(pairs):
        wide = slice(pair * depth, (pair + 1) * depth)
        rows = jnp.concatenate(
            [grad_in[wide, k * width : (k + 1) * width] for k in range(count)]
            + [grad_up[wide], tall[pair * down_rows : pair * down_rows + split]],
            0,
        ).astype(jnp.bfloat16)
        for part in range(ctx):
            part_ref[part, pair] = rows[part * chunk : (part + 1) * chunk]
        tail_ref[pair] = rows[front:]
        extra_ref[pair] = tall[pair * down_rows + split : (pair + 1) * down_rows]


def sent_weights_kernel(core_ref, *refs):
    half_weights(1 - core_ref[0], *refs)


def kept_weights_kernel(
    core_ref,
    att_ref,
    cot_ref,
    gm_ref,
    b_ref,
    hid_ref,
    gg_ref,
    wdown_ref,
    mixed_ref,
    part_ref,
    tail_ref,
    extra_ref,
    out_ref,
    turned,
    tall,
):
    half_weights(
        core_ref[0],
        att_ref,
        cot_ref,
        gm_ref,
        b_ref,
        hid_ref,
        gg_ref,
        part_ref,
        tail_ref,
        extra_ref,
        turned,
        tall,
    )
    local_len = out_ref.shape[1]
    result = mixed_ref[...] + product(hid_ref[...], wdown_ref[...])
    for seq in range(out_ref.shape[0]):
        out_ref[seq] = result[seq * local_len : (seq + 1) * local_len].astype(jnp.bfloat16)


def qkv_weights_kernel(
    core_ref,
    a_ref,
    g_ref,
    gain_one_ref,
    gain_two_ref,
    kept_extra_ref,
    away_extra_ref,
    kept_ref,
    away_ref,
    w_ref,
):
    pairs, depth, width = kept_ref.shape
    span3 = g_ref.shape[0]
    used = width - 128
    w_ref[:, :span3] = product(a_ref[...].T, g_ref[...], NT)
    lane = used - 128
    gains = jnp.concatenate(
        [
            jnp.zeros((span3 - lane, width), jnp.float32),
            gain_one_ref[...],
            gain_two_ref[...],
            jnp.zeros((used - span3 - 2, width), jnp.float32),
        ],
        0,
    ).T
    w_ref[:, span3:] = gains[:, span3 - lane :]
    core = core_ref[0]
    for pair in range(pairs):
        for ref, extra_ref, which in (
            (kept_ref, kept_extra_ref, core),
            (away_ref, away_extra_ref, 1 - core),
        ):
            rows = pl.ds(pl.multiple_of((2 * pair + which) * depth, 8), depth)
            extra = extra_ref[pair]
            ref[pair] = jnp.concatenate(
                [
                    w_ref[rows],
                    jnp.concatenate(
                        [extra[:, k * 128 : (k + 1) * 128] for k in range(width // 128)], 0
                    ),
                ],
                1,
            ).astype(jnp.bfloat16)


def first_kernel(group_ref, w_ref, gains_ref, out_ref):
    depth, used = out_ref.shape
    spread = 4
    span = w_ref.shape[1] // (3 * spread)
    own_group = group_ref[0]
    gains = gains_ref[...]

    for which in range(spread):

        @pl.when(own_group == which)
        def _():
            picked = [
                w_ref[
                    :, (k * spread + which) * span : (k * spread + which + 1) * span
                ].astype(jnp.float32)
                for k in range(3)
            ]
            out_ref[...] = jnp.concatenate([*picked, gains], 1).astype(jnp.bfloat16)


def finish_kernel(
    ends_ref, gain_one_ref, qkv_ref, wout_ref, gain_two_ref, win_ref, wdown_ref
):
    ctx, _, width = ends_ref.shape
    depth = qkv_ref.shape[0]
    down_rows = wdown_ref.shape[0]
    count = win_ref.shape[1] // width
    spread = ctx // 2
    span = width // spread
    f32 = jnp.float32
    last = [ends_ref[k, :depth].astype(f32) for k in range(ctx)]
    for group in range(spread):
        both = last[group] + last[group + spread]
        for part in range(3):
            qkv_ref[:, part * width + group * span : part * width + (group + 1) * span] = both[
                :, part * span : (part + 1) * span
            ]
    total = last[0]
    for k in range(1, ctx):
        total = total + last[k]
    lane = 3 * span // 128 * 128
    gains = total[:, lane : lane + 128].T
    gain_one_ref[...] = gains[3 * span - lane : 3 * span - lane + 1]
    gain_two_ref[...] = gains[3 * span - lane + 1 : 3 * span - lane + 2]
    chunk = (ends_ref.shape[1] - depth) // 2
    main = jnp.concatenate(
        [
            ends_ref[k, depth + part * chunk : depth + (part + 1) * chunk].astype(f32)
            for part in range(2)
            for k in range(ctx)
        ],
        0,
    )
    for k in range(count):
        win_ref[:, k * width : (k + 1) * width] = main[k * depth : (k + 1) * depth]
    wout_ref[...] = main[count * depth : (count + 1) * depth]
    split = main.shape[0] - (count + 1) * depth
    extra = down_rows - split
    wdown_ref[:split] = main[(count + 1) * depth :]
    wdown_ref[split:] = jnp.concatenate(
        [total[k * extra : (k + 1) * extra, width - 128 :] for k in range(width // 128)], 1
    )


def on_device(kernel, outs, args, micros, scratch=(), scalars=0, after=(), name=None):
    space = pl.BlockSpec(memory_space=pltpu.VMEM)
    scalar = pl.BlockSpec(memory_space=pltpu.SMEM)
    given = len(args)

    def ordered(*refs):
        kernel(*refs[:given], *refs[given + len(after) :])

    return pl.pallas_call(
        ordered,
        out_shape=[jax.ShapeDtypeStruct(shape, dtype) for shape, dtype in outs],
        in_specs=[scalar] * scalars
        + [space] * (given - scalars)
        + [pl.BlockSpec(memory_space=pl.ANY)] * len(after),
        out_specs=[space] * len(outs),
        scratch_shapes=list(scratch),
        compiler_params=pltpu.CompilerParams(vmem_limit_bytes=56 * 1024 * 1024),
        cost_estimate=pl.CostEstimate(
            flops=int(micros * 2e10), bytes_accessed=int(micros * 4e7), transcendentals=0
        ),
        name=name,
    )(*args, *after)


def sum_kernel(left_ref, right_ref, out_ref):
    for k in range(out_ref.shape[0]):
        out_ref[k] = (left_ref[k].astype(jnp.float32) + right_ref[k].astype(jnp.float32)).astype(
            jnp.bfloat16
        )


def interleave_kernel(late_ref, held_ref, came_ref, out_ref):
    late = late_ref[0]
    for k in range(held_ref.shape[0]):
        out_ref[k, late] = held_ref[k]
        out_ref[k, 1 - late] = came_ref[k]


def stack_kernel(upper_ref, lower_ref, out_ref):
    rows = upper_ref.shape[0]
    out_ref[:rows] = upper_ref[...]
    out_ref[rows:] = lower_ref[...]


def body(tokens, lengths, deal, gain_attn, w_qkv, w_out, gain_mlp, w_in, w_down, cotangent):
    seqs, local_len, width = tokens.shape
    ctx = lax.axis_size("ctx")
    fsdp = lax.axis_size("fsdp")
    spread = ctx // seqs
    group = HEADS // spread
    span = group * HD
    full_len = local_len * ctx
    rows = seqs * local_len
    context = lax.axis_index("ctx")
    own_seq = context // spread
    own_group = context % spread
    depth = w_qkv.shape[0]
    hidden = w_in.shape[1] // 2
    down_rows = w_down.shape[0]
    f32 = jnp.float32

    offsets = jnp.arange(BLK, dtype=jnp.int32)
    all_pos = (deal[:, None] * BLK + offsets[None, :]).reshape(full_len)
    length = lax.dynamic_slice_in_dim(lengths, own_seq, 1)[0]
    all_keep = all_pos < length

    used = 3 * span + 64
    gains_wide = jnp.pad(
        jnp.stack([gain_attn, gain_mlp], 1).astype(f32), ((0, 0), (0, used - 3 * span - 2))
    )
    first = on_device(
        first_kernel,
        [((depth, used), jnp.bfloat16)],
        (own_group.astype(jnp.int32)[None], w_qkv, gains_wide),
        0.05,
        scalars=1,
        name="first_pack",
    )[0]
    steps = [fsdp >> (k + 1) for k in range(fsdp.bit_length() - 1)]
    held = first[None]
    for bit in steps[:-1]:
        held = doubled(held, "fsdp", bit)
    first_all = doubled(held, "fsdp", steps[-1]).reshape(fsdp * depth, used)
    win_all = lax.all_gather(w_in, "fsdp", axis=0, tiled=True)
    sequence = lax.all_to_all(jnp.repeat(tokens, spread, axis=0), "ctx", 0, 0, tiled=True)
    stacked = on_device(
        stack_kernel,
        [((depth + down_rows, width), jnp.bfloat16)],
        (w_out, w_down),
        0.02,
        after=(held,),
        name="stack_rest",
    )[0]
    rest = doubled(stacked[None], "fsdp", steps[0])
    gain_one = first_all[:, 3 * span]
    gain_two = first_all[:, 3 * span + 1]

    cosine, sine = tables(all_pos)
    bias = jnp.where(all_keep, 0.0, NEGATIVE).astype(f32)[:, None]
    keep_row = all_keep.astype(f32)[None, :]
    sequence = sequence.reshape(full_len, width)
    attended, a_low, qkv, log_total, unrounded, mean, inverse = on_device(
        forward_kernel,
        [
            ((ctx, span, local_len), jnp.bfloat16),
            ((full_len, width), jnp.bfloat16),
            ((3 * span, full_len), jnp.bfloat16),
            ((8, full_len), f32),
            ((span, full_len), f32),
            ((full_len, 1), f32),
            ((full_len, 1), f32),
        ],
        (sequence, first_all, cosine, sine, bias, keep_row),
        0.6,
        name="attention_forward",
    )
    rest = doubled(rest, "fsdp", steps[1], after=(attended,))
    for bit in steps[2:]:
        rest = doubled(rest, "fsdp", bit)
    stacked_all = rest
    att_back = lax.all_to_all(attended, "ctx", 0, 0, tiled=True)
    att_turned = att_back.reshape(seqs, width, local_len)

    def whole(start, height):
        return stacked_all[:, start : start + height].reshape(fsdp * height, width)

    wout_all = whole(0, depth)
    wdown_all = whole(depth, down_rows)

    resid = tokens.astype(f32).reshape(rows, width)
    count = w_in.shape[1] // width
    main_rows = ((count + 1) * depth + down_rows) // (8 * ctx) * 8 * ctx
    chunk = main_rows // (2 * ctx)
    front = ctx * chunk
    split = main_rows - (count + 1) * depth
    extra = down_rows - split
    pairs = fsdp // 2
    core = (lax.axis_index("fsdp") % 2).astype(jnp.int32)[None]
    grad_heads, grad_mixed, mixed, b_low, hid_low, grad_gate_up, grad_gain_two = on_device(
        mlp_kernel,
        [
            ((ctx, span, local_len), jnp.bfloat16),
            ((rows, width), f32),
            ((rows, width), f32),
            ((rows, width), jnp.bfloat16),
            ((rows, hidden), jnp.bfloat16),
            ((rows, 2 * hidden), jnp.bfloat16),
            ((1, width), f32),
        ],
        (
            tokens,
            att_turned,
            cotangent,
            gain_two.astype(f32)[None, :],
            wout_all,
            win_all,
            wdown_all,
        ),
        0.5,
        name="mlp",
    )
    weights_in = (core, att_turned, cotangent, grad_mixed, b_low, hid_low, grad_gate_up)
    half_outs = [
        ((ctx, pairs, chunk, width), jnp.bfloat16),
        ((pairs, front, width), jnp.bfloat16),
        ((pairs, extra, width), f32),
    ]
    half_scratch = [
        pltpu.VMEM((2 * width + hidden, rows), f32),
        pltpu.VMEM((hidden // 2, width), f32),
    ]
    front_away, tail_away, away_extra = on_device(
        sent_weights_kernel,
        half_outs,
        weights_in,
        5,
        half_scratch,
        scalars=1,
        name="sent_weights",
    )
    front_kept, tail_kept, kept_extra, output = on_device(
        kept_weights_kernel,
        [*half_outs, (tokens.shape, jnp.bfloat16)],
        (*weights_in, wdown_all, mixed),
        0.05,
        half_scratch,
        scalars=1,
        after=(front_away,),
        name="kept_weights",
    )
    tail_pair = core_sum(tail_kept, tail_away, "fsdp", 0.02, name="sum_cores_tail")
    front_pair = core_sum(
        front_kept, front_away, "fsdp", 0.02, after=(tail_pair,), name="sum_cores_front"
    )
    front_part = lax.psum_scatter(
        front_pair.reshape(-1, chunk, width), "ctx", scatter_dimension=0, tiled=True
    )

    all_grad = lax.all_to_all(grad_heads, "ctx", 0, 0, tiled=True)
    grad_qkv, grad_a_part, grad_gain_one = on_device(
        backward_kernel,
        [
            ((3 * span, full_len), jnp.bfloat16),
            ((ctx, local_len, width), jnp.bfloat16),
            ((1, width), f32),
        ],
        (
            all_grad,
            qkv,
            log_total,
            unrounded,
            cosine,
            sine,
            bias,
            keep_row,
            sequence,
            mean,
            inverse,
            first_all,
        ),
        12,
        [pltpu.VMEM((HD, full_len), f32)] * 2,
        after=(front_pair,),
        name="attention_backward",
    )
    tail_part = spread_sum(tail_pair, "fsdp").reshape(ctx, chunk, width)
    both_parts = lax.all_to_all(
        jnp.concatenate([grad_a_part, tail_part], 1), "ctx", 0, 0, tiled=True
    )
    grad_a_parts = both_parts[:, :local_len]
    tail_share = low(jnp.sum(both_parts[:, local_len:].astype(f32), 0))
    last_kept, last_away = on_device(
        qkv_weights_kernel,
        [((pairs, depth, width), jnp.bfloat16)] * 2,
        (core, a_low, grad_qkv, grad_gain_one, grad_gain_two, kept_extra, away_extra),
        0.1,
        [pltpu.VMEM((width, used), f32)],
        scalars=1,
        name="qkv_weights",
    )
    last = core_sum(
        last_kept, last_away, "fsdp", 0.05, after=(both_parts,), name="sum_cores_last"
    )
    grad_a = jnp.sum(
        grad_a_parts.reshape(seqs, spread, local_len, width).astype(f32), 1
    ).reshape(rows, width)
    _, normed_one, inverse_one = norm_forward(resid, gain_one)
    grad_norm_one, _ = norm_backward(grad_a, gain_one, normed_one, inverse_one)
    grad_input = grad_mixed + grad_norm_one

    share = spread_sum(jnp.concatenate([last, front_part], 1), "fsdp")
    share = jnp.concatenate([share, tail_share], 0)
    ends = gather_by_exchange(share, "ctx", ctx)
    finished = on_device(
        finish_kernel,
        [
            ((1, depth), f32),
            (w_qkv.shape, f32),
            (w_out.shape, f32),
            ((1, depth), f32),
            (w_in.shape, f32),
            (w_down.shape, f32),
        ],
        (ends,),
        3,
        name="finish",
    )
    return (
        output,
        grad_input.reshape(tokens.shape),
        finished[0].reshape(depth),
        finished[1],
        finished[2],
        finished[3].reshape(depth),
        finished[4],
        finished[5],
    )


def solution(mesh):
    placed = (
        P("fsdp", "ctx", None),
        P("fsdp"),
        P(),
        P("fsdp"),
        P("fsdp", None),
        P("fsdp", None),
        P("fsdp"),
        P("fsdp", None),
        P("fsdp", None),
        P("fsdp", "ctx", None),
    )
    return jax.shard_map(
        body,
        mesh=mesh,
        in_specs=placed,
        out_specs=(
            P("fsdp", "ctx", None),
            P("fsdp", "ctx", None),
            P("fsdp"),
            P("fsdp", None),
            P("fsdp", None),
            P("fsdp"),
            P("fsdp", None),
            P("fsdp", None),
        ),
        check_vma=False,
    )
```

```python
import math

import jax
import jax.numpy as jnp
from jax import lax
from jax.experimental import pallas as pl
from jax.experimental.pallas import tpu as pltpu
from jax.sharding import PartitionSpec as P

HEADS = 12
HD = 64
BLK = 128


EPS = 1e-05
THETA = 160000.0
NEGATIVE = -1e30
INV_ROOT_TWO = 0.7071067811865476
INV_ROOT_TWO_PI = 0.3989422804014327


def gather_by_exchange(part, axis, n):
    return lax.all_to_all(jnp.broadcast_to(part[None], (n, *part.shape)), axis, 0, 0)


def core_pairs(n):
    return [(k, k ^ 1) for k in range(n)]


def core_groups(n):
    return [list(range(first, n, 2)) for first in range(2)]


def doubled(held, axis, bit, after=()):
    n = lax.axis_size(axis)
    index = lax.axis_index(axis)
    came = lax.ppermute(held, axis, [(k, k ^ bit) for k in range(n)])
    if after:
        held = on_device(
            interleave_kernel,
            [((held.shape[0], 2, *held.shape[1:]), held.dtype)],
            ((index // bit % 2).astype(jnp.int32)[None], held, came),
            0.02,
            scalars=1,
            after=after,
            name="interleave",
        )[0]
    else:
        first = (index & bit) == 0
        held = jnp.where(first, jnp.stack([held, came], 1), jnp.stack([came, held], 1))
    return held.reshape(-1, *held.shape[2:])


def core_sum(kept, away, axis, micros, after=(), name=None):
    came = lax.ppermute(away, axis, core_pairs(lax.axis_size(axis)))
    return on_device(
        sum_kernel, [(kept.shape, jnp.bfloat16)], (kept, came), micros, after=after, name=name
    )[0]


def spread_sum(parts, axis):
    groups = core_groups(lax.axis_size(axis))
    shares = lax.all_to_all(parts, axis, 0, 0, tiled=True, axis_index_groups=groups)
    return low(jnp.sum(shares.astype(jnp.float32), 0))


def spread_sum_permuted(parts, axis, after=()):
    n = lax.axis_size(axis)
    half = n // 2
    chip = lax.axis_index(axis) // 2
    total = lax.dynamic_index_in_dim(parts, chip, 0, keepdims=False).astype(jnp.float32)
    for away in range(1, half):
        piece = lax.dynamic_index_in_dim(parts, (chip + away) % half, 0, keepdims=False)
        moves = [(k, (k + 2 * away) % n) for k in range(n)]
        total = total + lax.ppermute(piece, axis, moves).astype(jnp.float32)
    return low(total)


def low(values):
    return values.astype(jnp.bfloat16)


def tables(positions):
    halves = jnp.arange(HD // 2, dtype=jnp.float32)
    frequency = THETA ** (-2.0 * halves / HD)
    angles = frequency[:, None] * positions.astype(jnp.float32)[None, :]
    return jnp.cos(angles), jnp.sin(angles)


def norm_forward(rows_in, gain):
    centre = rows_in - jnp.mean(rows_in, -1, keepdims=True)
    variance = jnp.mean(centre * centre, -1, keepdims=True)
    inverse = lax.rsqrt(variance + EPS)
    normed = centre * inverse
    return (normed * gain.astype(jnp.float32), normed, inverse)


def norm_backward(grad_rows, gain, normed, inverse):
    scaled = grad_rows * gain.astype(jnp.float32)
    grad_gain = jnp.sum(grad_rows * normed, 0)
    grad_rows_in = inverse * (
        scaled
        - jnp.mean(scaled, -1, keepdims=True)
        - normed * jnp.mean(scaled * normed, -1, keepdims=True)
    )
    return (grad_rows_in, grad_gain)


NN = (((1,), (0,)), ((), ()))
NT = (((1,), (1,)), ((), ()))
ROWS = 256
COLS = 256


def product(left, right, dims=NN):
    return lax.dot_general(left, right, dims, preferred_element_type=jnp.float32)


def project_kernel(
    seq_ref, w_ref, cos_ref, sin_ref, a_ref, qkv_ref, mean_ref, inverse_ref
):
    full_len, width = seq_ref.shape
    span = qkv_ref.shape[0] // 3
    group = span // HD
    half = HD // 2
    gain = w_ref[:, 512:640].astype(jnp.float32).T[3 * span - 512 : 3 * span - 511]
    w_turned = w_ref[:, : 3 * span].astype(jnp.float32).T.astype(jnp.bfloat16)
    for start in range(0, full_len, ROWS):
        rows = slice(start, start + ROWS)
        x = seq_ref[rows].astype(jnp.float32)
        mean = jnp.mean(x, -1, keepdims=True)
        centre = x - mean
        inverse = lax.rsqrt(jnp.mean(centre * centre, -1, keepdims=True) + EPS)
        mean_ref[rows] = mean
        inverse_ref[rows] = inverse
        a_low = (centre * inverse * gain).astype(jnp.bfloat16)
        a_ref[rows] = a_low
        joined = product(w_turned, a_low, NT)
        cosine = cos_ref[:, rows]
        sine = sin_ref[:, rows]
        for part in range(2 * group):
            one = joined[part * HD : part * HD + half]
            two = joined[part * HD + half : (part + 1) * HD]
            scale = HD ** (-0.5) if part < group else 1.0
            for at, value in (
                (0, one * cosine - two * sine),
                (half, two * cosine + one * sine),
            ):
                qkv_ref[part * HD + at : part * HD + at + half, rows] = (
                    value.astype(jnp.bfloat16) * scale
                ).astype(jnp.bfloat16)
        qkv_ref[2 * span :, rows] = joined[2 * span :].astype(jnp.bfloat16)


def forward_kernel(qkv_ref, bias_ref, keep_ref, out_ref, lse_ref, o_ref):
    span, full_len = o_ref.shape
    group = span // HD
    blk = out_ref.shape[2]
    for head in range(group):
        here = slice(head * HD, (head + 1) * HD)
        keys = qkv_ref[span + head * HD : span + (head + 1) * HD].T
        values = qkv_ref[2 * span + head * HD : 2 * span + (head + 1) * HD]
        for start in range(0, full_len, COLS):
            cols = slice(start, start + COLS)
            scores = product(keys, qkv_ref[here, cols]) + bias_ref[...]
            maximum = jnp.max(scores, 0, keepdims=True)
            exponent = jnp.exp(scores - maximum)
            total = jnp.sum(exponent, 0, keepdims=True)
            attended = product(values, exponent.astype(jnp.bfloat16))
            attended = attended * (keep_ref[:, cols] / total)
            o_ref[here, cols] = attended
            lse_ref[head : head + 1, cols] = maximum + jnp.log(total)
            for first in range(0, COLS, blk):
                out_ref[(start + first) // blk, here, :] = attended[
                    :, first : first + blk
                ].astype(jnp.bfloat16)


def backward_kernel(
    do_ref,
    qkv_ref,
    lse_ref,
    o_ref,
    cos_ref,
    sin_ref,
    bias_ref,
    keep_ref,
    seq_ref,
    mean_ref,
    inverse_ref,
    w_ref,
    g_ref,
    ga_ref,
    gain_ref,
    dk_ref,
    dv_ref,
):
    span, full_len = o_ref.shape
    group = span // HD
    half = HD // 2
    blk = do_ref.shape[2]
    for head in range(group):
        here = slice(head * HD, (head + 1) * HD)
        keys_turned = qkv_ref[span + head * HD : span + (head + 1) * HD]
        keys = keys_turned.T
        values = qkv_ref[2 * span + head * HD : 2 * span + (head + 1) * HD].T
        for start in range(0, full_len, COLS):
            cols = slice(start, start + COLS)
            query = qkv_ref[here, cols]
            grad_out = jnp.concatenate(
                [do_ref[(start + first) // blk, here, :] for first in range(0, COLS, blk)], 1
            )
            grad_out = grad_out.astype(jnp.float32) * keep_ref[:, cols]
            delta = jnp.sum(grad_out * o_ref[here, cols], 0, keepdims=True)
            grad_out = grad_out.astype(jnp.bfloat16)
            scores = product(keys, query) + bias_ref[...]
            probs = jnp.exp(scores - lse_ref[head : head + 1, cols])
            grad_scores = (probs * (product(values, grad_out) - delta)).astype(jnp.bfloat16)
            grad_value = product(grad_out, probs.astype(jnp.bfloat16), NT)
            grad_key = product(query, grad_scores, NT)
            if start == 0:
                dv_ref[...] = grad_value
                dk_ref[...] = grad_key
            else:
                dv_ref[...] += grad_value
                dk_ref[...] += grad_key
            grad_query = product(keys_turned, grad_scores) * HD ** (-0.5)
            cosine = cos_ref[:, cols]
            sine = sin_ref[:, cols]
            one, two = grad_query[:half], grad_query[half:]
            g_ref[head * HD : head * HD + half, cols] = (one * cosine + two * sine).astype(
                jnp.bfloat16
            )
            g_ref[head * HD + half : (head + 1) * HD, cols] = (
                two * cosine - one * sine
            ).astype(jnp.bfloat16)
        one, two = dk_ref[:half], dk_ref[half:]
        cosine = cos_ref[...]
        sine = sin_ref[...]
        low_at = span + head * HD
        g_ref[low_at : low_at + half] = (one * cosine + two * sine).astype(jnp.bfloat16)
        g_ref[low_at + half : low_at + HD] = (two * cosine - one * sine).astype(jnp.bfloat16)
        g_ref[2 * span + head * HD : 2 * span + (head + 1) * HD] = dv_ref[...].astype(
            jnp.bfloat16
        )
    for start in range(0, full_len, ROWS):
        rows = slice(start, start + ROWS)
        grad_a = product(g_ref[:, rows].T, w_ref[:, : 3 * span], NT)
        normed = (seq_ref[rows].astype(jnp.float32) - mean_ref[rows]) * inverse_ref[rows]
        summed = jnp.sum(grad_a * normed, 0, keepdims=True)
        gain_ref[...] = summed if start == 0 else gain_ref[...] + summed
        for first in range(0, ROWS, blk):
            ga_ref[(start + first) // blk] = grad_a[first : first + blk].astype(jnp.bfloat16)


def mlp_kernel(
    core_ref,
    tok_ref,
    att_ref,
    cot_ref,
    gain_ref,
    mine_ref,
    other_ref,
    win_ref,
    do_ref,
    gm_ref,
    mixed_ref,
    b_ref,
    hid_ref,
    gg_ref,
    grad_gain_ref,
    wdown_ref,
    wout_ref,
):
    pairs, height, _ = mine_ref.shape
    depth = wout_ref.shape[0] // (2 * pairs)
    down_rows = height - depth
    even = core_ref[0] == 0
    for pair in range(pairs):
        mine = mine_ref[pair].astype(jnp.float32)
        other = other_ref[pair].astype(jnp.float32)
        first = jnp.where(even, mine, other)
        second = jnp.where(even, other, mine)
        wout_ref[2 * pair * depth : 2 * (pair + 1) * depth] = jnp.concatenate(
            [first[:depth], second[:depth]], 0
        ).astype(jnp.bfloat16)
        wdown_ref[2 * pair * down_rows : 2 * (pair + 1) * down_rows] = jnp.concatenate(
            [first[depth:], second[depth:]], 0
        ).astype(jnp.bfloat16)
    seqs, local_len, width = tok_ref.shape
    spread = do_ref.shape[0] // seqs
    span = do_ref.shape[1]
    hidden = hid_ref.shape[1]
    resid = jnp.concatenate([tok_ref[k] for k in range(seqs)], 0).astype(jnp.float32)
    att = jnp.concatenate([att_ref[k].T for k in range(seqs)], 0)
    cot = jnp.concatenate([cot_ref[k] for k in range(seqs)], 0)
    mixed = resid + product(att, wout_ref[...])
    mixed_ref[...] = mixed
    centre = mixed - jnp.mean(mixed, -1, keepdims=True)
    inverse = lax.rsqrt(jnp.mean(centre * centre, -1, keepdims=True) + EPS)
    normed = centre * inverse
    b_low = (normed * gain_ref[...]).astype(jnp.bfloat16)
    b_ref[...] = b_low
    for first in range(0, hidden, hidden // 3):
        here = slice(first, first + hidden // 3)
        there = slice(hidden + first, hidden + first + hidden // 3)
        gate_in = product(b_low, win_ref[:, here])
        up_half = product(b_low, win_ref[:, there])
        grad_hid = product(cot, wdown_ref[here], NT)
        normal_cdf = 0.5 * (1.0 + lax.erf(gate_in * INV_ROOT_TWO))
        gelu_out = gate_in * normal_cdf
        hid_ref[:, here] = (gelu_out * up_half).astype(jnp.bfloat16)
        normal_pdf = jnp.exp(-0.5 * gate_in * gate_in) * INV_ROOT_TWO_PI
        gg_ref[:, here] = (grad_hid * up_half * (normal_cdf + gate_in * normal_pdf)).astype(
            jnp.bfloat16
        )
        gg_ref[:, there] = (grad_hid * gelu_out).astype(jnp.bfloat16)
    grad_b = product(gg_ref[...], win_ref[...], NT)
    grad_gain_ref[...] = jnp.sum(grad_b * normed, 0, keepdims=True)
    scaled = grad_b * gain_ref[...]
    grad_mixed = cot.astype(jnp.float32) + inverse * (
        scaled
        - jnp.mean(scaled, -1, keepdims=True)
        - normed * jnp.mean(scaled * normed, -1, keepdims=True)
    )
    gm_ref[...] = grad_mixed
    grad_heads = product(wout_ref[...], grad_mixed.astype(jnp.bfloat16), NT).astype(jnp.bfloat16)
    for seq in range(seqs):
        for part in range(spread):
            do_ref[seq * spread + part] = grad_heads[
                part * span : (part + 1) * span, seq * local_len : (seq + 1) * local_len
            ]


def half_weights(which, att_ref, cot_ref, gm_ref, b_ref, hid_ref, gg_ref, part_ref, extra_ref, turned, tall):
    seqs, width, local_len = att_ref.shape
    ctx, pairs, chunk, _ = part_ref.shape
    count = gg_ref.shape[1] // width
    depth = width // (2 * pairs)
    down_rows = hid_ref.shape[1] // (2 * pairs)
    split = ctx * chunk - (count + 1) * depth
    cot = jnp.concatenate([cot_ref[k] for k in range(seqs)], 0)
    turned[:width] = b_ref[...].astype(jnp.float32).T
    turned[width : 2 * width] = jnp.concatenate(
        [att_ref[k] for k in range(seqs)], 1
    ).astype(jnp.float32)
    turned[2 * width :] = hid_ref[...].astype(jnp.float32).T

    def chosen(first, height):
        return jnp.concatenate(
            [
                turned[pl.ds(pl.multiple_of(first + (2 * k + which) * height, 8), height)]
                for k in range(pairs)
            ],
            0,
        ).astype(jnp.bfloat16)

    grad_up = product(chosen(width, depth), gm_ref[...].astype(jnp.bfloat16))
    tall[...] = product(chosen(2 * width, down_rows), cot)
    grad_in = product(chosen(0, depth), gg_ref[...])
    for pair in range(pairs):
        wide = slice(pair * depth, (pair + 1) * depth)
        rows = jnp.concatenate(
            [grad_in[wide, k * width : (k + 1) * width] for k in range(count)]
            + [grad_up[wide], tall[pair * down_rows : pair * down_rows + split]],
            0,
        ).astype(jnp.bfloat16)
        for part in range(ctx):
            part_ref[part, pair] = rows[part * chunk : (part + 1) * chunk]
        extra_ref[pair] = tall[pair * down_rows + split : (pair + 1) * down_rows]


def sent_weights_kernel(core_ref, *refs):
    half_weights(1 - core_ref[0], *refs)


def kept_weights_kernel(
    core_ref,
    att_ref,
    cot_ref,
    gm_ref,
    b_ref,
    hid_ref,
    gg_ref,
    wdown_ref,
    mixed_ref,
    part_ref,
    extra_ref,
    out_ref,
    turned,
    tall,
):
    half_weights(
        core_ref[0],
        att_ref,
        cot_ref,
        gm_ref,
        b_ref,
        hid_ref,
        gg_ref,
        part_ref,
        extra_ref,
        turned,
        tall,
    )
    local_len = out_ref.shape[1]
    result = mixed_ref[...] + product(hid_ref[...], wdown_ref[...])
    for seq in range(out_ref.shape[0]):
        out_ref[seq] = result[seq * local_len : (seq + 1) * local_len].astype(jnp.bfloat16)


def qkv_weights_kernel(
    core_ref,
    a_ref,
    g_ref,
    gain_one_ref,
    gain_two_ref,
    kept_extra_ref,
    away_extra_ref,
    kept_ref,
    away_ref,
    w_ref,
):
    pairs, depth, width = kept_ref.shape
    span3 = g_ref.shape[0]
    used = width - 128
    w_ref[:, :span3] = product(a_ref[...].T, g_ref[...], NT)
    lane = used - 128
    gains = jnp.concatenate(
        [
            jnp.zeros((span3 - lane, width), jnp.float32),
            gain_one_ref[...],
            gain_two_ref[...],
            jnp.zeros((used - span3 - 2, width), jnp.float32),
        ],
        0,
    ).T
    w_ref[:, span3:] = gains[:, span3 - lane :]
    core = core_ref[0]
    for pair in range(pairs):
        for ref, extra_ref, which in (
            (kept_ref, kept_extra_ref, core),
            (away_ref, away_extra_ref, 1 - core),
        ):
            rows = pl.ds(pl.multiple_of((2 * pair + which) * depth, 8), depth)
            extra = extra_ref[pair]
            ref[pair] = jnp.concatenate(
                [
                    w_ref[rows],
                    jnp.concatenate(
                        [extra[:, k * 128 : (k + 1) * 128] for k in range(width // 128)], 0
                    ),
                ],
                1,
            ).astype(jnp.bfloat16)


def first_kernel(group_ref, w_ref, gains_ref, out_ref):
    depth, used = out_ref.shape
    spread = 4
    span = w_ref.shape[1] // (3 * spread)
    own_group = group_ref[0]
    gains = gains_ref[...]

    for which in range(spread):

        @pl.when(own_group == which)
        def _():
            picked = [
                w_ref[
                    :, (k * spread + which) * span : (k * spread + which + 1) * span
                ].astype(jnp.float32)
                for k in range(3)
            ]
            out_ref[...] = jnp.concatenate([*picked, gains], 1).astype(jnp.bfloat16)


def finish_kernel(
    ends_ref, gain_one_ref, qkv_ref, wout_ref, gain_two_ref, win_ref, wdown_ref
):
    ctx, _, width = ends_ref.shape
    depth = qkv_ref.shape[0]
    down_rows = wdown_ref.shape[0]
    count = win_ref.shape[1] // width
    spread = ctx // 2
    span = width // spread
    f32 = jnp.float32
    last = [ends_ref[k, :depth].astype(f32) for k in range(ctx)]
    for group in range(spread):
        both = last[group] + last[group + spread]
        for part in range(3):
            qkv_ref[:, part * width + group * span : part * width + (group + 1) * span] = both[
                :, part * span : (part + 1) * span
            ]
    total = last[0]
    for k in range(1, ctx):
        total = total + last[k]
    lane = 3 * span // 128 * 128
    gains = total[:, lane : lane + 128].T
    gain_one_ref[...] = gains[3 * span - lane : 3 * span - lane + 1]
    gain_two_ref[...] = gains[3 * span - lane + 1 : 3 * span - lane + 2]
    main = jnp.concatenate([ends_ref[k, depth:].astype(f32) for k in range(ctx)], 0)
    for k in range(count):
        win_ref[:, k * width : (k + 1) * width] = main[k * depth : (k + 1) * depth]
    wout_ref[...] = main[count * depth : (count + 1) * depth]
    split = main.shape[0] - (count + 1) * depth
    extra = down_rows - split
    wdown_ref[:split] = main[(count + 1) * depth :]
    wdown_ref[split:] = jnp.concatenate(
        [total[k * extra : (k + 1) * extra, width - 128 :] for k in range(width // 128)], 1
    )


def on_device(kernel, outs, args, micros, scratch=(), scalars=0, after=(), name=None):
    space = pl.BlockSpec(memory_space=pltpu.VMEM)
    scalar = pl.BlockSpec(memory_space=pltpu.SMEM)
    given = len(args)

    def ordered(*refs):
        kernel(*refs[:given], *refs[given + len(after) :])

    return pl.pallas_call(
        ordered,
        out_shape=[jax.ShapeDtypeStruct(shape, dtype) for shape, dtype in outs],
        in_specs=[scalar] * scalars
        + [space] * (given - scalars)
        + [pl.BlockSpec(memory_space=pl.ANY)] * len(after),
        out_specs=[space] * len(outs),
        scratch_shapes=list(scratch),
        compiler_params=pltpu.CompilerParams(vmem_limit_bytes=56 * 1024 * 1024),
        cost_estimate=pl.CostEstimate(
            flops=int(micros * 2e10), bytes_accessed=int(micros * 4e7), transcendentals=0
        ),
        name=name,
    )(*args, *after)


def sum_kernel(left_ref, right_ref, out_ref):
    for k in range(out_ref.shape[0]):
        out_ref[k] = (left_ref[k].astype(jnp.float32) + right_ref[k].astype(jnp.float32)).astype(
            jnp.bfloat16
        )


def pass_kernel(in_ref, out_ref):
    out_ref[...] = in_ref[...]


def interleave_kernel(late_ref, held_ref, came_ref, out_ref):
    late = late_ref[0]
    for k in range(held_ref.shape[0]):
        out_ref[k, late] = held_ref[k]
        out_ref[k, 1 - late] = came_ref[k]


def stack_kernel(upper_ref, lower_ref, out_ref):
    rows = upper_ref.shape[0]
    out_ref[:rows] = upper_ref[...]
    out_ref[rows:] = lower_ref[...]


def body(tokens, lengths, deal, gain_attn, w_qkv, w_out, gain_mlp, w_in, w_down, cotangent):
    seqs, local_len, width = tokens.shape
    ctx = lax.axis_size("ctx")
    fsdp = lax.axis_size("fsdp")
    spread = ctx // seqs
    group = HEADS // spread
    span = group * HD
    full_len = local_len * ctx
    rows = seqs * local_len
    context = lax.axis_index("ctx")
    own_seq = context // spread
    own_group = context % spread
    depth = w_qkv.shape[0]
    hidden = w_in.shape[1] // 2
    down_rows = w_down.shape[0]
    f32 = jnp.float32

    offsets = jnp.arange(BLK, dtype=jnp.int32)
    all_pos = (deal[:, None] * BLK + offsets[None, :]).reshape(full_len)
    length = lax.dynamic_slice_in_dim(lengths, own_seq, 1)[0]
    all_keep = all_pos < length

    used = 3 * span + 64
    gains_wide = jnp.pad(
        jnp.stack([gain_attn, gain_mlp], 1).astype(f32), ((0, 0), (0, used - 3 * span - 2))
    )
    first = on_device(
        first_kernel,
        [((depth, used), jnp.bfloat16)],
        (own_group.astype(jnp.int32)[None], w_qkv, gains_wide),
        0.05,
        scalars=1,
        name="first_pack",
    )[0]
    steps = [fsdp >> (k + 1) for k in range(fsdp.bit_length() - 1)]
    held = first[None]
    for bit in steps[:-1]:
        held = doubled(held, "fsdp", bit)
    first_all = doubled(held, "fsdp", steps[-1]).reshape(fsdp * depth, used)
    win_all = lax.all_gather(w_in, "fsdp", axis=0, tiled=True)
    sequence = lax.all_to_all(jnp.repeat(tokens, spread, axis=0), "ctx", 0, 0, tiled=True)
    stacked = on_device(
        stack_kernel,
        [((depth + down_rows, width), jnp.bfloat16)],
        (w_out, w_down),
        0.02,
        after=(held,),
        name="stack_rest",
    )[0]
    rest = doubled(stacked[None], "fsdp", steps[0])
    gain_one = first_all[:, 3 * span]
    gain_two = first_all[:, 3 * span + 1]

    cosine, sine = tables(all_pos)
    bias = jnp.where(all_keep, 0.0, NEGATIVE).astype(f32)[:, None]
    keep_row = all_keep.astype(f32)[None, :]
    sequence = sequence.reshape(full_len, width)
    a_low, qkv, mean, inverse = on_device(
        project_kernel,
        [
            ((full_len, width), jnp.bfloat16),
            ((3 * span, full_len), jnp.bfloat16),
            ((full_len, 1), f32),
            ((full_len, 1), f32),
        ],
        (sequence, first_all, cosine, sine),
        0.3,
        name="project",
    )
    rest = doubled(rest, "fsdp", steps[1], after=(qkv,))
    attended, log_total, unrounded = on_device(
        forward_kernel,
        [
            ((ctx, span, local_len), jnp.bfloat16),
            ((8, full_len), f32),
            ((span, full_len), f32),
        ],
        (qkv, bias, keep_row),
        0.4,
        after=(rest,),
        name="attention_forward",
    )
    att_back = lax.all_to_all(attended, "ctx", 0, 0, tiled=True)
    rest = doubled(rest, "fsdp", steps[2], after=(att_back,))
    rest_other = lax.ppermute(rest, "fsdp", core_pairs(fsdp))
    att_turned = att_back.reshape(seqs, width, local_len)

    resid = tokens.astype(f32).reshape(rows, width)
    count = w_in.shape[1] // width
    main_rows = ((count + 1) * depth + down_rows) // (8 * ctx) * 8 * ctx
    chunk = main_rows // ctx
    split = main_rows - (count + 1) * depth
    extra = down_rows - split
    pairs = fsdp // 2
    core = (lax.axis_index("fsdp") % 2).astype(jnp.int32)[None]
    (
        grad_heads,
        grad_mixed,
        mixed,
        b_low,
        hid_low,
        grad_gate_up,
        grad_gain_two,
        wdown_all,
    ) = on_device(
        mlp_kernel,
        [
            ((ctx, span, local_len), jnp.bfloat16),
            ((rows, width), f32),
            ((rows, width), f32),
            ((rows, width), jnp.bfloat16),
            ((rows, hidden), jnp.bfloat16),
            ((rows, 2 * hidden), jnp.bfloat16),
            ((1, width), f32),
            ((hidden, width), jnp.bfloat16),
        ],
        (
            core,
            tokens,
            att_turned,
            cotangent,
            gain_two.astype(f32)[None, :],
            rest,
            rest_other,
            win_all,
        ),
        0.5,
        [pltpu.VMEM((fsdp * depth, width), jnp.bfloat16)],
        scalars=1,
        name="mlp",
    )
    weights_in = (core, att_turned, cotangent, grad_mixed, b_low, hid_low, grad_gate_up)
    half_outs = [
        ((ctx, pairs, chunk, width), jnp.bfloat16),
        ((pairs, extra, width), f32),
    ]
    half_scratch = [
        pltpu.VMEM((2 * width + hidden, rows), f32),
        pltpu.VMEM((hidden // 2, width), f32),
    ]
    main_away, away_extra = on_device(
        sent_weights_kernel,
        half_outs,
        weights_in,
        5,
        half_scratch,
        scalars=1,
        name="sent_weights",
    )
    main_kept, kept_extra, output = on_device(
        kept_weights_kernel,
        [*half_outs, (tokens.shape, jnp.bfloat16)],
        (*weights_in, wdown_all, mixed),
        0.05,
        half_scratch,
        scalars=1,
        after=(main_away,),
        name="kept_weights",
    )
    main_pair = core_sum(main_kept, main_away, "fsdp", 0.02, name="sum_cores")
    main_part = lax.psum_scatter(
        main_pair.reshape(-1, chunk, width), "ctx", scatter_dimension=0, tiled=True
    )

    all_grad = lax.all_to_all(grad_heads, "ctx", 0, 0, tiled=True)
    grad_qkv, grad_a_part, grad_gain_one = on_device(
        backward_kernel,
        [
            ((3 * span, full_len), jnp.bfloat16),
            ((ctx, local_len, width), jnp.bfloat16),
            ((1, width), f32),
        ],
        (
            all_grad,
            qkv,
            log_total,
            unrounded,
            cosine,
            sine,
            bias,
            keep_row,
            sequence,
            mean,
            inverse,
            first_all,
        ),
        12,
        [pltpu.VMEM((HD, full_len), f32)] * 2,
        after=(main_pair,),
        name="attention_backward",
    )
    grad_a_parts = lax.all_to_all(grad_a_part, "ctx", 0, 0, tiled=True)
    last_kept, last_away = on_device(
        qkv_weights_kernel,
        [((pairs, depth, width), jnp.bfloat16)] * 2,
        (core, a_low, grad_qkv, grad_gain_one, grad_gain_two, kept_extra, away_extra),
        0.1,
        [pltpu.VMEM((width, used), f32)],
        scalars=1,
        name="qkv_weights",
    )
    last = core_sum(
        last_kept, last_away, "fsdp", 0.05, name="sum_cores_last"
    )
    grad_a = jnp.sum(
        grad_a_parts.reshape(seqs, spread, local_len, width).astype(f32), 1
    ).reshape(rows, width)
    _, normed_one, inverse_one = norm_forward(resid, gain_one)
    grad_norm_one, _ = norm_backward(grad_a, gain_one, normed_one, inverse_one)
    grad_input = grad_mixed + grad_norm_one

    last = spread_sum_permuted(last, "fsdp")
    main_part = on_device(
        pass_kernel,
        [(main_part.shape, jnp.bfloat16)],
        (main_part,),
        0.02,
        after=(grad_a_parts,),
        name="after_exchange",
    )[0]
    main_part = spread_sum(main_part, "fsdp")
    share = jnp.concatenate([last, main_part], 0)
    ends = gather_by_exchange(share, "ctx", ctx)
    finished = on_device(
        finish_kernel,
        [
            ((1, depth), f32),
            (w_qkv.shape, f32),
            (w_out.shape, f32),
            ((1, depth), f32),
            (w_in.shape, f32),
            (w_down.shape, f32),
        ],
        (ends,),
        3,
        name="finish",
    )
    return (
        output,
        grad_input.reshape(tokens.shape),
        finished[0].reshape(depth),
        finished[1],
        finished[2],
        finished[3].reshape(depth),
        finished[4],
        finished[5],
    )


def solution(mesh):
    placed = (
        P("fsdp", "ctx", None),
        P("fsdp"),
        P(),
        P("fsdp"),
        P("fsdp", None),
        P("fsdp", None),
        P("fsdp"),
        P("fsdp", None),
        P("fsdp", None),
        P("fsdp", "ctx", None),
    )
    return jax.shard_map(
        body,
        mesh=mesh,
        in_specs=placed,
        out_specs=(
            P("fsdp", "ctx", None),
            P("fsdp", "ctx", None),
            P("fsdp"),
            P("fsdp", None),
            P("fsdp", None),
            P("fsdp"),
            P("fsdp", None),
            P("fsdp", None),
        ),
        check_vma=False,
    )
```

```python
import math

import jax
import jax.numpy as jnp
from jax import lax
from jax.experimental import pallas as pl
from jax.experimental.pallas import tpu as pltpu
from jax.sharding import PartitionSpec as P

HEADS = 12
HD = 64
BLK = 128


EPS = 1e-05
THETA = 160000.0
NEGATIVE = -1e30
INV_ROOT_TWO = 0.7071067811865476
INV_ROOT_TWO_PI = 0.3989422804014327


def gather_by_exchange(part, axis, n):
    return lax.all_to_all(jnp.broadcast_to(part[None], (n, *part.shape)), axis, 0, 0)


def core_pairs(n):
    return [(k, k ^ 1) for k in range(n)]


def core_groups(n):
    return [list(range(first, n, 2)) for first in range(2)]


def doubled(held, axis, bit, after=()):
    n = lax.axis_size(axis)
    index = lax.axis_index(axis)
    came = lax.ppermute(held, axis, [(k, k ^ bit) for k in range(n)])
    if after:
        held = on_device(
            interleave_kernel,
            [((held.shape[0], 2, *held.shape[1:]), held.dtype)],
            ((index // bit % 2).astype(jnp.int32)[None], held, came),
            0.02,
            scalars=1,
            after=after,
            name="interleave",
        )[0]
    else:
        first = (index & bit) == 0
        held = jnp.where(first, jnp.stack([held, came], 1), jnp.stack([came, held], 1))
    return held.reshape(-1, *held.shape[2:])


def core_sum(kept, away, axis, micros, after=(), name=None):
    came = lax.ppermute(away, axis, core_pairs(lax.axis_size(axis)))
    return on_device(
        sum_kernel, [(kept.shape, jnp.bfloat16)], (kept, came), micros, after=after, name=name
    )[0]


def spread_sum(parts, axis):
    groups = core_groups(lax.axis_size(axis))
    shares = lax.all_to_all(parts, axis, 0, 0, tiled=True, axis_index_groups=groups)
    return low(jnp.sum(shares.astype(jnp.float32), 0))


def spread_sum_permuted(parts, axis, after=()):
    n = lax.axis_size(axis)
    half = n // 2
    chip = lax.axis_index(axis) // 2
    total = lax.dynamic_index_in_dim(parts, chip, 0, keepdims=False).astype(jnp.float32)
    for away in range(1, half):
        piece = lax.dynamic_index_in_dim(parts, (chip + away) % half, 0, keepdims=False)
        moves = [(k, (k + 2 * away) % n) for k in range(n)]
        total = total + lax.ppermute(piece, axis, moves).astype(jnp.float32)
    return low(total)


def low(values):
    return values.astype(jnp.bfloat16)


def tables(positions):
    halves = jnp.arange(HD // 2, dtype=jnp.float32)
    frequency = THETA ** (-2.0 * halves / HD)
    angles = frequency[:, None] * positions.astype(jnp.float32)[None, :]
    return jnp.cos(angles), jnp.sin(angles)


def norm_forward(rows_in, gain):
    centre = rows_in - jnp.mean(rows_in, -1, keepdims=True)
    variance = jnp.mean(centre * centre, -1, keepdims=True)
    inverse = lax.rsqrt(variance + EPS)
    normed = centre * inverse
    return (normed * gain.astype(jnp.float32), normed, inverse)


def norm_backward(grad_rows, gain, normed, inverse):
    scaled = grad_rows * gain.astype(jnp.float32)
    grad_gain = jnp.sum(grad_rows * normed, 0)
    grad_rows_in = inverse * (
        scaled
        - jnp.mean(scaled, -1, keepdims=True)
        - normed * jnp.mean(scaled * normed, -1, keepdims=True)
    )
    return (grad_rows_in, grad_gain)


NN = (((1,), (0,)), ((), ()))
NT = (((1,), (1,)), ((), ()))
ROWS = 256
COLS = 256


def product(left, right, dims=NN):
    return lax.dot_general(left, right, dims, preferred_element_type=jnp.float32)


def project_kernel(
    seq_ref, w_ref, cos_ref, sin_ref, a_ref, qkv_ref, mean_ref, inverse_ref
):
    full_len, width = seq_ref.shape
    span = qkv_ref.shape[0] // 3
    group = span // HD
    half = HD // 2
    gain = w_ref[:, 512:640].astype(jnp.float32).T[3 * span - 512 : 3 * span - 511]
    w_turned = w_ref[:, : 3 * span].astype(jnp.float32).T.astype(jnp.bfloat16)
    for start in range(0, full_len, ROWS):
        rows = slice(start, start + ROWS)
        x = seq_ref[rows].astype(jnp.float32)
        mean = jnp.mean(x, -1, keepdims=True)
        centre = x - mean
        inverse = lax.rsqrt(jnp.mean(centre * centre, -1, keepdims=True) + EPS)
        mean_ref[rows] = mean
        inverse_ref[rows] = inverse
        a_low = (centre * inverse * gain).astype(jnp.bfloat16)
        a_ref[rows] = a_low
        joined = product(w_turned, a_low, NT)
        cosine = cos_ref[:, rows]
        sine = sin_ref[:, rows]
        for part in range(2 * group):
            one = joined[part * HD : part * HD + half]
            two = joined[part * HD + half : (part + 1) * HD]
            scale = HD ** (-0.5) if part < group else 1.0
            for at, value in (
                (0, one * cosine - two * sine),
                (half, two * cosine + one * sine),
            ):
                qkv_ref[part * HD + at : part * HD + at + half, rows] = (
                    value.astype(jnp.bfloat16) * scale
                ).astype(jnp.bfloat16)
        qkv_ref[2 * span :, rows] = joined[2 * span :].astype(jnp.bfloat16)


def forward_kernel(qkv_ref, bias_ref, keep_ref, out_ref, lse_ref, o_ref):
    span, full_len = o_ref.shape
    group = span // HD
    blk = out_ref.shape[2]
    for head in range(group):
        here = slice(head * HD, (head + 1) * HD)
        keys = qkv_ref[span + head * HD : span + (head + 1) * HD].T
        values = qkv_ref[2 * span + head * HD : 2 * span + (head + 1) * HD]
        for start in range(0, full_len, COLS):
            cols = slice(start, start + COLS)
            scores = product(keys, qkv_ref[here, cols]) + bias_ref[...]
            maximum = jnp.max(scores, 0, keepdims=True)
            exponent = jnp.exp(scores - maximum)
            total = jnp.sum(exponent, 0, keepdims=True)
            attended = product(values, exponent.astype(jnp.bfloat16))
            attended = attended * (keep_ref[:, cols] / total)
            o_ref[here, cols] = attended
            lse_ref[head : head + 1, cols] = maximum + jnp.log(total)
            for first in range(0, COLS, blk):
                out_ref[(start + first) // blk, here, :] = attended[
                    :, first : first + blk
                ].astype(jnp.bfloat16)


def backward_kernel(
    do_ref,
    qkv_ref,
    lse_ref,
    o_ref,
    cos_ref,
    sin_ref,
    bias_ref,
    keep_ref,
    seq_ref,
    mean_ref,
    inverse_ref,
    w_ref,
    g_ref,
    ga_ref,
    gain_ref,
    dk_ref,
    dv_ref,
):
    span, full_len = o_ref.shape
    group = span // HD
    half = HD // 2
    blk = do_ref.shape[2]
    for head in range(group):
        here = slice(head * HD, (head + 1) * HD)
        keys_turned = qkv_ref[span + head * HD : span + (head + 1) * HD]
        keys = keys_turned.T
        values = qkv_ref[2 * span + head * HD : 2 * span + (head + 1) * HD].T
        for start in range(0, full_len, COLS):
            cols = slice(start, start + COLS)
            query = qkv_ref[here, cols]
            grad_out = jnp.concatenate(
                [do_ref[(start + first) // blk, here, :] for first in range(0, COLS, blk)], 1
            )
            grad_out = grad_out.astype(jnp.float32) * keep_ref[:, cols]
            delta = jnp.sum(grad_out * o_ref[here, cols], 0, keepdims=True)
            grad_out = grad_out.astype(jnp.bfloat16)
            scores = product(keys, query) + bias_ref[...]
            probs = jnp.exp(scores - lse_ref[head : head + 1, cols])
            grad_scores = (probs * (product(values, grad_out) - delta)).astype(jnp.bfloat16)
            grad_value = product(grad_out, probs.astype(jnp.bfloat16), NT)
            grad_key = product(query, grad_scores, NT)
            if start == 0:
                dv_ref[...] = grad_value
                dk_ref[...] = grad_key
            else:
                dv_ref[...] += grad_value
                dk_ref[...] += grad_key
            grad_query = product(keys_turned, grad_scores) * HD ** (-0.5)
            cosine = cos_ref[:, cols]
            sine = sin_ref[:, cols]
            one, two = grad_query[:half], grad_query[half:]
            g_ref[head * HD : head * HD + half, cols] = (one * cosine + two * sine).astype(
                jnp.bfloat16
            )
            g_ref[head * HD + half : (head + 1) * HD, cols] = (
                two * cosine - one * sine
            ).astype(jnp.bfloat16)
        one, two = dk_ref[:half], dk_ref[half:]
        cosine = cos_ref[...]
        sine = sin_ref[...]
        low_at = span + head * HD
        g_ref[low_at : low_at + half] = (one * cosine + two * sine).astype(jnp.bfloat16)
        g_ref[low_at + half : low_at + HD] = (two * cosine - one * sine).astype(jnp.bfloat16)
        g_ref[2 * span + head * HD : 2 * span + (head + 1) * HD] = dv_ref[...].astype(
            jnp.bfloat16
        )
    for start in range(0, full_len, ROWS):
        rows = slice(start, start + ROWS)
        grad_a = product(g_ref[:, rows].T, w_ref[:, : 3 * span], NT)
        normed = (seq_ref[rows].astype(jnp.float32) - mean_ref[rows]) * inverse_ref[rows]
        summed = jnp.sum(grad_a * normed, 0, keepdims=True)
        gain_ref[...] = summed if start == 0 else gain_ref[...] + summed
        for first in range(0, ROWS, blk):
            ga_ref[(start + first) // blk] = grad_a[first : first + blk].astype(jnp.bfloat16)


def mlp_kernel(
    core_ref,
    tok_ref,
    att_ref,
    cot_ref,
    gain_ref,
    mine_ref,
    other_ref,
    win_ref,
    do_ref,
    gm_ref,
    mixed_ref,
    b_ref,
    hid_ref,
    gg_ref,
    grad_gain_ref,
    wdown_ref,
    wout_ref,
):
    pairs, height, _ = mine_ref.shape
    depth = wout_ref.shape[0] // (2 * pairs)
    down_rows = height - depth
    even = core_ref[0] == 0
    for pair in range(pairs):
        mine = mine_ref[pair].astype(jnp.float32)
        other = other_ref[pair].astype(jnp.float32)
        first = jnp.where(even, mine, other)
        second = jnp.where(even, other, mine)
        wout_ref[2 * pair * depth : 2 * (pair + 1) * depth] = jnp.concatenate(
            [first[:depth], second[:depth]], 0
        ).astype(jnp.bfloat16)
        wdown_ref[2 * pair * down_rows : 2 * (pair + 1) * down_rows] = jnp.concatenate(
            [first[depth:], second[depth:]], 0
        ).astype(jnp.bfloat16)
    seqs, local_len, width = tok_ref.shape
    spread = do_ref.shape[0] // seqs
    span = do_ref.shape[1]
    hidden = hid_ref.shape[1]
    resid = jnp.concatenate([tok_ref[k] for k in range(seqs)], 0).astype(jnp.float32)
    att = jnp.concatenate([att_ref[k].T for k in range(seqs)], 0)
    cot = jnp.concatenate([cot_ref[k] for k in range(seqs)], 0)
    mixed = resid + product(att, wout_ref[...])
    mixed_ref[...] = mixed
    centre = mixed - jnp.mean(mixed, -1, keepdims=True)
    inverse = lax.rsqrt(jnp.mean(centre * centre, -1, keepdims=True) + EPS)
    normed = centre * inverse
    b_low = (normed * gain_ref[...]).astype(jnp.bfloat16)
    b_ref[...] = b_low
    for first in range(0, hidden, hidden // 3):
        here = slice(first, first + hidden // 3)
        there = slice(hidden + first, hidden + first + hidden // 3)
        gate_in = product(b_low, win_ref[:, here])
        up_half = product(b_low, win_ref[:, there])
        grad_hid = product(cot, wdown_ref[here], NT)
        normal_cdf = 0.5 * (1.0 + lax.erf(gate_in * INV_ROOT_TWO))
        gelu_out = gate_in * normal_cdf
        hid_ref[:, here] = (gelu_out * up_half).astype(jnp.bfloat16)
        normal_pdf = jnp.exp(-0.5 * gate_in * gate_in) * INV_ROOT_TWO_PI
        gg_ref[:, here] = (grad_hid * up_half * (normal_cdf + gate_in * normal_pdf)).astype(
            jnp.bfloat16
        )
        gg_ref[:, there] = (grad_hid * gelu_out).astype(jnp.bfloat16)
    grad_b = product(gg_ref[...], win_ref[...], NT)
    grad_gain_ref[...] = jnp.sum(grad_b * normed, 0, keepdims=True)
    scaled = grad_b * gain_ref[...]
    grad_mixed = cot.astype(jnp.float32) + inverse * (
        scaled
        - jnp.mean(scaled, -1, keepdims=True)
        - normed * jnp.mean(scaled * normed, -1, keepdims=True)
    )
    gm_ref[...] = grad_mixed
    grad_heads = product(wout_ref[...], grad_mixed.astype(jnp.bfloat16), NT).astype(jnp.bfloat16)
    for seq in range(seqs):
        for part in range(spread):
            do_ref[seq * spread + part] = grad_heads[
                part * span : (part + 1) * span, seq * local_len : (seq + 1) * local_len
            ]


def mlp_weights_kernel(
    core_ref,
    att_ref,
    cot_ref,
    gm_ref,
    b_ref,
    hid_ref,
    gg_ref,
    away_ref,
    away_extra_ref,
    kept_ref,
    kept_extra_ref,
    turned,
    tall,
):
    seqs, width, _ = att_ref.shape
    ctx, pairs, chunk, _ = kept_ref.shape
    count = gg_ref.shape[1] // width
    depth = width // (2 * pairs)
    down_rows = hid_ref.shape[1] // (2 * pairs)
    split = ctx * chunk - (count + 1) * depth
    cot = jnp.concatenate([cot_ref[k] for k in range(seqs)], 0)
    grad_att = gm_ref[...].astype(jnp.bfloat16)
    turned[:width] = b_ref[...].astype(jnp.float32).T
    turned[width : 2 * width] = jnp.concatenate(
        [att_ref[k] for k in range(seqs)], 1
    ).astype(jnp.float32)
    turned[2 * width :] = hid_ref[...].astype(jnp.float32).T
    core = core_ref[0]
    for which, part_ref, extra_ref in (
        (1 - core, away_ref, away_extra_ref),
        (core, kept_ref, kept_extra_ref),
    ):

        def chosen(first, height):
            return jnp.concatenate(
                [
                    turned[pl.ds(pl.multiple_of(first + (2 * k + which) * height, 8), height)]
                    for k in range(pairs)
                ],
                0,
            ).astype(jnp.bfloat16)

        grad_up = product(chosen(width, depth), grad_att)
        tall[...] = product(chosen(2 * width, down_rows), cot)
        grad_in = product(chosen(0, depth), gg_ref[...])
        for pair in range(pairs):
            wide = slice(pair * depth, (pair + 1) * depth)
            rows = jnp.concatenate(
                [grad_in[wide, k * width : (k + 1) * width] for k in range(count)]
                + [grad_up[wide], tall[pair * down_rows : pair * down_rows + split]],
                0,
            ).astype(jnp.bfloat16)
            for part in range(ctx):
                part_ref[part, pair] = rows[part * chunk : (part + 1) * chunk]
            extra_ref[pair] = tall[pair * down_rows + split : (pair + 1) * down_rows]


def layer_out_kernel(mixed_ref, hid_ref, wdown_ref, out_ref):
    local_len = out_ref.shape[1]
    result = mixed_ref[...] + product(hid_ref[...], wdown_ref[...])
    for seq in range(out_ref.shape[0]):
        out_ref[seq] = result[seq * local_len : (seq + 1) * local_len].astype(jnp.bfloat16)


def qkv_weights_kernel(
    core_ref,
    a_ref,
    g_ref,
    gain_one_ref,
    gain_two_ref,
    kept_extra_ref,
    away_extra_ref,
    kept_ref,
    away_ref,
    w_ref,
):
    pairs, depth, width = kept_ref.shape
    span3 = g_ref.shape[0]
    used = width - 128
    w_ref[:, :span3] = product(a_ref[...].T, g_ref[...], NT)
    lane = used - 128
    gains = jnp.concatenate(
        [
            jnp.zeros((span3 - lane, width), jnp.float32),
            gain_one_ref[...],
            gain_two_ref[...],
            jnp.zeros((used - span3 - 2, width), jnp.float32),
        ],
        0,
    ).T
    w_ref[:, span3:] = gains[:, span3 - lane :]
    core = core_ref[0]
    for pair in range(pairs):
        for ref, extra_ref, which in (
            (kept_ref, kept_extra_ref, core),
            (away_ref, away_extra_ref, 1 - core),
        ):
            rows = pl.ds(pl.multiple_of((2 * pair + which) * depth, 8), depth)
            extra = extra_ref[pair]
            ref[pair] = jnp.concatenate(
                [
                    w_ref[rows],
                    jnp.concatenate(
                        [extra[:, k * 128 : (k + 1) * 128] for k in range(width // 128)], 0
                    ),
                ],
                1,
            ).astype(jnp.bfloat16)


def first_kernel(group_ref, w_ref, gains_ref, out_ref):
    depth, used = out_ref.shape
    spread = 4
    span = w_ref.shape[1] // (3 * spread)
    own_group = group_ref[0]
    gains = gains_ref[...]

    for which in range(spread):

        @pl.when(own_group == which)
        def _():
            picked = [
                w_ref[
                    :, (k * spread + which) * span : (k * spread + which + 1) * span
                ].astype(jnp.float32)
                for k in range(3)
            ]
            out_ref[...] = jnp.concatenate([*picked, gains], 1).astype(jnp.bfloat16)


def finish_kernel(
    ends_ref, gain_one_ref, qkv_ref, wout_ref, gain_two_ref, win_ref, wdown_ref
):
    ctx, _, width = ends_ref.shape
    depth = qkv_ref.shape[0]
    down_rows = wdown_ref.shape[0]
    count = win_ref.shape[1] // width
    spread = ctx // 2
    span = width // spread
    f32 = jnp.float32
    last = [ends_ref[k, :depth].astype(f32) for k in range(ctx)]
    for group in range(spread):
        both = last[group] + last[group + spread]
        for part in range(3):
            qkv_ref[:, part * width + group * span : part * width + (group + 1) * span] = both[
                :, part * span : (part + 1) * span
            ]
    total = last[0]
    for k in range(1, ctx):
        total = total + last[k]
    lane = 3 * span // 128 * 128
    gains = total[:, lane : lane + 128].T
    gain_one_ref[...] = gains[3 * span - lane : 3 * span - lane + 1]
    gain_two_ref[...] = gains[3 * span - lane + 1 : 3 * span - lane + 2]
    main = jnp.concatenate([ends_ref[k, depth:].astype(f32) for k in range(ctx)], 0)
    for k in range(count):
        win_ref[:, k * width : (k + 1) * width] = main[k * depth : (k + 1) * depth]
    wout_ref[...] = main[count * depth : (count + 1) * depth]
    split = main.shape[0] - (count + 1) * depth
    extra = down_rows - split
    wdown_ref[:split] = main[(count + 1) * depth :]
    wdown_ref[split:] = jnp.concatenate(
        [total[k * extra : (k + 1) * extra, width - 128 :] for k in range(width // 128)], 1
    )


def on_device(kernel, outs, args, micros, scratch=(), scalars=0, after=(), name=None):
    space = pl.BlockSpec(memory_space=pltpu.VMEM)
    scalar = pl.BlockSpec(memory_space=pltpu.SMEM)
    given = len(args)

    def ordered(*refs):
        kernel(*refs[:given], *refs[given + len(after) :])

    return pl.pallas_call(
        ordered,
        out_shape=[jax.ShapeDtypeStruct(shape, dtype) for shape, dtype in outs],
        in_specs=[scalar] * scalars
        + [space] * (given - scalars)
        + [pl.BlockSpec(memory_space=pl.ANY)] * len(after),
        out_specs=[space] * len(outs),
        scratch_shapes=list(scratch),
        compiler_params=pltpu.CompilerParams(vmem_limit_bytes=24 * 1024 * 1024),
        cost_estimate=pl.CostEstimate(
            flops=int(micros * 2e10), bytes_accessed=int(micros * 4e7), transcendentals=0
        ),
        name=name,
    )(*args, *after)


def sum_kernel(left_ref, right_ref, out_ref):
    for k in range(out_ref.shape[0]):
        out_ref[k] = (left_ref[k].astype(jnp.float32) + right_ref[k].astype(jnp.float32)).astype(
            jnp.bfloat16
        )


def pass_kernel(in_ref, out_ref):
    out_ref[...] = in_ref[...]


def interleave_kernel(late_ref, held_ref, came_ref, out_ref):
    late = late_ref[0]
    for k in range(held_ref.shape[0]):
        out_ref[k, late] = held_ref[k]
        out_ref[k, 1 - late] = came_ref[k]


def stack_kernel(upper_ref, lower_ref, out_ref):
    rows = upper_ref.shape[0]
    out_ref[:rows] = upper_ref[...]
    out_ref[rows:] = lower_ref[...]


def body(tokens, lengths, deal, gain_attn, w_qkv, w_out, gain_mlp, w_in, w_down, cotangent):
    seqs, local_len, width = tokens.shape
    ctx = lax.axis_size("ctx")
    fsdp = lax.axis_size("fsdp")
    spread = ctx // seqs
    group = HEADS // spread
    span = group * HD
    full_len = local_len * ctx
    rows = seqs * local_len
    context = lax.axis_index("ctx")
    own_seq = context // spread
    own_group = context % spread
    depth = w_qkv.shape[0]
    hidden = w_in.shape[1] // 2
    down_rows = w_down.shape[0]
    f32 = jnp.float32

    offsets = jnp.arange(BLK, dtype=jnp.int32)
    all_pos = (deal[:, None] * BLK + offsets[None, :]).reshape(full_len)
    length = lax.dynamic_slice_in_dim(lengths, own_seq, 1)[0]
    all_keep = all_pos < length

    used = 3 * span + 64
    gains_wide = jnp.pad(
        jnp.stack([gain_attn, gain_mlp], 1).astype(f32), ((0, 0), (0, used - 3 * span - 2))
    )
    first = on_device(
        first_kernel,
        [((depth, used), jnp.bfloat16)],
        (own_group.astype(jnp.int32)[None], w_qkv, gains_wide),
        0.05,
        scalars=1,
        name="first_pack",
    )[0]
    steps = [fsdp >> (k + 1) for k in range(fsdp.bit_length() - 1)]
    held = first[None]
    for bit in steps[:-1]:
        held = doubled(held, "fsdp", bit)
    first_all = doubled(held, "fsdp", steps[-1]).reshape(fsdp * depth, used)
    win_all = lax.all_gather(w_in, "fsdp", axis=0, tiled=True)
    sequence = lax.all_to_all(jnp.repeat(tokens, spread, axis=0), "ctx", 0, 0, tiled=True)
    stacked = on_device(
        stack_kernel,
        [((depth + down_rows, width), jnp.bfloat16)],
        (w_out, w_down),
        0.02,
        after=(held,),
        name="stack_rest",
    )[0]
    gain_one = first_all[:, 3 * span]
    gain_two = first_all[:, 3 * span + 1]

    cosine, sine = tables(all_pos)
    bias = jnp.where(all_keep, 0.0, NEGATIVE).astype(f32)[:, None]
    keep_row = all_keep.astype(f32)[None, :]
    sequence = sequence.reshape(full_len, width)
    a_low, qkv, mean, inverse = on_device(
        project_kernel,
        [
            ((full_len, width), jnp.bfloat16),
            ((3 * span, full_len), jnp.bfloat16),
            ((full_len, 1), f32),
            ((full_len, 1), f32),
        ],
        (sequence, first_all, cosine, sine),
        0.3,
        name="project",
    )
    rest = doubled(stacked[None], "fsdp", steps[0], after=(qkv,))
    attended, log_total, unrounded = on_device(
        forward_kernel,
        [
            ((ctx, span, local_len), jnp.bfloat16),
            ((8, full_len), f32),
            ((span, full_len), f32),
        ],
        (qkv, bias, keep_row),
        0.8,
        after=(rest,),
        name="attention_forward",
    )
    rest = doubled(rest, "fsdp", steps[1], after=(attended,))
    att_back = lax.all_to_all(attended, "ctx", 0, 0, tiled=True)
    rest = doubled(rest, "fsdp", steps[2], after=(att_back,))
    rest_other = lax.ppermute(rest, "fsdp", core_pairs(fsdp))
    att_turned = att_back.reshape(seqs, width, local_len)

    resid = tokens.astype(f32).reshape(rows, width)
    count = w_in.shape[1] // width
    main_rows = ((count + 1) * depth + down_rows) // (8 * ctx) * 8 * ctx
    chunk = main_rows // ctx
    split = main_rows - (count + 1) * depth
    extra = down_rows - split
    pairs = fsdp // 2
    core = (lax.axis_index("fsdp") % 2).astype(jnp.int32)[None]
    (
        grad_heads,
        grad_mixed,
        mixed,
        b_low,
        hid_low,
        grad_gate_up,
        grad_gain_two,
        wdown_all,
    ) = on_device(
        mlp_kernel,
        [
            ((ctx, span, local_len), jnp.bfloat16),
            ((rows, width), f32),
            ((rows, width), f32),
            ((rows, width), jnp.bfloat16),
            ((rows, hidden), jnp.bfloat16),
            ((rows, 2 * hidden), jnp.bfloat16),
            ((1, width), f32),
            ((hidden, width), jnp.bfloat16),
        ],
        (
            core,
            tokens,
            att_turned,
            cotangent,
            gain_two.astype(f32)[None, :],
            rest,
            rest_other,
            win_all,
        ),
        0.5,
        [pltpu.VMEM((fsdp * depth, width), jnp.bfloat16)],
        scalars=1,
        name="mlp",
    )
    half_outs = [
        ((ctx, pairs, chunk, width), jnp.bfloat16),
        ((pairs, extra, width), f32),
    ]
    main_away, away_extra, main_kept, kept_extra = on_device(
        mlp_weights_kernel,
        half_outs * 2,
        (core, att_turned, cotangent, grad_mixed, b_low, hid_low, grad_gate_up),
        0.05,
        [
            pltpu.VMEM((2 * width + hidden, rows), f32),
            pltpu.VMEM((hidden // 2, width), f32),
        ],
        scalars=1,
        name="mlp_weights",
    )
    main_pair = core_sum(main_kept, main_away, "fsdp", 0.02, name="sum_cores")
    main_part = lax.psum_scatter(
        main_pair.reshape(-1, chunk, width), "ctx", scatter_dimension=0, tiled=True
    )

    all_grad = lax.all_to_all(grad_heads, "ctx", 0, 0, tiled=True)
    grad_qkv, grad_a_part, grad_gain_one = on_device(
        backward_kernel,
        [
            ((3 * span, full_len), jnp.bfloat16),
            ((ctx, local_len, width), jnp.bfloat16),
            ((1, width), f32),
        ],
        (
            all_grad,
            qkv,
            log_total,
            unrounded,
            cosine,
            sine,
            bias,
            keep_row,
            sequence,
            mean,
            inverse,
            first_all,
        ),
        12,
        [pltpu.VMEM((HD, full_len), f32)] * 2,
        after=(main_pair,),
        name="attention_backward",
    )
    grad_a_parts = lax.all_to_all(grad_a_part, "ctx", 0, 0, tiled=True)
    output = on_device(
        layer_out_kernel,
        [(tokens.shape, jnp.bfloat16)],
        (mixed, hid_low, wdown_all),
        0.05,
        after=(grad_a_part,),
        name="layer_out",
    )[0]
    last_kept, last_away = on_device(
        qkv_weights_kernel,
        [((pairs, depth, width), jnp.bfloat16)] * 2,
        (core, a_low, grad_qkv, grad_gain_one, grad_gain_two, kept_extra, away_extra),
        0.1,
        [pltpu.VMEM((width, used), f32)],
        scalars=1,
        name="qkv_weights",
    )
    last = core_sum(
        last_kept, last_away, "fsdp", 0.05, name="sum_cores_last"
    )
    grad_a = jnp.sum(
        grad_a_parts.reshape(seqs, spread, local_len, width).astype(f32), 1
    ).reshape(rows, width)
    _, normed_one, inverse_one = norm_forward(resid, gain_one)
    grad_norm_one, _ = norm_backward(grad_a, gain_one, normed_one, inverse_one)
    grad_input = grad_mixed + grad_norm_one

    last = spread_sum_permuted(last, "fsdp")
    main_part = on_device(
        pass_kernel,
        [(main_part.shape, jnp.bfloat16)],
        (main_part,),
        0.02,
        after=(grad_a_parts, last),
        name="after_exchange",
    )[0]
    main_part = spread_sum(main_part, "fsdp")
    share = jnp.concatenate([last, main_part], 0)
    ends = gather_by_exchange(share, "ctx", ctx)
    finished = on_device(
        finish_kernel,
        [
            ((1, depth), f32),
            (w_qkv.shape, f32),
            (w_out.shape, f32),
            ((1, depth), f32),
            (w_in.shape, f32),
            (w_down.shape, f32),
        ],
        (ends,),
        3,
        name="finish",
    )
    return (
        output,
        grad_input.reshape(tokens.shape),
        finished[0].reshape(depth),
        finished[1],
        finished[2],
        finished[3].reshape(depth),
        finished[4],
        finished[5],
    )


def solution(mesh):
    placed = (
        P("fsdp", "ctx", None),
        P("fsdp"),
        P(),
        P("fsdp"),
        P("fsdp", None),
        P("fsdp", None),
        P("fsdp"),
        P("fsdp", None),
        P("fsdp", None),
        P("fsdp", "ctx", None),
    )
    return jax.shard_map(
        body,
        mesh=mesh,
        in_specs=placed,
        out_specs=(
            P("fsdp", "ctx", None),
            P("fsdp", "ctx", None),
            P("fsdp"),
            P("fsdp", None),
            P("fsdp", None),
            P("fsdp"),
            P("fsdp", None),
            P("fsdp", None),
        ),
        check_vma=False,
    )
```

```python
import math

import jax
import jax.numpy as jnp
from jax import lax
from jax.experimental import pallas as pl
from jax.experimental.pallas import tpu as pltpu
from jax.sharding import PartitionSpec as P

HEADS = 12
HD = 64
BLK = 128


EPS = 1e-05
THETA = 160000.0
NEGATIVE = -1e30
INV_ROOT_TWO = 0.7071067811865476
INV_ROOT_TWO_PI = 0.3989422804014327


def gather_by_exchange(part, axis, n):
    return lax.all_to_all(jnp.broadcast_to(part[None], (n, *part.shape)), axis, 0, 0)


def core_pairs(n):
    return [(k, k ^ 1) for k in range(n)]


def core_groups(n):
    return [list(range(first, n, 2)) for first in range(2)]


def doubled(held, axis, bit, after=()):
    n = lax.axis_size(axis)
    index = lax.axis_index(axis)
    came = lax.ppermute(held, axis, [(k, k ^ bit) for k in range(n)])
    if after:
        held = on_device(
            interleave_kernel,
            [((held.shape[0], 2, *held.shape[1:]), held.dtype)],
            ((index // bit % 2).astype(jnp.int32)[None], held, came),
            0.02,
            scalars=1,
            after=after,
            name="interleave",
        )[0]
    else:
        first = (index & bit) == 0
        held = jnp.where(first, jnp.stack([held, came], 1), jnp.stack([came, held], 1))
    return held.reshape(-1, *held.shape[2:])


def core_sum(kept, away, axis, micros, after=(), name=None):
    came = lax.ppermute(away, axis, core_pairs(lax.axis_size(axis)))
    return on_device(
        sum_kernel, [(kept.shape, jnp.bfloat16)], (kept, came), micros, after=after, name=name
    )[0]


def spread_sum(parts, axis):
    groups = core_groups(lax.axis_size(axis))
    shares = lax.all_to_all(parts, axis, 0, 0, tiled=True, axis_index_groups=groups)
    return low(jnp.sum(shares.astype(jnp.float32), 0))


def spread_sum_permuted(parts, axis, after=()):
    n = lax.axis_size(axis)
    half = n // 2
    chip = lax.axis_index(axis) // 2
    total = lax.dynamic_index_in_dim(parts, chip, 0, keepdims=False).astype(jnp.float32)
    for away in range(1, half):
        piece = lax.dynamic_index_in_dim(parts, (chip + away) % half, 0, keepdims=False)
        moves = [(k, (k + 2 * away) % n) for k in range(n)]
        total = total + lax.ppermute(piece, axis, moves).astype(jnp.float32)
    return low(total)


def low(values):
    return values.astype(jnp.bfloat16)


def tables(positions):
    halves = jnp.arange(HD // 2, dtype=jnp.float32)
    frequency = THETA ** (-2.0 * halves / HD)
    angles = frequency[:, None] * positions.astype(jnp.float32)[None, :]
    return jnp.cos(angles), jnp.sin(angles)


def norm_forward(rows_in, gain):
    centre = rows_in - jnp.mean(rows_in, -1, keepdims=True)
    variance = jnp.mean(centre * centre, -1, keepdims=True)
    inverse = lax.rsqrt(variance + EPS)
    normed = centre * inverse
    return (normed * gain.astype(jnp.float32), normed, inverse)


def norm_backward(grad_rows, gain, normed, inverse):
    scaled = grad_rows * gain.astype(jnp.float32)
    grad_gain = jnp.sum(grad_rows * normed, 0)
    grad_rows_in = inverse * (
        scaled
        - jnp.mean(scaled, -1, keepdims=True)
        - normed * jnp.mean(scaled * normed, -1, keepdims=True)
    )
    return (grad_rows_in, grad_gain)


NN = (((1,), (0,)), ((), ()))
NT = (((1,), (1,)), ((), ()))
ROWS = 256
COLS = 256


def product(left, right, dims=NN):
    return lax.dot_general(left, right, dims, preferred_element_type=jnp.float32)


def project_kernel(
    seq_ref, w_ref, cos_ref, sin_ref, a_ref, qkv_ref, mean_ref, inverse_ref
):
    full_len, width = seq_ref.shape
    span = qkv_ref.shape[0] // 3
    group = span // HD
    half = HD // 2
    gain = w_ref[:, 512:640].astype(jnp.float32).T[3 * span - 512 : 3 * span - 511]
    w_turned = w_ref[:, : 3 * span].astype(jnp.float32).T.astype(jnp.bfloat16)
    for start in range(0, full_len, ROWS):
        rows = slice(start, start + ROWS)
        x = seq_ref[rows].astype(jnp.float32)
        mean = jnp.mean(x, -1, keepdims=True)
        centre = x - mean
        inverse = lax.rsqrt(jnp.mean(centre * centre, -1, keepdims=True) + EPS)
        mean_ref[rows] = mean
        inverse_ref[rows] = inverse
        a_low = (centre * inverse * gain).astype(jnp.bfloat16)
        a_ref[rows] = a_low
        joined = product(w_turned, a_low, NT)
        cosine = cos_ref[:, rows]
        sine = sin_ref[:, rows]
        for part in range(2 * group):
            one = joined[part * HD : part * HD + half]
            two = joined[part * HD + half : (part + 1) * HD]
            scale = HD ** (-0.5) if part < group else 1.0
            for at, value in (
                (0, one * cosine - two * sine),
                (half, two * cosine + one * sine),
            ):
                qkv_ref[part * HD + at : part * HD + at + half, rows] = (
                    value.astype(jnp.bfloat16) * scale
                ).astype(jnp.bfloat16)
        qkv_ref[2 * span :, rows] = joined[2 * span :].astype(jnp.bfloat16)


def forward_kernel(qkv_ref, bias_ref, keep_ref, out_ref, lse_ref, o_ref):
    span, full_len = o_ref.shape
    group = span // HD
    blk = out_ref.shape[2]
    for head in range(group):
        here = slice(head * HD, (head + 1) * HD)
        keys = qkv_ref[span + head * HD : span + (head + 1) * HD].T
        values = qkv_ref[2 * span + head * HD : 2 * span + (head + 1) * HD]
        for start in range(0, full_len, COLS):
            cols = slice(start, start + COLS)
            scores = product(keys, qkv_ref[here, cols]) + bias_ref[...]
            maximum = jnp.max(scores, 0, keepdims=True)
            exponent = jnp.exp(scores - maximum)
            total = jnp.sum(exponent, 0, keepdims=True)
            attended = product(values, exponent.astype(jnp.bfloat16))
            attended = attended * (keep_ref[:, cols] / total)
            o_ref[here, cols] = attended
            lse_ref[head : head + 1, cols] = maximum + jnp.log(total)
            for first in range(0, COLS, blk):
                out_ref[(start + first) // blk, here, :] = attended[
                    :, first : first + blk
                ].astype(jnp.bfloat16)


def backward_kernel(
    do_ref,
    qkv_ref,
    lse_ref,
    o_ref,
    cos_ref,
    sin_ref,
    bias_ref,
    keep_ref,
    seq_ref,
    mean_ref,
    inverse_ref,
    w_ref,
    g_ref,
    ga_ref,
    gain_ref,
    dk_ref,
    dv_ref,
):
    span, full_len = o_ref.shape
    group = span // HD
    half = HD // 2
    blk = do_ref.shape[2]
    for head in range(group):
        here = slice(head * HD, (head + 1) * HD)
        keys_turned = qkv_ref[span + head * HD : span + (head + 1) * HD]
        keys = keys_turned.T
        values = qkv_ref[2 * span + head * HD : 2 * span + (head + 1) * HD].T
        for start in range(0, full_len, COLS):
            cols = slice(start, start + COLS)
            query = qkv_ref[here, cols]
            grad_out = jnp.concatenate(
                [do_ref[(start + first) // blk, here, :] for first in range(0, COLS, blk)], 1
            )
            grad_out = grad_out.astype(jnp.float32) * keep_ref[:, cols]
            delta = jnp.sum(grad_out * o_ref[here, cols], 0, keepdims=True)
            grad_out = grad_out.astype(jnp.bfloat16)
            scores = product(keys, query) + bias_ref[...]
            probs = jnp.exp(scores - lse_ref[head : head + 1, cols])
            grad_scores = (probs * (product(values, grad_out) - delta)).astype(jnp.bfloat16)
            grad_value = product(grad_out, probs.astype(jnp.bfloat16), NT)
            grad_key = product(query, grad_scores, NT)
            if start == 0:
                dv_ref[...] = grad_value
                dk_ref[...] = grad_key
            else:
                dv_ref[...] += grad_value
                dk_ref[...] += grad_key
            grad_query = product(keys_turned, grad_scores) * HD ** (-0.5)
            cosine = cos_ref[:, cols]
            sine = sin_ref[:, cols]
            one, two = grad_query[:half], grad_query[half:]
            g_ref[head * HD : head * HD + half, cols] = (one * cosine + two * sine).astype(
                jnp.bfloat16
            )
            g_ref[head * HD + half : (head + 1) * HD, cols] = (
                two * cosine - one * sine
            ).astype(jnp.bfloat16)
        one, two = dk_ref[:half], dk_ref[half:]
        cosine = cos_ref[...]
        sine = sin_ref[...]
        low_at = span + head * HD
        g_ref[low_at : low_at + half] = (one * cosine + two * sine).astype(jnp.bfloat16)
        g_ref[low_at + half : low_at + HD] = (two * cosine - one * sine).astype(jnp.bfloat16)
        g_ref[2 * span + head * HD : 2 * span + (head + 1) * HD] = dv_ref[...].astype(
            jnp.bfloat16
        )
    for start in range(0, full_len, ROWS):
        rows = slice(start, start + ROWS)
        grad_a = product(g_ref[:, rows].T, w_ref[:, : 3 * span], NT)
        normed = (seq_ref[rows].astype(jnp.float32) - mean_ref[rows]) * inverse_ref[rows]
        summed = jnp.sum(grad_a * normed, 0, keepdims=True)
        gain_ref[...] = summed if start == 0 else gain_ref[...] + summed
        for first in range(0, ROWS, blk):
            ga_ref[(start + first) // blk] = grad_a[first : first + blk].astype(jnp.bfloat16)


def mlp_kernel(
    core_ref,
    tok_ref,
    att_ref,
    cot_ref,
    gain_ref,
    mine_ref,
    other_ref,
    win_ref,
    do_ref,
    gm_ref,
    mixed_ref,
    b_ref,
    hid_ref,
    gg_ref,
    grad_gain_ref,
    wdown_ref,
    wout_ref,
):
    pairs, height, _ = mine_ref.shape
    depth = wout_ref.shape[0] // (2 * pairs)
    down_rows = height - depth
    even = core_ref[0] == 0
    for pair in range(pairs):
        mine = mine_ref[pair].astype(jnp.float32)
        other = other_ref[pair].astype(jnp.float32)
        first = jnp.where(even, mine, other)
        second = jnp.where(even, other, mine)
        wout_ref[2 * pair * depth : 2 * (pair + 1) * depth] = jnp.concatenate(
            [first[:depth], second[:depth]], 0
        ).astype(jnp.bfloat16)
        wdown_ref[2 * pair * down_rows : 2 * (pair + 1) * down_rows] = jnp.concatenate(
            [first[depth:], second[depth:]], 0
        ).astype(jnp.bfloat16)
    seqs, local_len, width = tok_ref.shape
    spread = do_ref.shape[0] // seqs
    span = do_ref.shape[1]
    hidden = hid_ref.shape[1]
    resid = jnp.concatenate([tok_ref[k] for k in range(seqs)], 0).astype(jnp.float32)
    att = jnp.concatenate([att_ref[k].T for k in range(seqs)], 0)
    cot = jnp.concatenate([cot_ref[k] for k in range(seqs)], 0)
    mixed = resid + product(att, wout_ref[...])
    mixed_ref[...] = mixed
    centre = mixed - jnp.mean(mixed, -1, keepdims=True)
    inverse = lax.rsqrt(jnp.mean(centre * centre, -1, keepdims=True) + EPS)
    normed = centre * inverse
    b_low = (normed * gain_ref[...]).astype(jnp.bfloat16)
    b_ref[...] = b_low
    for first in range(0, hidden, hidden // 3):
        here = slice(first, first + hidden // 3)
        there = slice(hidden + first, hidden + first + hidden // 3)
        gate_in = product(b_low, win_ref[:, here])
        up_half = product(b_low, win_ref[:, there])
        grad_hid = product(cot, wdown_ref[here], NT)
        normal_cdf = 0.5 * (1.0 + lax.erf(gate_in * INV_ROOT_TWO))
        gelu_out = gate_in * normal_cdf
        hid_ref[:, here] = (gelu_out * up_half).astype(jnp.bfloat16)
        normal_pdf = jnp.exp(-0.5 * gate_in * gate_in) * INV_ROOT_TWO_PI
        gg_ref[:, here] = (grad_hid * up_half * (normal_cdf + gate_in * normal_pdf)).astype(
            jnp.bfloat16
        )
        gg_ref[:, there] = (grad_hid * gelu_out).astype(jnp.bfloat16)
    grad_b = product(gg_ref[...], win_ref[...], NT)
    grad_gain_ref[...] = jnp.sum(grad_b * normed, 0, keepdims=True)
    scaled = grad_b * gain_ref[...]
    grad_mixed = cot.astype(jnp.float32) + inverse * (
        scaled
        - jnp.mean(scaled, -1, keepdims=True)
        - normed * jnp.mean(scaled * normed, -1, keepdims=True)
    )
    gm_ref[...] = grad_mixed
    grad_heads = product(wout_ref[...], grad_mixed.astype(jnp.bfloat16), NT).astype(jnp.bfloat16)
    for seq in range(seqs):
        for part in range(spread):
            do_ref[seq * spread + part] = grad_heads[
                part * span : (part + 1) * span, seq * local_len : (seq + 1) * local_len
            ]


def mlp_weights_kernel(
    core_ref,
    att_ref,
    cot_ref,
    gm_ref,
    b_ref,
    hid_ref,
    gg_ref,
    away_ref,
    away_extra_ref,
    kept_ref,
    kept_extra_ref,
    turned,
    tall,
):
    seqs, width, _ = att_ref.shape
    ctx, pairs, chunk, _ = kept_ref.shape
    count = gg_ref.shape[1] // width
    depth = width // (2 * pairs)
    down_rows = hid_ref.shape[1] // (2 * pairs)
    split = ctx * chunk - (count + 1) * depth
    cot = jnp.concatenate([cot_ref[k] for k in range(seqs)], 0)
    grad_att = gm_ref[...].astype(jnp.bfloat16)
    turned[:width] = b_ref[...].astype(jnp.float32).T
    turned[width : 2 * width] = jnp.concatenate(
        [att_ref[k] for k in range(seqs)], 1
    ).astype(jnp.float32)
    turned[2 * width :] = hid_ref[...].astype(jnp.float32).T
    core = core_ref[0]
    for which, part_ref, extra_ref in (
        (1 - core, away_ref, away_extra_ref),
        (core, kept_ref, kept_extra_ref),
    ):

        def chosen(first, height):
            return jnp.concatenate(
                [
                    turned[pl.ds(pl.multiple_of(first + (2 * k + which) * height, 8), height)]
                    for k in range(pairs)
                ],
                0,
            ).astype(jnp.bfloat16)

        grad_up = product(chosen(width, depth), grad_att)
        tall[...] = product(chosen(2 * width, down_rows), cot)
        grad_in = product(chosen(0, depth), gg_ref[...])
        for pair in range(pairs):
            wide = slice(pair * depth, (pair + 1) * depth)
            rows = jnp.concatenate(
                [grad_in[wide, k * width : (k + 1) * width] for k in range(count)]
                + [grad_up[wide], tall[pair * down_rows : pair * down_rows + split]],
                0,
            ).astype(jnp.bfloat16)
            for part in range(ctx):
                part_ref[part, pair] = rows[part * chunk : (part + 1) * chunk]
            extra_ref[pair] = tall[pair * down_rows + split : (pair + 1) * down_rows]


def layer_out_kernel(mixed_ref, hid_ref, wdown_ref, out_ref):
    local_len = out_ref.shape[1]
    result = mixed_ref[...] + product(hid_ref[...], wdown_ref[...])
    for seq in range(out_ref.shape[0]):
        out_ref[seq] = result[seq * local_len : (seq + 1) * local_len].astype(jnp.bfloat16)


def qkv_weights_kernel(
    core_ref,
    a_ref,
    g_ref,
    gain_one_ref,
    gain_two_ref,
    kept_extra_ref,
    away_extra_ref,
    kept_ref,
    away_ref,
    w_ref,
):
    pairs, depth, width = kept_ref.shape
    span3 = g_ref.shape[0]
    used = width - 128
    w_ref[:, :span3] = product(a_ref[...].T, g_ref[...], NT)
    lane = used - 128
    gains = jnp.concatenate(
        [
            jnp.zeros((span3 - lane, width), jnp.float32),
            gain_one_ref[...],
            gain_two_ref[...],
            jnp.zeros((used - span3 - 2, width), jnp.float32),
        ],
        0,
    ).T
    w_ref[:, span3:] = gains[:, span3 - lane :]
    core = core_ref[0]
    for pair in range(pairs):
        for ref, extra_ref, which in (
            (kept_ref, kept_extra_ref, core),
            (away_ref, away_extra_ref, 1 - core),
        ):
            rows = pl.ds(pl.multiple_of((2 * pair + which) * depth, 8), depth)
            extra = extra_ref[pair]
            ref[pair] = jnp.concatenate(
                [
                    w_ref[rows],
                    jnp.concatenate(
                        [extra[:, k * 128 : (k + 1) * 128] for k in range(width // 128)], 0
                    ),
                ],
                1,
            ).astype(jnp.bfloat16)


def first_kernel(group_ref, w_ref, gains_ref, out_ref):
    depth, used = out_ref.shape
    spread = 4
    span = w_ref.shape[1] // (3 * spread)
    own_group = group_ref[0]
    gains = gains_ref[...]

    for which in range(spread):

        @pl.when(own_group == which)
        def _():
            picked = [
                w_ref[
                    :, (k * spread + which) * span : (k * spread + which + 1) * span
                ].astype(jnp.float32)
                for k in range(3)
            ]
            out_ref[...] = jnp.concatenate([*picked, gains], 1).astype(jnp.bfloat16)


def finish_kernel(
    ends_ref, gain_one_ref, qkv_ref, wout_ref, gain_two_ref, win_ref, wdown_ref
):
    ctx, _, width = ends_ref.shape
    depth = qkv_ref.shape[0]
    down_rows = wdown_ref.shape[0]
    count = win_ref.shape[1] // width
    spread = ctx // 2
    span = width // spread
    f32 = jnp.float32
    last = [ends_ref[k, :depth].astype(f32) for k in range(ctx)]
    for group in range(spread):
        both = last[group] + last[group + spread]
        for part in range(3):
            qkv_ref[:, part * width + group * span : part * width + (group + 1) * span] = both[
                :, part * span : (part + 1) * span
            ]
    total = last[0]
    for k in range(1, ctx):
        total = total + last[k]
    lane = 3 * span // 128 * 128
    gains = total[:, lane : lane + 128].T
    gain_one_ref[...] = gains[3 * span - lane : 3 * span - lane + 1]
    gain_two_ref[...] = gains[3 * span - lane + 1 : 3 * span - lane + 2]
    main = jnp.concatenate([ends_ref[k, depth:].astype(f32) for k in range(ctx)], 0)
    for k in range(count):
        win_ref[:, k * width : (k + 1) * width] = main[k * depth : (k + 1) * depth]
    wout_ref[...] = main[count * depth : (count + 1) * depth]
    split = main.shape[0] - (count + 1) * depth
    extra = down_rows - split
    wdown_ref[:split] = main[(count + 1) * depth :]
    wdown_ref[split:] = jnp.concatenate(
        [total[k * extra : (k + 1) * extra, width - 128 :] for k in range(width // 128)], 1
    )


def on_device(kernel, outs, args, micros, scratch=(), scalars=0, after=(), name=None):
    space = pl.BlockSpec(memory_space=pltpu.VMEM)
    scalar = pl.BlockSpec(memory_space=pltpu.SMEM)
    given = len(args)

    def ordered(*refs):
        kernel(*refs[:given], *refs[given + len(after) :])

    return pl.pallas_call(
        ordered,
        out_shape=[jax.ShapeDtypeStruct(shape, dtype) for shape, dtype in outs],
        in_specs=[scalar] * scalars
        + [space] * (given - scalars)
        + [pl.BlockSpec(memory_space=pl.ANY)] * len(after),
        out_specs=[space] * len(outs),
        scratch_shapes=list(scratch),
        compiler_params=pltpu.CompilerParams(vmem_limit_bytes=24 * 1024 * 1024),
        cost_estimate=pl.CostEstimate(
            flops=int(micros * 2e10), bytes_accessed=int(micros * 4e7), transcendentals=0
        ),
        name=name,
    )(*args, *after)


def sum_kernel(left_ref, right_ref, out_ref):
    for k in range(out_ref.shape[0]):
        out_ref[k] = (left_ref[k].astype(jnp.float32) + right_ref[k].astype(jnp.float32)).astype(
            jnp.bfloat16
        )


def spread_kernel(tokens_ref, out_ref):
    copies = out_ref.shape[0] // tokens_ref.shape[0]
    for k in range(out_ref.shape[0]):
        out_ref[k] = tokens_ref[k // copies]


def pass_kernel(in_ref, out_ref):
    out_ref[...] = in_ref[...]


def interleave_kernel(late_ref, held_ref, came_ref, out_ref):
    late = late_ref[0]
    for k in range(held_ref.shape[0]):
        out_ref[k, late] = held_ref[k]
        out_ref[k, 1 - late] = came_ref[k]


def stack_kernel(upper_ref, lower_ref, out_ref):
    rows = upper_ref.shape[0]
    out_ref[:rows] = upper_ref[...]
    out_ref[rows:] = lower_ref[...]


def body(tokens, lengths, deal, gain_attn, w_qkv, w_out, gain_mlp, w_in, w_down, cotangent):
    seqs, local_len, width = tokens.shape
    ctx = lax.axis_size("ctx")
    fsdp = lax.axis_size("fsdp")
    spread = ctx // seqs
    group = HEADS // spread
    span = group * HD
    full_len = local_len * ctx
    rows = seqs * local_len
    context = lax.axis_index("ctx")
    own_seq = context // spread
    own_group = context % spread
    depth = w_qkv.shape[0]
    hidden = w_in.shape[1] // 2
    down_rows = w_down.shape[0]
    f32 = jnp.float32

    offsets = jnp.arange(BLK, dtype=jnp.int32)
    all_pos = (deal[:, None] * BLK + offsets[None, :]).reshape(full_len)
    length = lax.dynamic_slice_in_dim(lengths, own_seq, 1)[0]
    all_keep = all_pos < length

    used = 3 * span + 64
    gains_wide = jnp.pad(
        jnp.stack([gain_attn, gain_mlp], 1).astype(f32), ((0, 0), (0, used - 3 * span - 2))
    )
    first = on_device(
        first_kernel,
        [((depth, used), jnp.bfloat16)],
        (own_group.astype(jnp.int32)[None], w_qkv, gains_wide),
        0.05,
        scalars=1,
        name="first_pack",
    )[0]
    steps = [fsdp >> (k + 1) for k in range(fsdp.bit_length() - 1)]
    held = first[None]
    held = doubled(held, "fsdp", steps[0])
    early = held
    for bit in steps[1:-1]:
        held = doubled(held, "fsdp", bit)
    first_all = doubled(held, "fsdp", steps[-1]).reshape(fsdp * depth, used)
    win_all = lax.all_gather(w_in, "fsdp", axis=0, tiled=True)
    to_send = on_device(
        spread_kernel,
        [((ctx, local_len, width), jnp.bfloat16)],
        (tokens,),
        0.02,
        after=(early,),
        name="spread_tokens",
    )[0]
    sequence = lax.all_to_all(to_send, "ctx", 0, 0, tiled=True)
    stacked = on_device(
        stack_kernel,
        [((depth + down_rows, width), jnp.bfloat16)],
        (w_out, w_down),
        0.02,
        after=(held,),
        name="stack_rest",
    )[0]
    gain_one = first_all[:, 3 * span]
    gain_two = first_all[:, 3 * span + 1]

    cosine, sine = tables(all_pos)
    bias = jnp.where(all_keep, 0.0, NEGATIVE).astype(f32)[:, None]
    keep_row = all_keep.astype(f32)[None, :]
    sequence = sequence.reshape(full_len, width)
    a_low, qkv, mean, inverse = on_device(
        project_kernel,
        [
            ((full_len, width), jnp.bfloat16),
            ((3 * span, full_len), jnp.bfloat16),
            ((full_len, 1), f32),
            ((full_len, 1), f32),
        ],
        (sequence, first_all, cosine, sine),
        0.3,
        name="project",
    )
    rest = doubled(stacked[None], "fsdp", steps[0], after=(qkv,))
    attended, log_total, unrounded = on_device(
        forward_kernel,
        [
            ((ctx, span, local_len), jnp.bfloat16),
            ((8, full_len), f32),
            ((span, full_len), f32),
        ],
        (qkv, bias, keep_row),
        0.8,
        after=(rest,),
        name="attention_forward",
    )
    rest = doubled(rest, "fsdp", steps[1], after=(attended,))
    att_back = lax.all_to_all(attended, "ctx", 0, 0, tiled=True)
    rest = doubled(rest, "fsdp", steps[2], after=(att_back,))
    rest_other = lax.ppermute(rest, "fsdp", core_pairs(fsdp))
    att_turned = att_back.reshape(seqs, width, local_len)

    resid = tokens.astype(f32).reshape(rows, width)
    count = w_in.shape[1] // width
    main_rows = ((count + 1) * depth + down_rows) // (8 * ctx) * 8 * ctx
    chunk = main_rows // ctx
    split = main_rows - (count + 1) * depth
    extra = down_rows - split
    pairs = fsdp // 2
    core = (lax.axis_index("fsdp") % 2).astype(jnp.int32)[None]
    (
        grad_heads,
        grad_mixed,
        mixed,
        b_low,
        hid_low,
        grad_gate_up,
        grad_gain_two,
        wdown_all,
    ) = on_device(
        mlp_kernel,
        [
            ((ctx, span, local_len), jnp.bfloat16),
            ((rows, width), f32),
            ((rows, width), f32),
            ((rows, width), jnp.bfloat16),
            ((rows, hidden), jnp.bfloat16),
            ((rows, 2 * hidden), jnp.bfloat16),
            ((1, width), f32),
            ((hidden, width), jnp.bfloat16),
        ],
        (
            core,
            tokens,
            att_turned,
            cotangent,
            gain_two.astype(f32)[None, :],
            rest,
            rest_other,
            win_all,
        ),
        0.5,
        [pltpu.VMEM((fsdp * depth, width), jnp.bfloat16)],
        scalars=1,
        name="mlp",
    )
    half_outs = [
        ((ctx, pairs, chunk, width), jnp.bfloat16),
        ((pairs, extra, width), f32),
    ]
    main_away, away_extra, main_kept, kept_extra = on_device(
        mlp_weights_kernel,
        half_outs * 2,
        (core, att_turned, cotangent, grad_mixed, b_low, hid_low, grad_gate_up),
        0.05,
        [
            pltpu.VMEM((2 * width + hidden, rows), f32),
            pltpu.VMEM((hidden // 2, width), f32),
        ],
        scalars=1,
        name="mlp_weights",
    )
    main_pair = core_sum(main_kept, main_away, "fsdp", 0.02, name="sum_cores")
    main_part = lax.psum_scatter(
        main_pair.reshape(-1, chunk, width), "ctx", scatter_dimension=0, tiled=True
    )

    all_grad = lax.all_to_all(grad_heads, "ctx", 0, 0, tiled=True)
    grad_qkv, grad_a_part, grad_gain_one = on_device(
        backward_kernel,
        [
            ((3 * span, full_len), jnp.bfloat16),
            ((ctx, local_len, width), jnp.bfloat16),
            ((1, width), f32),
        ],
        (
            all_grad,
            qkv,
            log_total,
            unrounded,
            cosine,
            sine,
            bias,
            keep_row,
            sequence,
            mean,
            inverse,
            first_all,
        ),
        12,
        [pltpu.VMEM((HD, full_len), f32)] * 2,
        after=(main_pair,),
        name="attention_backward",
    )
    grad_a_parts = lax.all_to_all(grad_a_part, "ctx", 0, 0, tiled=True)
    output = on_device(
        layer_out_kernel,
        [(tokens.shape, jnp.bfloat16)],
        (mixed, hid_low, wdown_all),
        0.05,
        after=(grad_a_part,),
        name="layer_out",
    )[0]
    last_kept, last_away = on_device(
        qkv_weights_kernel,
        [((pairs, depth, width), jnp.bfloat16)] * 2,
        (core, a_low, grad_qkv, grad_gain_one, grad_gain_two, kept_extra, away_extra),
        0.1,
        [pltpu.VMEM((width, used), f32)],
        scalars=1,
        name="qkv_weights",
    )
    last = core_sum(
        last_kept, last_away, "fsdp", 0.05, name="sum_cores_last"
    )
    grad_a = jnp.sum(
        grad_a_parts.reshape(seqs, spread, local_len, width).astype(f32), 1
    ).reshape(rows, width)
    _, normed_one, inverse_one = norm_forward(resid, gain_one)
    grad_norm_one, _ = norm_backward(grad_a, gain_one, normed_one, inverse_one)
    grad_input = grad_mixed + grad_norm_one

    last = spread_sum_permuted(last, "fsdp")
    main_part = on_device(
        pass_kernel,
        [(main_part.shape, jnp.bfloat16)],
        (main_part,),
        0.02,
        after=(grad_a_parts, last),
        name="after_exchange",
    )[0]
    main_part = spread_sum(main_part, "fsdp")
    share = jnp.concatenate([last, main_part], 0)
    ends = gather_by_exchange(share, "ctx", ctx)
    finished = on_device(
        finish_kernel,
        [
            ((1, depth), f32),
            (w_qkv.shape, f32),
            (w_out.shape, f32),
            ((1, depth), f32),
            (w_in.shape, f32),
            (w_down.shape, f32),
        ],
        (ends,),
        3,
        name="finish",
    )
    return (
        output,
        grad_input.reshape(tokens.shape),
        finished[0].reshape(depth),
        finished[1],
        finished[2],
        finished[3].reshape(depth),
        finished[4],
        finished[5],
    )


def solution(mesh):
    placed = (
        P("fsdp", "ctx", None),
        P("fsdp"),
        P(),
        P("fsdp"),
        P("fsdp", None),
        P("fsdp", None),
        P("fsdp"),
        P("fsdp", None),
        P("fsdp", None),
        P("fsdp", "ctx", None),
    )
    return jax.shard_map(
        body,
        mesh=mesh,
        in_specs=placed,
        out_specs=(
            P("fsdp", "ctx", None),
            P("fsdp", "ctx", None),
            P("fsdp"),
            P("fsdp", None),
            P("fsdp", None),
            P("fsdp"),
            P("fsdp", None),
            P("fsdp", None),
        ),
        check_vma=False,
    )
```

```python
import math

import jax
import jax.numpy as jnp
from jax import lax
from jax.experimental import pallas as pl
from jax.experimental.pallas import tpu as pltpu
from jax.sharding import PartitionSpec as P

HEADS = 12
HD = 64
BLK = 128


EPS = 1e-05
THETA = 160000.0
NEGATIVE = -1e30
INV_ROOT_TWO = 0.7071067811865476
INV_ROOT_TWO_PI = 0.3989422804014327


def core_pairs(n):
    return [(k, k ^ 1) for k in range(n)]


def core_groups(n):
    return [list(range(first, n, 2)) for first in range(2)]


def doubled(held, axis, bit, after=()):
    n = lax.axis_size(axis)
    index = lax.axis_index(axis)
    came = lax.ppermute(held, axis, [(k, k ^ bit) for k in range(n)])
    if after:
        held = on_device(
            interleave_kernel,
            [((held.shape[0], 2, *held.shape[1:]), held.dtype)],
            ((index // bit % 2).astype(jnp.int32)[None], held, came),
            0.02,
            scalars=1,
            after=after,
            name="interleave",
        )[0]
    else:
        first = (index & bit) == 0
        held = jnp.where(first, jnp.stack([held, came], 1), jnp.stack([came, held], 1))
    return held.reshape(-1, *held.shape[2:])


def core_sum(kept, away, axis, micros, after=(), name=None):
    came = lax.ppermute(away, axis, core_pairs(lax.axis_size(axis)))
    return on_device(
        sum_kernel, [(kept.shape, jnp.bfloat16)], (kept, came), micros, after=after, name=name
    )[0]


def spread_sum_permuted(parts, axis, after=()):
    n = lax.axis_size(axis)
    half = n // 2
    chip = lax.axis_index(axis) // 2
    total = lax.dynamic_index_in_dim(parts, chip, 0, keepdims=False).astype(jnp.float32)
    for away in range(1, half):
        piece = lax.dynamic_index_in_dim(parts, (chip + away) % half, 0, keepdims=False)
        moves = [(k, (k + 2 * away) % n) for k in range(n)]
        total = total + lax.ppermute(piece, axis, moves).astype(jnp.float32)
    return low(total)


def low(values):
    return values.astype(jnp.bfloat16)


def tables(positions):
    halves = jnp.arange(HD // 2, dtype=jnp.float32)
    frequency = THETA ** (-2.0 * halves / HD)
    angles = frequency[:, None] * positions.astype(jnp.float32)[None, :]
    return jnp.cos(angles), jnp.sin(angles)


def norm_forward(rows_in, gain):
    centre = rows_in - jnp.mean(rows_in, -1, keepdims=True)
    variance = jnp.mean(centre * centre, -1, keepdims=True)
    inverse = lax.rsqrt(variance + EPS)
    normed = centre * inverse
    return (normed * gain.astype(jnp.float32), normed, inverse)


def norm_backward(grad_rows, gain, normed, inverse):
    scaled = grad_rows * gain.astype(jnp.float32)
    grad_gain = jnp.sum(grad_rows * normed, 0)
    grad_rows_in = inverse * (
        scaled
        - jnp.mean(scaled, -1, keepdims=True)
        - normed * jnp.mean(scaled * normed, -1, keepdims=True)
    )
    return (grad_rows_in, grad_gain)


NN = (((1,), (0,)), ((), ()))
NT = (((1,), (1,)), ((), ()))
ROWS = 256
COLS = 256


def product(left, right, dims=NN):
    return lax.dot_general(left, right, dims, preferred_element_type=jnp.float32)


def project_kernel(
    seq_ref, w_ref, cos_ref, sin_ref, a_ref, qkv_ref, mean_ref, inverse_ref
):
    full_len, width = seq_ref.shape
    span = qkv_ref.shape[0] // 3
    group = span // HD
    half = HD // 2
    gain = w_ref[:, 512:640].astype(jnp.float32).T[3 * span - 512 : 3 * span - 511]
    w_turned = w_ref[:, : 3 * span].astype(jnp.float32).T.astype(jnp.bfloat16)
    for start in range(0, full_len, ROWS):
        rows = slice(start, start + ROWS)
        x = seq_ref[rows].astype(jnp.float32)
        mean = jnp.mean(x, -1, keepdims=True)
        centre = x - mean
        inverse = lax.rsqrt(jnp.mean(centre * centre, -1, keepdims=True) + EPS)
        mean_ref[rows] = mean
        inverse_ref[rows] = inverse
        a_low = (centre * inverse * gain).astype(jnp.bfloat16)
        a_ref[rows] = a_low
        joined = product(w_turned, a_low, NT)
        cosine = cos_ref[:, rows]
        sine = sin_ref[:, rows]
        for part in range(2 * group):
            one = joined[part * HD : part * HD + half]
            two = joined[part * HD + half : (part + 1) * HD]
            scale = HD ** (-0.5) if part < group else 1.0
            for at, value in (
                (0, one * cosine - two * sine),
                (half, two * cosine + one * sine),
            ):
                qkv_ref[part * HD + at : part * HD + at + half, rows] = (
                    value.astype(jnp.bfloat16) * scale
                ).astype(jnp.bfloat16)
        qkv_ref[2 * span :, rows] = joined[2 * span :].astype(jnp.bfloat16)


def forward_kernel(qkv_ref, bias_ref, keep_ref, out_ref, lse_ref, o_ref):
    span, full_len = o_ref.shape
    group = span // HD
    blk = out_ref.shape[2]
    for head in range(group):
        here = slice(head * HD, (head + 1) * HD)
        keys = qkv_ref[span + head * HD : span + (head + 1) * HD].T
        values = qkv_ref[2 * span + head * HD : 2 * span + (head + 1) * HD]
        for start in range(0, full_len, COLS):
            cols = slice(start, start + COLS)
            scores = product(keys, qkv_ref[here, cols]) + bias_ref[...]
            maximum = jnp.max(scores, 0, keepdims=True)
            exponent = jnp.exp(scores - maximum)
            total = jnp.sum(exponent, 0, keepdims=True)
            attended = product(values, exponent.astype(jnp.bfloat16))
            attended = attended * (keep_ref[:, cols] / total)
            o_ref[here, cols] = attended
            lse_ref[head : head + 1, cols] = maximum + jnp.log(total)
            for first in range(0, COLS, blk):
                out_ref[(start + first) // blk, here, :] = attended[
                    :, first : first + blk
                ].astype(jnp.bfloat16)


def backward_kernel(
    do_ref,
    qkv_ref,
    lse_ref,
    o_ref,
    cos_ref,
    sin_ref,
    bias_ref,
    keep_ref,
    seq_ref,
    mean_ref,
    inverse_ref,
    w_ref,
    g_ref,
    ga_ref,
    gain_ref,
    dk_ref,
    dv_ref,
    seq_held,
    w_held,
    sems,
):
    copies = [
        pltpu.make_async_copy(seq_ref, seq_held, sems.at[0]),
        pltpu.make_async_copy(w_ref, w_held, sems.at[1]),
    ]
    for copy in copies:
        copy.start()
    span, full_len = o_ref.shape
    group = span // HD
    half = HD // 2
    blk = do_ref.shape[2]
    for head in range(group):
        here = slice(head * HD, (head + 1) * HD)
        keys_turned = qkv_ref[span + head * HD : span + (head + 1) * HD]
        keys = keys_turned.T
        values = qkv_ref[2 * span + head * HD : 2 * span + (head + 1) * HD].T
        for start in range(0, full_len, COLS):
            cols = slice(start, start + COLS)
            query = qkv_ref[here, cols]
            grad_out = jnp.concatenate(
                [do_ref[(start + first) // blk, here, :] for first in range(0, COLS, blk)], 1
            )
            grad_out = grad_out.astype(jnp.float32) * keep_ref[:, cols]
            delta = jnp.sum(grad_out * o_ref[here, cols], 0, keepdims=True)
            grad_out = grad_out.astype(jnp.bfloat16)
            scores = product(keys, query) + bias_ref[...]
            probs = jnp.exp(scores - lse_ref[head : head + 1, cols])
            grad_scores = (probs * (product(values, grad_out) - delta)).astype(jnp.bfloat16)
            grad_value = product(grad_out, probs.astype(jnp.bfloat16), NT)
            grad_key = product(query, grad_scores, NT)
            if start == 0:
                dv_ref[...] = grad_value
                dk_ref[...] = grad_key
            else:
                dv_ref[...] += grad_value
                dk_ref[...] += grad_key
            grad_query = product(keys_turned, grad_scores) * HD ** (-0.5)
            cosine = cos_ref[:, cols]
            sine = sin_ref[:, cols]
            one, two = grad_query[:half], grad_query[half:]
            g_ref[head * HD : head * HD + half, cols] = (one * cosine + two * sine).astype(
                jnp.bfloat16
            )
            g_ref[head * HD + half : (head + 1) * HD, cols] = (
                two * cosine - one * sine
            ).astype(jnp.bfloat16)
        one, two = dk_ref[:half], dk_ref[half:]
        cosine = cos_ref[...]
        sine = sin_ref[...]
        low_at = span + head * HD
        g_ref[low_at : low_at + half] = (one * cosine + two * sine).astype(jnp.bfloat16)
        g_ref[low_at + half : low_at + HD] = (two * cosine - one * sine).astype(jnp.bfloat16)
        g_ref[2 * span + head * HD : 2 * span + (head + 1) * HD] = dv_ref[...].astype(
            jnp.bfloat16
        )
    for copy in copies:
        copy.wait()
    for start in range(0, full_len, ROWS):
        rows = slice(start, start + ROWS)
        grad_a = product(g_ref[:, rows].T, w_held[:, : 3 * span], NT)
        normed = (seq_held[rows].astype(jnp.float32) - mean_ref[rows]) * inverse_ref[rows]
        summed = jnp.sum(grad_a * normed, 0, keepdims=True)
        gain_ref[...] = summed if start == 0 else gain_ref[...] + summed
        for first in range(0, ROWS, blk):
            ga_ref[(start + first) // blk] = grad_a[first : first + blk].astype(jnp.bfloat16)


def mlp_kernel(
    core_ref,
    tok_ref,
    att_ref,
    cot_ref,
    gain_ref,
    mine_ref,
    other_ref,
    win_ref,
    do_ref,
    gm_ref,
    mixed_ref,
    b_ref,
    hid_ref,
    gg_ref,
    grad_gain_ref,
    wdown_ref,
    wout_ref,
):
    pairs, height, _ = mine_ref.shape
    depth = wout_ref.shape[0] // (2 * pairs)
    down_rows = height - depth
    even = core_ref[0] == 0
    for pair in range(pairs):
        mine = mine_ref[pair].astype(jnp.float32)
        other = other_ref[pair].astype(jnp.float32)
        first = jnp.where(even, mine, other)
        second = jnp.where(even, other, mine)
        wout_ref[2 * pair * depth : 2 * (pair + 1) * depth] = jnp.concatenate(
            [first[:depth], second[:depth]], 0
        ).astype(jnp.bfloat16)
        wdown_ref[2 * pair * down_rows : 2 * (pair + 1) * down_rows] = jnp.concatenate(
            [first[depth:], second[depth:]], 0
        ).astype(jnp.bfloat16)
    seqs, local_len, width = tok_ref.shape
    spread = do_ref.shape[0] // seqs
    span = do_ref.shape[1]
    hidden = hid_ref.shape[1]
    resid = jnp.concatenate([tok_ref[k] for k in range(seqs)], 0).astype(jnp.float32)
    att = jnp.concatenate([att_ref[k].T for k in range(seqs)], 0)
    cot = jnp.concatenate([cot_ref[k] for k in range(seqs)], 0)
    mixed = resid + product(att, wout_ref[...])
    mixed_ref[...] = mixed
    centre = mixed - jnp.mean(mixed, -1, keepdims=True)
    inverse = lax.rsqrt(jnp.mean(centre * centre, -1, keepdims=True) + EPS)
    normed = centre * inverse
    b_low = (normed * gain_ref[...]).astype(jnp.bfloat16)
    b_ref[...] = b_low
    for first in range(0, hidden, hidden // 3):
        here = slice(first, first + hidden // 3)
        there = slice(hidden + first, hidden + first + hidden // 3)
        gate_in = product(b_low, win_ref[:, here])
        up_half = product(b_low, win_ref[:, there])
        grad_hid = product(cot, wdown_ref[here], NT)
        normal_cdf = 0.5 * (1.0 + lax.erf(gate_in * INV_ROOT_TWO))
        gelu_out = gate_in * normal_cdf
        hid_ref[:, here] = (gelu_out * up_half).astype(jnp.bfloat16)
        normal_pdf = jnp.exp(-0.5 * gate_in * gate_in) * INV_ROOT_TWO_PI
        gg_ref[:, here] = (grad_hid * up_half * (normal_cdf + gate_in * normal_pdf)).astype(
            jnp.bfloat16
        )
        gg_ref[:, there] = (grad_hid * gelu_out).astype(jnp.bfloat16)
    grad_b = product(gg_ref[...], win_ref[...], NT)
    grad_gain_ref[...] = jnp.sum(grad_b * normed, 0, keepdims=True)
    scaled = grad_b * gain_ref[...]
    grad_mixed = cot.astype(jnp.float32) + inverse * (
        scaled
        - jnp.mean(scaled, -1, keepdims=True)
        - normed * jnp.mean(scaled * normed, -1, keepdims=True)
    )
    gm_ref[...] = grad_mixed
    grad_heads = product(wout_ref[...], grad_mixed.astype(jnp.bfloat16), NT).astype(jnp.bfloat16)
    for seq in range(seqs):
        for part in range(spread):
            do_ref[seq * spread + part] = grad_heads[
                part * span : (part + 1) * span, seq * local_len : (seq + 1) * local_len
            ]


def mlp_weights_kernel(
    core_ref,
    att_ref,
    cot_ref,
    gm_ref,
    b_ref,
    hid_ref,
    gg_ref,
    away_ref,
    away_extra_ref,
    kept_ref,
    kept_extra_ref,
    turned,
    tall,
):
    seqs, width, _ = att_ref.shape
    ctx, pairs, chunk, _ = kept_ref.shape
    count = gg_ref.shape[1] // width
    depth = width // (2 * pairs)
    down_rows = hid_ref.shape[1] // (2 * pairs)
    split = ctx * chunk - (count + 1) * depth
    cot = jnp.concatenate([cot_ref[k] for k in range(seqs)], 0)
    grad_att = gm_ref[...].astype(jnp.bfloat16)
    turned[:width] = b_ref[...].astype(jnp.float32).T
    turned[width : 2 * width] = jnp.concatenate(
        [att_ref[k] for k in range(seqs)], 1
    ).astype(jnp.float32)
    turned[2 * width :] = hid_ref[...].astype(jnp.float32).T
    core = core_ref[0]
    for which, part_ref, extra_ref in (
        (1 - core, away_ref, away_extra_ref),
        (core, kept_ref, kept_extra_ref),
    ):

        def chosen(first, height):
            return jnp.concatenate(
                [
                    turned[pl.ds(pl.multiple_of(first + (2 * k + which) * height, 8), height)]
                    for k in range(pairs)
                ],
                0,
            ).astype(jnp.bfloat16)

        grad_up = product(chosen(width, depth), grad_att)
        tall[...] = product(chosen(2 * width, down_rows), cot)
        grad_in = product(chosen(0, depth), gg_ref[...])
        for pair in range(pairs):
            wide = slice(pair * depth, (pair + 1) * depth)
            rows = jnp.concatenate(
                [grad_in[wide, k * width : (k + 1) * width] for k in range(count)]
                + [grad_up[wide], tall[pair * down_rows : pair * down_rows + split]],
                0,
            ).astype(jnp.bfloat16)
            for part in range(ctx):
                part_ref[part, pair] = rows[part * chunk : (part + 1) * chunk]
            extra_ref[pair] = tall[pair * down_rows + split : (pair + 1) * down_rows]


def layer_out_kernel(mixed_ref, hid_ref, wdown_ref, out_ref):
    local_len = out_ref.shape[1]
    result = mixed_ref[...] + product(hid_ref[...], wdown_ref[...])
    for seq in range(out_ref.shape[0]):
        out_ref[seq] = result[seq * local_len : (seq + 1) * local_len].astype(jnp.bfloat16)


def qkv_weights_kernel(
    core_ref,
    a_ref,
    g_ref,
    gain_one_ref,
    gain_two_ref,
    kept_extra_ref,
    away_extra_ref,
    kept_ref,
    away_ref,
    w_ref,
):
    pairs, depth, width = kept_ref.shape
    span3 = g_ref.shape[0]
    used = width - 128
    w_ref[:, :span3] = product(a_ref[...].T, g_ref[...], NT)
    lane = used - 128
    gains = jnp.concatenate(
        [
            jnp.zeros((span3 - lane, width), jnp.float32),
            gain_one_ref[...],
            gain_two_ref[...],
            jnp.zeros((used - span3 - 2, width), jnp.float32),
        ],
        0,
    ).T
    w_ref[:, span3:] = gains[:, span3 - lane :]
    core = core_ref[0]
    for pair in range(pairs):
        for ref, extra_ref, which in (
            (kept_ref, kept_extra_ref, core),
            (away_ref, away_extra_ref, 1 - core),
        ):
            rows = pl.ds(pl.multiple_of((2 * pair + which) * depth, 8), depth)
            extra = extra_ref[pair]
            ref[pair] = jnp.concatenate(
                [
                    w_ref[rows],
                    jnp.concatenate(
                        [extra[:, k * 128 : (k + 1) * 128] for k in range(width // 128)], 0
                    ),
                ],
                1,
            ).astype(jnp.bfloat16)


def first_kernel(group_ref, w_ref, gains_ref, out_ref):
    depth, used = out_ref.shape
    spread = 4
    span = w_ref.shape[1] // (3 * spread)
    own_group = group_ref[0]
    gains = gains_ref[...]

    for which in range(spread):

        @pl.when(own_group == which)
        def _():
            picked = [
                w_ref[
                    :, (k * spread + which) * span : (k * spread + which + 1) * span
                ].astype(jnp.float32)
                for k in range(3)
            ]
            out_ref[...] = jnp.concatenate([*picked, gains], 1).astype(jnp.bfloat16)


def finish_kernel(
    ends_ref, gain_one_ref, qkv_ref, wout_ref, gain_two_ref, win_ref, wdown_ref
):
    ctx, _, width = ends_ref.shape
    depth = qkv_ref.shape[0]
    down_rows = wdown_ref.shape[0]
    count = win_ref.shape[1] // width
    spread = ctx // 2
    span = width // spread
    f32 = jnp.float32
    last = [ends_ref[k, :depth].astype(f32) for k in range(ctx)]
    for group in range(spread):
        both = last[group] + last[group + spread]
        for part in range(3):
            qkv_ref[:, part * width + group * span : part * width + (group + 1) * span] = both[
                :, part * span : (part + 1) * span
            ]
    total = last[0]
    for k in range(1, ctx):
        total = total + last[k]
    lane = 3 * span // 128 * 128
    gains = total[:, lane : lane + 128].T
    gain_one_ref[...] = gains[3 * span - lane : 3 * span - lane + 1]
    gain_two_ref[...] = gains[3 * span - lane + 1 : 3 * span - lane + 2]
    main = jnp.concatenate([ends_ref[k, depth:].astype(f32) for k in range(ctx)], 0)
    for k in range(count):
        win_ref[:, k * width : (k + 1) * width] = main[k * depth : (k + 1) * depth]
    wout_ref[...] = main[count * depth : (count + 1) * depth]
    split = main.shape[0] - (count + 1) * depth
    extra = down_rows - split
    wdown_ref[:split] = main[(count + 1) * depth :]
    wdown_ref[split:] = jnp.concatenate(
        [total[k * extra : (k + 1) * extra, width - 128 :] for k in range(width // 128)], 1
    )


def on_device(
    kernel, outs, args, micros, scratch=(), scalars=0, after=(), held=(), name=None
):
    space = pl.BlockSpec(memory_space=pltpu.VMEM)
    scalar = pl.BlockSpec(memory_space=pltpu.SMEM)
    given = len(args)

    def ordered(*refs):
        kernel(*refs[:given], *refs[given + len(after) :])

    return pl.pallas_call(
        ordered,
        out_shape=[jax.ShapeDtypeStruct(shape, dtype) for shape, dtype in outs],
        in_specs=[scalar] * scalars
        + [
            pl.BlockSpec(memory_space=pl.ANY) if k in held else space
            for k in range(scalars, given)
        ]
        + [pl.BlockSpec(memory_space=pl.ANY)] * len(after),
        out_specs=[space] * len(outs),
        scratch_shapes=list(scratch),
        compiler_params=pltpu.CompilerParams(vmem_limit_bytes=24 * 1024 * 1024),
        cost_estimate=pl.CostEstimate(
            flops=int(micros * 2e10), bytes_accessed=int(micros * 4e7), transcendentals=0
        ),
        name=name,
    )(*args, *after)


def sum_kernel(left_ref, right_ref, out_ref):
    for k in range(out_ref.shape[0]):
        out_ref[k] = (left_ref[k].astype(jnp.float32) + right_ref[k].astype(jnp.float32)).astype(
            jnp.bfloat16
        )


def spread_kernel(tokens_ref, out_ref):
    copies = out_ref.shape[0] // tokens_ref.shape[0]
    for k in range(out_ref.shape[0]):
        out_ref[k] = tokens_ref[k // copies]


def pass_kernel(in_ref, out_ref):
    out_ref[...] = in_ref[...]


def share_kernel(last_ref, shares_ref, out_ref):
    depth = last_ref.shape[0]
    total = shares_ref[0].astype(jnp.float32)
    for k in range(1, shares_ref.shape[0]):
        total = total + shares_ref[k].astype(jnp.float32)
    total = total.astype(jnp.bfloat16)
    for k in range(out_ref.shape[0]):
        out_ref[k, :depth] = last_ref[...]
        out_ref[k, depth:] = total


def interleave_kernel(late_ref, held_ref, came_ref, out_ref):
    late = late_ref[0]
    for k in range(held_ref.shape[0]):
        out_ref[k, late] = held_ref[k]
        out_ref[k, 1 - late] = came_ref[k]


def stack_kernel(upper_ref, lower_ref, out_ref):
    rows = upper_ref.shape[0]
    out_ref[:rows] = upper_ref[...]
    out_ref[rows:] = lower_ref[...]


def body(tokens, lengths, deal, gain_attn, w_qkv, w_out, gain_mlp, w_in, w_down, cotangent):
    seqs, local_len, width = tokens.shape
    ctx = lax.axis_size("ctx")
    fsdp = lax.axis_size("fsdp")
    spread = ctx // seqs
    group = HEADS // spread
    span = group * HD
    full_len = local_len * ctx
    rows = seqs * local_len
    context = lax.axis_index("ctx")
    own_seq = context // spread
    own_group = context % spread
    depth = w_qkv.shape[0]
    hidden = w_in.shape[1] // 2
    down_rows = w_down.shape[0]
    f32 = jnp.float32

    offsets = jnp.arange(BLK, dtype=jnp.int32)
    all_pos = (deal[:, None] * BLK + offsets[None, :]).reshape(full_len)
    length = lax.dynamic_slice_in_dim(lengths, own_seq, 1)[0]
    all_keep = all_pos < length

    used = 3 * span + 64
    gains_wide = jnp.pad(
        jnp.stack([gain_attn, gain_mlp], 1).astype(f32), ((0, 0), (0, used - 3 * span - 2))
    )
    first = on_device(
        first_kernel,
        [((depth, used), jnp.bfloat16)],
        (own_group.astype(jnp.int32)[None], w_qkv, gains_wide),
        0.05,
        scalars=1,
        name="first_pack",
    )[0]
    steps = [fsdp >> (k + 1) for k in range(fsdp.bit_length() - 1)]
    held = first[None]
    held = doubled(held, "fsdp", steps[0])
    early = held
    for bit in steps[1:-1]:
        held = doubled(held, "fsdp", bit)
    first_all = doubled(held, "fsdp", steps[-1]).reshape(fsdp * depth, used)
    win_all = lax.all_gather(w_in, "fsdp", axis=0, tiled=True)
    to_send = on_device(
        spread_kernel,
        [((ctx, local_len, width), jnp.bfloat16)],
        (tokens,),
        0.02,
        after=(early,),
        name="spread_tokens",
    )[0]
    sequence = lax.all_to_all(to_send, "ctx", 0, 0, tiled=True)
    stacked = on_device(
        stack_kernel,
        [((depth + down_rows, width), jnp.bfloat16)],
        (w_out, w_down),
        0.02,
        after=(held,),
        name="stack_rest",
    )[0]
    gain_one = first_all[:, 3 * span]
    gain_two = first_all[:, 3 * span + 1]

    cosine, sine = tables(all_pos)
    bias = jnp.where(all_keep, 0.0, NEGATIVE).astype(f32)[:, None]
    keep_row = all_keep.astype(f32)[None, :]
    sequence = sequence.reshape(full_len, width)
    a_low, qkv, mean, inverse = on_device(
        project_kernel,
        [
            ((full_len, width), jnp.bfloat16),
            ((3 * span, full_len), jnp.bfloat16),
            ((full_len, 1), f32),
            ((full_len, 1), f32),
        ],
        (sequence, first_all, cosine, sine),
        0.3,
        name="project",
    )
    rest = doubled(stacked[None], "fsdp", steps[0], after=(qkv,))
    attended, log_total, unrounded = on_device(
        forward_kernel,
        [
            ((ctx, span, local_len), jnp.bfloat16),
            ((8, full_len), f32),
            ((span, full_len), f32),
        ],
        (qkv, bias, keep_row),
        0.8,
        after=(rest,),
        name="attention_forward",
    )
    rest = doubled(rest, "fsdp", steps[1], after=(attended,))
    att_back = lax.all_to_all(attended, "ctx", 0, 0, tiled=True)
    rest = doubled(rest, "fsdp", steps[2], after=(att_back,))
    rest_other = lax.ppermute(rest, "fsdp", core_pairs(fsdp))
    att_turned = att_back.reshape(seqs, width, local_len)

    resid = tokens.astype(f32).reshape(rows, width)
    count = w_in.shape[1] // width
    main_rows = ((count + 1) * depth + down_rows) // (8 * ctx) * 8 * ctx
    chunk = main_rows // ctx
    split = main_rows - (count + 1) * depth
    extra = down_rows - split
    pairs = fsdp // 2
    core = (lax.axis_index("fsdp") % 2).astype(jnp.int32)[None]
    (
        grad_heads,
        grad_mixed,
        mixed,
        b_low,
        hid_low,
        grad_gate_up,
        grad_gain_two,
        wdown_all,
    ) = on_device(
        mlp_kernel,
        [
            ((ctx, span, local_len), jnp.bfloat16),
            ((rows, width), f32),
            ((rows, width), f32),
            ((rows, width), jnp.bfloat16),
            ((rows, hidden), jnp.bfloat16),
            ((rows, 2 * hidden), jnp.bfloat16),
            ((1, width), f32),
            ((hidden, width), jnp.bfloat16),
        ],
        (
            core,
            tokens,
            att_turned,
            cotangent,
            gain_two.astype(f32)[None, :],
            rest,
            rest_other,
            win_all,
        ),
        0.5,
        [pltpu.VMEM((fsdp * depth, width), jnp.bfloat16)],
        scalars=1,
        name="mlp",
    )
    half_outs = [
        ((ctx, pairs, chunk, width), jnp.bfloat16),
        ((pairs, extra, width), f32),
    ]
    main_away, away_extra, main_kept, kept_extra = on_device(
        mlp_weights_kernel,
        half_outs * 2,
        (core, att_turned, cotangent, grad_mixed, b_low, hid_low, grad_gate_up),
        0.05,
        [
            pltpu.VMEM((2 * width + hidden, rows), f32),
            pltpu.VMEM((hidden // 2, width), f32),
        ],
        scalars=1,
        name="mlp_weights",
    )
    main_pair = core_sum(main_kept, main_away, "fsdp", 0.02, name="sum_cores")
    main_part = lax.psum_scatter(
        main_pair.reshape(-1, chunk, width), "ctx", scatter_dimension=0, tiled=True
    )

    all_grad = lax.all_to_all(grad_heads, "ctx", 0, 0, tiled=True)
    grad_qkv, grad_a_part, grad_gain_one = on_device(
        backward_kernel,
        [
            ((3 * span, full_len), jnp.bfloat16),
            ((ctx, local_len, width), jnp.bfloat16),
            ((1, width), f32),
        ],
        (
            all_grad,
            qkv,
            log_total,
            unrounded,
            cosine,
            sine,
            bias,
            keep_row,
            sequence,
            mean,
            inverse,
            first_all,
        ),
        12,
        [
            pltpu.VMEM((HD, full_len), f32),
            pltpu.VMEM((HD, full_len), f32),
            pltpu.VMEM((full_len, width), jnp.bfloat16),
            pltpu.VMEM((width, used), jnp.bfloat16),
            pltpu.SemaphoreType.DMA((2,)),
        ],
        held=(8, 11),
        after=(main_pair,),
        name="attention_backward",
    )
    grad_a_parts = lax.all_to_all(grad_a_part, "ctx", 0, 0, tiled=True)
    output = on_device(
        layer_out_kernel,
        [(tokens.shape, jnp.bfloat16)],
        (mixed, hid_low, wdown_all),
        0.05,
        after=(grad_a_part,),
        name="layer_out",
    )[0]
    last_kept, last_away = on_device(
        qkv_weights_kernel,
        [((pairs, depth, width), jnp.bfloat16)] * 2,
        (core, a_low, grad_qkv, grad_gain_one, grad_gain_two, kept_extra, away_extra),
        0.1,
        [pltpu.VMEM((width, used), f32)],
        scalars=1,
        name="qkv_weights",
    )
    last = core_sum(
        last_kept, last_away, "fsdp", 0.05, name="sum_cores_last"
    )
    grad_a = jnp.sum(
        grad_a_parts.reshape(seqs, spread, local_len, width).astype(f32), 1
    ).reshape(rows, width)
    _, normed_one, inverse_one = norm_forward(resid, gain_one)
    grad_norm_one, _ = norm_backward(grad_a, gain_one, normed_one, inverse_one)
    grad_input = grad_mixed + grad_norm_one

    last = spread_sum_permuted(last, "fsdp")
    main_part = on_device(
        pass_kernel,
        [(main_part.shape, jnp.bfloat16)],
        (main_part,),
        0.02,
        after=(grad_a_parts, last),
        name="after_exchange",
    )[0]
    shares = lax.all_to_all(
        main_part, "fsdp", 0, 0, tiled=True, axis_index_groups=core_groups(fsdp)
    )
    ends = on_device(
        share_kernel,
        [((ctx, depth + chunk, width), jnp.bfloat16)],
        (last, shares),
        0.02,
        name="share",
    )[0]
    ends = lax.all_to_all(ends, "ctx", 0, 0, tiled=True)
    finished = on_device(
        finish_kernel,
        [
            ((1, depth), f32),
            (w_qkv.shape, f32),
            (w_out.shape, f32),
            ((1, depth), f32),
            (w_in.shape, f32),
            (w_down.shape, f32),
        ],
        (ends,),
        3,
        name="finish",
    )
    return (
        output,
        grad_input.reshape(tokens.shape),
        finished[0].reshape(depth),
        finished[1],
        finished[2],
        finished[3].reshape(depth),
        finished[4],
        finished[5],
    )


def solution(mesh):
    placed = (
        P("fsdp", "ctx", None),
        P("fsdp"),
        P(),
        P("fsdp"),
        P("fsdp", None),
        P("fsdp", None),
        P("fsdp"),
        P("fsdp", None),
        P("fsdp", None),
        P("fsdp", "ctx", None),
    )
    return jax.shard_map(
        body,
        mesh=mesh,
        in_specs=placed,
        out_specs=(
            P("fsdp", "ctx", None),
            P("fsdp", "ctx", None),
            P("fsdp"),
            P("fsdp", None),
            P("fsdp", None),
            P("fsdp"),
            P("fsdp", None),
            P("fsdp", None),
        ),
        check_vma=False,
    )
```
